128 devices in a mesh: ctx: 16 (over z, y), tp: 4 (over x_lo, core), fsdp: 2 (over x_hi).
Axes of the slice: x: 4 (x_hi: 2, x_lo: 2; x = x_hi * 2 + x_lo), y: 4, z: 4, core: 2. Of those that a mesh axis runs over, the one named last changes fastest.
Arguments:
- tokens: bfloat16 [8, 2048, 768], P('fsdp', 'ctx'), may hold values from -6 to 6
- cotangent: bfloat16 [8, 2048, 768], P('fsdp', 'ctx'), may hold values from -6 to 6
- lengths: int32 [8], P('fsdp'), may hold values from 1 to 2048, as said below
- w_qkv: bfloat16 [3, 768, 768], P(None, 'fsdp', 'tp'), may hold values from -0.21875 to 0.21875
- b_qv: bfloat16 [2, 768], P(None, ('tp', 'fsdp')), may hold values from -1.1953125 to 1.1953125
- w_out: bfloat16 [768, 768], P('tp', 'fsdp'), may hold values from -1.75 to 1.75
- b_out: bfloat16 [768], P('fsdp'), may hold values from -3 to 3
- ln1_gain: bfloat16 [768], P('fsdp'), may hold values from 0.5 to 1.5
- ln1_bias: bfloat16 [768], P('fsdp'), may hold values from -3 to 3
- w_in: bfloat16 [768, 3072], P('fsdp', 'tp'), may hold values from -0.21875 to 0.21875
- b_in: bfloat16 [3072], P(('tp', 'fsdp')), may hold values from -3 to 3
- w_down: bfloat16 [3072, 768], P('tp', 'fsdp'), may hold values from -0.109375 to 0.109375
- b_down: bfloat16 [768], P('fsdp'), may hold values from -3 to 3
- ln2_gain: bfloat16 [768], P('fsdp'), may hold values from 0.5 to 1.5
- ln2_bias: bfloat16 [768], P('fsdp'), may hold values from -3 to 3
Outputs:
- output: bfloat16 [8, 2048, 768], P('fsdp', 'ctx')
- grad_tokens: bfloat16 [8, 2048, 768], P('fsdp', 'ctx')
- grad_w_qkv: float32 [3, 768, 768], P(None, 'fsdp', 'tp')
- grad_b_qv: float32 [2, 768], P(None, ('tp', 'fsdp'))
- grad_w_out: float32 [768, 768], P('tp', 'fsdp')
- grad_b_out: float32 [768], P('fsdp')
- grad_ln1_gain: float32 [768], P('fsdp')
- grad_ln1_bias: float32 [768], P('fsdp')
- grad_w_in: float32 [768, 3072], P('fsdp', 'tp')
- grad_b_in: float32 [3072], P(('tp', 'fsdp'))
- grad_w_down: float32 [3072, 768], P('tp', 'fsdp')
- grad_b_down: float32 [768], P('fsdp')
- grad_ln2_gain: float32 [768], P('fsdp')
- grad_ln2_bias: float32 [768], P('fsdp')
The draws below stay inside these ranges and needn't reach their ends.
Inputs may be any that keep to these rules, and one draw needn't show every extreme that they name: `lengths`: among the 4 sequences of each index of fsdp, one drawn from the seed has length 2048.
All inputs are finite; a program needn't handle non-finite values.
Results may differ from the reference program's by a relative error of at most 0.025.
Values may be sent and summed in bfloat16 or wider, within the bound.
No kernel may reach another device: no remote copies, remote signals or barrier semaphores. Data moves between devices by JAX's collectives and lax.ppermute only.
A program may use at most 128 MiB of HBM per device.

```python
import jax
import jax.numpy as jnp
from jax import lax

D = 768
HEADS = 12
HEAD = 64
FF = 3072
SEQS = 4
SEQ_LEN = 2048
SEQUENCES = 8
N_FSDP = 2


def draw_lengths(key, part):
    key = jax.random.fold_in(key, 7)
    first, second = jax.random.split(key)
    others = jax.random.randint(first, (N_FSDP, SEQS), 1, SEQ_LEN + 1)
    chosen = jax.random.randint(second, (N_FSDP, 1), 0, SEQS)
    longest = jnp.arange(SEQS)[None, :] == chosen
    return jnp.where(longest, SEQ_LEN, others).reshape(N_FSDP * SEQS).astype(jnp.int32)


def block_levels(own_key, shape, shards, smallest, largest):
    def one(axis_at, blocks):
        heights = jax.random.uniform(jax.random.fold_in(jax.random.fold_in(own_key, 6), axis_at), (blocks,), jnp.float32, smallest / len(shards), largest / len(shards))
        return jnp.repeat(jnp.exp(heights), shape[axis_at] // blocks).reshape((-1,) + (1,) * (len(shape) - axis_at - 1))

    level = one(*shards[0])
    for cut in shards[1:]:
        level = level * one(*cut)
    return level


def centred(stream_key, extent, width, bound, pieces=(), kind=jnp.bfloat16):
    values = width * jax.random.normal(stream_key, extent, jnp.float32)
    if pieces:
        values = values * block_levels(stream_key, extent, pieces, -0.22, 0.18)
    return jnp.clip(values, -bound, bound).astype(kind)


def setup_inputs(seed: int = 0) -> dict:
    arg_keys = jax.random.split(jax.random.key(seed), 16)
    tokens = centred(arg_keys[0], (SEQUENCES, SEQ_LEN, D), 1.0, 6.0, ((0, 2), (1, 16)))
    cotangent = centred(arg_keys[1], (SEQUENCES, SEQ_LEN, D), 1.0, 6.0, ((0, 2), (1, 16)))
    lengths = draw_lengths(jax.random.fold_in(arg_keys[15], 71), 0)
    w_qkv = centred(arg_keys[3], (3, D, D), D ** -0.5, 0.21875, ((1, 2), (2, 4)))
    b_qv = centred(arg_keys[4], (2, D), 0.2, 1.1953125, ((1, 8),))
    w_out = centred(arg_keys[5], (D, D), (D // 64) ** -0.5, 1.75, ((0, 4), (1, 2)))
    b_out = centred(arg_keys[6], (D,), 0.5, 3.0, ((0, 2),))
    ln1_gain = jnp.clip(1.0 + 0.1 * jax.random.normal(arg_keys[7], (D,), jnp.float32), 0.5, 1.5).astype(jnp.bfloat16)
    ln1_bias = centred(arg_keys[8], (D,), 0.5, 3.0, ((0, 2),))
    w_in = centred(arg_keys[9], (D, FF), D ** -0.5, 0.21875, ((0, 2), (1, 4)))
    b_in = centred(arg_keys[10], (FF,), 0.5, 3.0, ((0, 8),))
    w_down = centred(arg_keys[11], (FF, D), FF ** -0.5, 0.109375, ((0, 4), (1, 2)))
    b_down = centred(arg_keys[12], (D,), 0.5, 3.0, ((0, 2),))
    ln2_gain = jnp.clip(1.0 + 0.1 * jax.random.normal(arg_keys[13], (D,), jnp.float32), 0.5, 1.5).astype(jnp.bfloat16)
    ln2_bias = centred(arg_keys[14], (D,), 0.5, 3.0, ((0, 2),))
    return dict(tokens=tokens, cotangent=cotangent, lengths=lengths, w_qkv=w_qkv, b_qv=b_qv, w_out=w_out, b_out=b_out, ln1_gain=ln1_gain, ln1_bias=ln1_bias, w_in=w_in, b_in=b_in, w_down=w_down, b_down=b_down, ln2_gain=ln2_gain, ln2_bias=ln2_bias)


epsilon = 1e-06
masked_score = -1000000000.0

@jax.custom_vjp
def low(v):
    return lax.optimization_barrier(v.astype(jnp.bfloat16)).astype(jnp.float32)

@jax.custom_vjp
def low_back(v):
    return v

def low_keep(v):
    return (low(v), None)

def low_pass(kept, grad):
    return (grad,)

def back_keep(v):
    return (v, None)

def back_low(kept, grad):
    return (low(grad),)
low.defvjp(low_keep, low_pass)
low_back.defvjp(back_keep, back_low)

def layer_norm(resid, gain, shift):
    center = resid - lax.optimization_barrier(jnp.mean(resid, axis=-1, keepdims=True))
    spread = lax.optimization_barrier(jnp.mean(center * center, axis=-1, keepdims=True))
    return center * lax.rsqrt(spread + epsilon) * gain + shift

def layer(tokens, length, params):
    w_qkv, b_qv, w_out, b_out, gain_one, shift_one, w_in, b_in, w_down, b_down, gain_two, shift_two = params
    highest = lax.Precision.HIGHEST
    seq_len = tokens.shape[0]
    block = min(512, seq_len)
    query = low_back(low(jnp.dot(tokens, w_qkv[0], precision=highest) + b_qv[0]))
    keys = low_back(low(jnp.dot(tokens, w_qkv[1], precision=highest)))
    values = low_back(low(jnp.dot(tokens, w_qkv[2], precision=highest) + b_qv[1]))
    query_heads = query.reshape(seq_len // block, block, HEADS, HEAD).transpose(0, 2, 1, 3)
    key_heads = keys.reshape(seq_len, HEADS, HEAD).transpose(1, 0, 2)
    value_heads = values.reshape(seq_len, HEADS, HEAD).transpose(1, 0, 2)
    valid = jnp.arange(seq_len) < length

    def attend(block_query):
        scores = jnp.einsum('hqd,hkd->hqk', block_query, key_heads, precision=highest) * HEAD ** (-0.5)
        scores = low_back(jnp.where(valid[None, None, :], scores, masked_score))
        probs = low(jax.nn.softmax(scores, axis=-1))
        return jnp.einsum('hqk,hkd->hqd', probs, value_heads, precision=highest)
    blocks = lax.map(jax.checkpoint(attend), query_heads)
    attn = low_back(low(blocks.transpose(0, 2, 1, 3).reshape(seq_len, D)))
    resid_one = tokens + low_back(jnp.dot(attn, w_out, precision=highest)) + b_out
    hidden = layer_norm(resid_one, gain_one, shift_one)
    gelu_input = low_back(jnp.dot(low(hidden), w_in, precision=highest) + b_in)
    gelu_out = low(jax.nn.gelu(gelu_input, approximate=False))
    resid_two = hidden + low_back(jnp.dot(gelu_out, w_down, precision=highest)) + b_down
    return layer_norm(resid_two, gain_two, shift_two)

def reference(tokens, cotangent, lengths, w_qkv, b_qv, w_out, b_out, ln1_gain, ln1_bias, w_in, b_in, w_down, b_down, ln2_gain, ln2_bias):
    params = tuple((item.astype(jnp.float32) for item in (w_qkv, b_qv, w_out, b_out, ln1_gain, ln1_bias, w_in, b_in, w_down, b_down, ln2_gain, ln2_bias)))

    def one_sequence(total, inputs):
        seq_tokens, seq_grad, seq_length = inputs

        def forward(token_rows, weights):
            return layer(token_rows, seq_length, weights)
        result, pullback = jax.vjp(forward, seq_tokens.astype(jnp.float32), params)
        grad_rows, grad_params = pullback(seq_grad.astype(jnp.float32))
        total = jax.tree.map(jnp.add, total, grad_params)
        return (total, (result.astype(jnp.bfloat16), grad_rows.astype(jnp.bfloat16)))
    start = jax.tree.map(jnp.zeros_like, params)
    total, (results, grad_rows) = lax.scan(one_sequence, start, (tokens, cotangent, lengths))
    return (results, grad_rows) + tuple(total)
```

```python
import jax
import jax.numpy as jnp
from jax import lax
from jax.experimental import pallas as pl
from jax.experimental.pallas import tpu as pltpu
from jax.sharding import PartitionSpec as P


EPS = 1e-06
MASKED = -1000000000.0
HEADS = 3
F32 = jnp.float32
BF16 = jnp.bfloat16
VMEM = pl.BlockSpec(memory_space=pltpu.VMEM)
SMEM = pl.BlockSpec(memory_space=pltpu.SMEM)


def z_shift(value, step):
    return lax.ppermute(
        value, "ctx", [(z * 4 + y, (z + step) % 4 * 4 + y) for z in range(4) for y in range(4)]
    )


def y_shift(value, step):
    return lax.ppermute(
        value, "ctx", [(z * 4 + y, z * 4 + (y + step) % 4) for z in range(4) for y in range(4)]
    )


def core_swap(value):
    return lax.ppermute(value, "tp", [(t, t ^ 1) for t in range(4)])


def chip_swap(value):
    return lax.ppermute(value, "tp", [(t, t ^ 2) for t in range(4)])


def fsdp_swap(value):
    return lax.ppermute(value, "fsdp", [(0, 1), (1, 0)])


def tp_sum(own, other):
    mine = (own + core_swap(other).astype(F32)).astype(BF16)
    return mine, chip_swap(mine)


def sum_axis(value, shift):
    total = value
    for step in (1, 2, 3):
        total = total + shift(value, step)
    return total


def scatter_axis(value, shift, place):
    total = lax.dynamic_index_in_dim(value, place, 0, keepdims=False).astype(F32)
    for step in (1, 2, 3):
        piece = lax.dynamic_index_in_dim(value, (place + step) % 4, 0, keepdims=False)
        total = total + shift(piece, step).astype(F32)
    return total.astype(BF16)


def gather_axis(value, shift):
    return jnp.stack([value] + [shift(value, -step) for step in (1, 2, 3)])


def call(kernel, outs, *args, smem=0, flops=0, scratch=(), limit=40):
    size = sum(a.size * a.dtype.itemsize for a in args)
    size += sum(o.size * jnp.dtype(o.dtype).itemsize for o in outs)
    return pl.pallas_call(
        kernel,
        out_shape=outs,
        in_specs=[SMEM] * smem + [VMEM] * (len(args) - smem),
        out_specs=[VMEM] * len(outs),
        scratch_shapes=list(scratch),
        compiler_params=pltpu.CompilerParams(vmem_limit_bytes=limit * 1024 * 1024),
        cost_estimate=pl.CostEstimate(flops=flops, bytes_accessed=size, transcendentals=0),
    )(*args)


def shape(dims, kind):
    return jax.ShapeDtypeStruct(dims, kind)


def dot(a, b):
    return jnp.dot(a, b, preferred_element_type=F32)


def dot_t(a, b):
    return lax.dot_general(a, b, (((1,), (1,)), ((), ())), preferred_element_type=F32)


def pick_kernel(info, src, *pieces):
    y, c, h = info[1], info[2], info[3]
    for step in range(4):
        row = src[lax.rem(y + step, 4), pl.ds(pl.multiple_of(c * 64, 64), 64), :]
        low, high = row[:, :384], row[:, 384:]
        pieces[step][:, :384] = jnp.where(h == 0, low, high)
        pieces[step][:, 384:] = jnp.where(h == 0, high, low)


def place_kernel(info, own, other, out):
    y, c, h = info[1], info[2], info[3]
    for ref, at in ((own, c), (other, 1 - c)):
        for step in range(4):
            row = ref[step]
            first, second = row[:, :384], row[:, 384:]
            rows = pl.ds(pl.multiple_of(at * 64, 64), 64)
            seq = lax.rem(y + step, 4)
            out[seq, rows, :384] = jnp.where(h == 0, first, second)
            out[seq, rows, 384:] = jnp.where(h == 0, second, first)


def qkv_kernel(x_own, x_other, w_own, w_other, bias, q_ref, kv_ref):
    for half, x in enumerate((x_own, x_other)):
        rows = slice(half * 256, half * 256 + 256)
        value = dot_t(x[:, :384], w_own[...]) + dot_t(x[:, 384:], w_other[...]) + bias[...]
        q_ref[rows, :192] = (value[:, :192].astype(BF16) * BF16(0.125)).astype(BF16)
        q_ref[rows, 192:] = jnp.zeros((256, 64), BF16)
        kv_ref[rows, :] = value[:, 192:].astype(BF16)


def mask_rows(info, away):
    z, y, c, length = info[0], info[1], info[2], info[4]
    row = lax.broadcasted_iota(jnp.int32, (512, 128), 0)
    half = lax.shift_right_logical(row, 8)
    block = lax.bitwise_and(lax.shift_right_logical(row, 6), 3)
    place = (
        512 * lax.rem(z + 4 - away, 4)
        + 128 * lax.bitwise_and(y + 4 - block, 3)
        + 64 * jnp.where(half == c, 0, 1)
        + lax.bitwise_and(row, 63)
    )
    bias = jnp.where(place < length, 0.0, MASKED).astype(F32)
    return jnp.concatenate([bias] * 4, axis=1)


def head_lanes(value, head, offset):
    lane = lax.broadcasted_iota(jnp.int32, value.shape, 1)
    low = offset + 64 * head
    return jnp.where((lane >= low) & (lane < low + 64), value, jnp.zeros_like(value))


def attend_kernel(info, q_ref, kv0, kv1, kv2, kv3, o_ref, lse_ref, vt_ref, bias_ref):
    chunks = (kv0, kv1, kv2, kv3)
    for step, kv in enumerate(chunks):
        vt_ref[step] = kv[:, 128:].astype(F32).T.astype(BF16)
        bias_ref[step] = mask_rows(info, step)
    parts = [jnp.zeros((64, 512), F32)]
    logs = []
    for head in range(HEADS):
        query = head_lanes(q_ref[...], head, 0)
        top = jnp.full((1, 512), -1e30, F32)
        total = jnp.zeros((1, 512), F32)
        acc = jnp.zeros((64, 512), F32)
        for step, kv in enumerate(chunks):
            scores = dot_t(kv[:, :256], query) + bias_ref[step]
            peak = jnp.maximum(top, jnp.max(scores, axis=0, keepdims=True))
            keep = jnp.exp(top - peak)
            expo = jnp.exp(scores - peak)
            total = total * keep + jnp.sum(expo, axis=0, keepdims=True)
            low = 64 + 64 * head
            acc = acc * keep + dot(vt_ref[step, low : low + 64, :], expo.astype(BF16))
            top = peak
        parts.append(acc / total)
        logs.append(top + jnp.log(total))
    o_ref[...] = jnp.concatenate(parts, axis=0).T.astype(BF16)
    lse_ref[...] = jnp.concatenate(logs + [jnp.zeros((5, 512), F32)], axis=0)


def attend_back_kernel(away, first, *refs):
    if first:
        info, q_ref, do_ref, kv, lse, inner, dkv_ref, dq_ref = refs
    else:
        info, q_ref, do_ref, kv, lse, inner, dq_in, dkv_ref, dq_ref = refs
    bias = mask_rows(info, away)
    keys, values = kv[:, :256], kv[:, 128:]
    keys_t = keys.astype(F32).T.astype(BF16)
    dk = jnp.zeros((512, 256), F32)
    dv = jnp.zeros((512, 256), F32)
    for head in range(HEADS):
        query = head_lanes(q_ref[...], head, 0)
        grad = head_lanes(do_ref[...], head, 64)
        probs = jnp.exp(dot_t(keys, query) + bias - lse[head : head + 1, :])
        grad_probs = dot_t(values, grad) - inner[head : head + 1, :]
        grad_scores = (probs * grad_probs).astype(BF16)
        dk = dk + dot(grad_scores, query)
        dv = dv + dot(probs.astype(BF16), grad)
        rows = slice(64 * head, 64 * head + 64)
        dq = dot(keys_t[rows, :], grad_scores)
        if not first:
            dq = dq + dq_in[rows, :]
        dq_ref[rows, :] = dq
    dkv_ref[:, :128] = dk[:, :128].astype(BF16)
    dkv_ref[:, 128:256] = (dk[:, 128:] + dv[:, :128]).astype(BF16)
    dkv_ref[:, 256:] = dv[:, 128:].astype(BF16)


def out_kernel(o_ref, w_own, w_other, own, other):
    for rows, ref in ((slice(256, 512), other), (slice(0, 256), own)):
        ref[:, :384] = dot(o_ref[rows, :], w_own[...]).astype(ref.dtype)
        ref[:, 384:] = dot(o_ref[rows, :], w_other[...]).astype(ref.dtype)


def normalize(value):
    center = value - jnp.mean(value, axis=1, keepdims=True)
    inverse = lax.rsqrt(jnp.mean(center * center, axis=1, keepdims=True) + EPS)
    return center * inverse, inverse


def back_normalize(grad, normed, inverse, gain):
    scaled = grad * gain
    return inverse * (
        scaled
        - jnp.mean(scaled, axis=1, keepdims=True)
        - normed * jnp.mean(scaled * normed, axis=1, keepdims=True)
    )


def column_sums(*values):
    rows = [jnp.sum(value, axis=0, keepdims=True) for value in values]
    return jnp.concatenate(rows + [jnp.zeros((8 - len(rows), rows[0].shape[1]), F32)], axis=0)


def norm_one_kernel(x, a, b, small, normed_ref, inverse_ref, low_ref):
    resid = x[...].astype(F32) + (a[...].astype(F32) + b[...].astype(F32)) + small[0:1, :]
    normed, inverse = normalize(resid)
    normed_ref[...] = normed
    inverse_ref[...] = jnp.broadcast_to(inverse, (256, 128))
    low_ref[...] = (normed * small[1:2, :] + small[2:3, :]).astype(BF16)


def norm_two_kernel(normed_one, a, b, cot, small, result_ref, grad_ref, low_ref, sums_ref):
    hidden = normed_one[...] * small[1:2, :] + small[2:3, :]
    resid = hidden + (a[...].astype(F32) + b[...].astype(F32)) + small[3:4, :]
    normed, inverse = normalize(resid)
    gain = small[4:5, :]
    result_ref[...] = (normed * gain + small[5:6, :]).astype(BF16)
    dy = cot[...].astype(F32)
    grad = back_normalize(dy, normed, inverse, gain)
    grad_ref[...] = grad
    low_ref[...] = grad.astype(BF16)
    sums_ref[...] = column_sums(dy * normed, dy, grad)


def norm_back_kernel(grad_two, a, b, normed_one, inverse_one, small, grad_ref, low_ref, sums_ref):
    dh = grad_two[...] + (a[...].astype(F32) + b[...].astype(F32))
    normed = normed_one[...]
    grad = back_normalize(dh, normed, inverse_one[:, :1], small[1:2, :])
    grad_ref[...] = grad
    low_ref[...] = grad.astype(BF16)
    sums_ref[...] = column_sums(dh * normed, dh, grad)


def mlp_kernel(
    h_own, h_other, in_own, in_other, bias, down_own, down_other, g_ref, slope_ref, own, other
):
    for rows, h, ref in ((slice(256, 512), h_other, other), (slice(0, 256), h_own, own)):
        u = dot(h[:, :384], in_own[...]) + dot(h[:, 384:], in_other[...]) + bias[...]
        cdf = 0.5 + 0.5 * lax.erf(u * 0.7071067811865476)
        slope_ref[rows, :] = cdf + u * (0.3989422804014327 * jnp.exp(-0.5 * u * u))
        g = (u * cdf).astype(BF16)
        g_ref[rows, :] = g
        ref[:, :384] = dot(g, down_own[...]).astype(ref.dtype)
        ref[:, 384:] = dot(g, down_other[...]).astype(ref.dtype)


def mlp_back_kernel(
    dz_own, dz_other, down_own, down_other, slope, in_own, in_other, du_ref, own, other, sums_ref
):
    total = jnp.zeros((1, 768), F32)
    for rows, dz, ref in ((slice(256, 512), dz_other, other), (slice(0, 256), dz_own, own)):
        dg = dot_t(dz[:, :384], down_own[...]) + dot_t(dz[:, 384:], down_other[...])
        du = (dg * slope[rows, :]).astype(BF16)
        du_ref[rows, :] = du
        total = total + jnp.sum(du.astype(F32), axis=0, keepdims=True)
        ref[:, :384] = dot_t(du, in_own[...]).astype(ref.dtype)
        ref[:, 384:] = dot_t(du, in_other[...]).astype(ref.dtype)
    sums_ref[...] = jnp.broadcast_to(total, (8, 768))


def out_back_kernel(da_own, da_other, w_own, w_other, o_ref, do_ref, inner_ref):
    for half, da in enumerate((da_own, da_other)):
        rows = slice(half * 256, half * 256 + 256)
        value = dot_t(da[:, :384], w_own[...]) + dot_t(da[:, 384:], w_other[...])
        do_ref[rows, :] = value.astype(BF16)
    product = (do_ref[...].astype(F32) * o_ref[...].astype(F32)).T
    rows = [jnp.sum(product[64 + 64 * k : 128 + 64 * k], axis=0, keepdims=True) for k in range(HEADS)]
    inner_ref[...] = jnp.concatenate(rows + [jnp.zeros((5, 512), F32)], axis=0)


def input_back_kernel(dkv, r1, r2, r3, dq_t, w_own, w_other, low_ref, own, other, sums_ref):
    dq = (dq_t[...].T * 0.125).astype(BF16)
    low_ref[:, :256] = jnp.concatenate([dq, jnp.zeros((512, 64), BF16)], axis=1)
    total = dkv[...].astype(F32) + r1[...].astype(F32) + (r2[...].astype(F32) + r3[...].astype(F32))
    low_ref[:, 256:] = total.astype(BF16)
    sums_ref[...] = jnp.broadcast_to(
        jnp.sum(low_ref[...].astype(F32), axis=0, keepdims=True), (8, 640)
    )
    for rows, ref in ((slice(256, 512), other), (slice(0, 256), own)):
        for cols, w in ((slice(0, 384), w_own), (slice(384, 768), w_other)):
            value = dot(low_ref[rows, :192], w[:192, :]) + dot(low_ref[rows, 256:], w[192:, :])
            ref[:, cols] = value.astype(ref.dtype)


def spread_kernel(info, first, second, *refs):
    out = refs[4]
    for i in range(4):
        for j in range(4):
            out[lax.rem(info[first] + i, 4), lax.rem(info[second] + j, 4)] = refs[i][j].astype(F32)


def gradient(pair, outer, outer_at, inner, inner_at):
    rows = pair.shape[1] // 16
    value = pair.reshape(2, 4, 4, rows, 384).transpose(1, 0, 2, 3, 4)
    value = scatter_axis(value, outer, outer_at)
    value = scatter_axis(value.transpose(1, 0, 2, 3), inner, inner_at)
    value = (value[0].astype(F32) + fsdp_swap(value[1]).astype(F32)).astype(BF16)
    stack = gather_axis(value, inner)
    return [stack] + [outer(stack, -step) for step in (1, 2, 3)]


def spread(info, pieces, first, second):
    rows = pieces[0].shape[1]
    (out,) = call(
        lambda *refs: spread_kernel(refs[0], first, second, *refs[1:]),
        [shape((4, 4, rows, 384), F32)],
        info,
        *pieces,
        smem=1,
    )
    return out.reshape(16 * rows, 384)


def to_owner(value, info):
    pieces = [value[64 * s : 64 * s + 64] for s in range(4)]
    own = jnp.stack([pieces[0]] + [y_shift(pieces[s], -s) for s in (1, 2, 3)])
    (out,) = call(place_kernel, [shape((4, 128, 768), BF16)], info, own, core_swap(own), smem=1)
    return out


def body(
    tokens,
    cotangent,
    lengths,
    w_qkv,
    b_qv,
    w_out,
    b_out,
    ln1_gain,
    ln1_bias,
    w_in,
    b_in,
    w_down,
    b_down,
    ln2_gain,
    ln2_bias,
):
    ctx, tp, h = lax.axis_index("ctx"), lax.axis_index("tp"), lax.axis_index("fsdp")
    z, y, c = ctx // 4, ctx % 4, tp % 2
    length = lax.dynamic_index_in_dim(lengths, y, 0, keepdims=False)
    info = jnp.stack([z, y, c, h, length, z, z, z]).astype(jnp.int32)

    pieces = call(pick_kernel, [shape((64, 768), BF16)] * 4, info, tokens, smem=1)
    wt_own = w_qkv.transpose(0, 2, 1).reshape(576, 384)
    packed = jnp.stack(
        [
            b_out,
            ln1_gain,
            ln1_bias,
            b_down,
            ln2_gain,
            ln2_bias,
            b_in,
            jnp.concatenate([b_qv.reshape(192), jnp.zeros((192,), BF16)]),
        ]
    )
    x_own = jnp.concatenate([pieces[0]] + [y_shift(pieces[s], s) for s in (1, 2, 3)])
    wt_other = fsdp_swap(wt_own)
    packed_other = fsdp_swap(packed)
    x_other = core_swap(x_own)
    small = jnp.concatenate([packed, packed_other], axis=1).astype(F32)

    def in_order(own, other):
        return jnp.where(h == 0, jnp.concatenate([own, other]), jnp.concatenate([other, own]))

    bias_in = in_order(packed[6], packed_other[6]).astype(F32).reshape(1, 768)
    bias_q = in_order(packed[7, :96], packed_other[7, :96]).astype(F32)
    bias_v = in_order(packed[7, 96:192], packed_other[7, 96:192]).astype(F32)
    bias = jnp.concatenate([bias_q, jnp.zeros((192,), F32), bias_v]).reshape(1, 576)

    query, kv = call(
        qkv_kernel,
        [shape((512, 256), BF16), shape((512, 384), BF16)],
        x_own,
        x_other,
        wt_own,
        wt_other,
        bias,
        flops=2 * 512 * 768 * 576,
    )
    away = [kv] + [z_shift(kv, s) for s in (1, 2, 3)]

    w_out, w_in, w_down, cotangent, _ = lax.optimization_barrier(
        (w_out, w_in, w_down, cotangent, kv)
    )
    out_own = jnp.pad(w_out, ((64, 0), (0, 0)))
    out_other = jnp.pad(fsdp_swap(w_out), ((64, 0), (0, 0)))
    in_other = fsdp_swap(w_in)
    down_other = fsdp_swap(w_down)
    cot_pieces = call(pick_kernel, [shape((64, 768), BF16)] * 4, info, cotangent, smem=1)
    cot = jnp.concatenate([cot_pieces[0]] + [y_shift(cot_pieces[s], s) for s in (1, 2, 3)])

    attn, log_total = call(
        attend_kernel,
        [shape((512, 256), BF16), shape((8, 512), F32)],
        info,
        query,
        *away,
        smem=1,
        flops=4 * 12 * 128 * 2048 * 64 * 4,
        scratch=[pltpu.VMEM((4, 256, 512), BF16), pltpu.VMEM((4, 512, 512), F32)],
    )
    halves = [shape((256, 768), F32), shape((256, 768), BF16)]
    own, other = call(out_kernel, halves, attn, out_own, out_other, flops=2 * 512 * 768 * 256)
    a, b = tp_sum(own, other)
    normed_one, inverse_one, hidden_own = call(
        norm_one_kernel,
        [shape((256, 768), F32), shape((256, 128), F32), shape((256, 768), BF16)],
        x_own,
        a,
        b,
        small,
    )
    hidden_other = core_swap(hidden_own)
    gelu, slope, own, other = call(
        mlp_kernel,
        [shape((512, 768), BF16), shape((512, 768), F32)] + halves,
        hidden_own,
        hidden_other,
        w_in,
        in_other,
        bias_in,
        w_down,
        down_other,
        flops=4 * 512 * 768 * 768,
    )
    a, b = tp_sum(own, other)
    result, grad_two, dz_own, sums_two = call(
        norm_two_kernel,
        [
            shape((256, 768), BF16),
            shape((256, 768), F32),
            shape((256, 768), BF16),
            shape((8, 768), F32),
        ],
        normed_one,
        a,
        b,
        cot,
        small,
    )
    dz_other = core_swap(dz_own)
    du, own, other, sums_in = call(
        mlp_back_kernel,
        [shape((512, 768), BF16)] + halves + [shape((8, 768), F32)],
        dz_own,
        dz_other,
        w_down,
        down_other,
        slope,
        w_in,
        in_other,
        flops=4 * 512 * 768 * 768,
    )
    a, b = tp_sum(own, other)
    output = to_owner(result, info)
    dz = jnp.concatenate([dz_own, dz_other])
    d_down = jnp.einsum("tf,td->fd", gelu, dz, preferred_element_type=F32).astype(BF16)
    down_pieces = gradient(
        jnp.stack([d_down[:, :384], d_down[:, 384:]]), y_shift, y, z_shift, z
    )
    grad_one, da_own, sums_one = call(
        norm_back_kernel,
        [shape((256, 768), F32), shape((256, 768), BF16), shape((8, 768), F32)],
        grad_two,
        a,
        b,
        normed_one,
        inverse_one,
        small,
    )
    da_other = core_swap(da_own)
    grad_heads, inner = call(
        out_back_kernel,
        [shape((512, 256), BF16), shape((8, 512), F32)],
        da_own,
        da_other,
        out_own,
        out_other,
        attn,
        flops=2 * 512 * 768 * 256,
    )
    hidden = jnp.concatenate([hidden_own, hidden_other])
    da = jnp.concatenate([da_own, da_other])
    d_in = jnp.einsum("td,tf->df", hidden, du, preferred_element_type=F32).astype(BF16)
    d_out = jnp.einsum("te,td->ed", attn, da, preferred_element_type=F32).astype(BF16)

    def rows_of(at):
        return jnp.concatenate(
            [
                d_in[384 * at : 384 * at + 384, :384],
                d_in[384 * at : 384 * at + 384, 384:],
                d_out[:, 384 * at : 384 * at + 384],
            ]
        )

    in_pieces = gradient(jnp.stack([rows_of(0), rows_of(1)]), y_shift, y, z_shift, z)

    grad_keys, dq = {}, None
    for s in (1, 2, 3, 0):
        first = dq is None
        grad_keys[s], dq = call(
            lambda *refs, s=s, first=first: attend_back_kernel(s, first, *refs),
            [shape((512, 384), BF16), shape((192, 512), F32)],
            info,
            query,
            grad_heads,
            away[s],
            log_total,
            inner,
            *(() if first else (dq,)),
            smem=1,
            flops=10 * 3 * 512 * 512 * 64 * 4,
        )
    back = [z_shift(grad_keys[s], -s) for s in (1, 2, 3)]
    grad_qkv, own, other, sums_qkv = call(
        input_back_kernel,
        [shape((512, 640), BF16)] + halves + [shape((8, 640), F32)],
        grad_keys[0],
        *back,
        dq,
        wt_own,
        wt_other,
        flops=2 * 512 * 768 * 576,
    )
    a, b = tp_sum(own, other)
    x = jnp.concatenate([x_own, x_other])
    d_proj = jnp.einsum("te,td->ed", grad_qkv, x, preferred_element_type=F32).astype(BF16)
    proj_pieces = gradient(
        jnp.stack([d_proj[:, :384], d_proj[:, 384:]]), z_shift, z, y_shift, y
    )
    grad_x = (grad_one + (a.astype(F32) + b.astype(F32))).astype(BF16)
    grad_tokens = to_owner(grad_x, info)

    rows_two = jnp.concatenate([sums_two[:3], sums_one[:3], jnp.zeros((2, 768), F32)])
    rows_two = rows_two + core_swap(rows_two)
    vectors = jnp.concatenate([rows_two[:6], sums_in[:1], jnp.zeros((1, 768), F32)])
    vectors = sum_axis(sum_axis(vectors, z_shift), y_shift)
    late = sum_axis(sum_axis(sums_qkv[:1], y_shift), z_shift)

    def ordered(row):
        half = row.shape[0] // 2
        return (
            jnp.where(h == 0, row[:half], row[half:]),
            jnp.where(h == 0, row[half:], row[:half]),
        )

    in_mine, in_yours = ordered(vectors[6])
    mine = jnp.concatenate([vectors[:6, :384], in_mine[None]])
    yours = jnp.concatenate([vectors[:6, 384:], in_yours[None]])
    vector = mine + fsdp_swap(yours)
    q_mine, q_yours = ordered(late[0, :192])
    v_mine, v_yours = ordered(late[0, 448:])
    grad_b_qv = jnp.stack([q_mine, v_mine]) + fsdp_swap(jnp.stack([q_yours, v_yours]))

    grad_down = spread(info, down_pieces, 1, 0)
    grad_in = spread(info, in_pieces, 1, 0)
    grad_proj = spread(info, proj_pieces, 0, 1)
    grad_proj = jnp.concatenate([grad_proj[:192], grad_proj[256:]])
    return (
        output,
        grad_tokens,
        grad_proj.reshape(3, 192, 384).transpose(0, 2, 1),
        grad_b_qv,
        grad_in[832:],
        vector[5],
        vector[3],
        vector[4],
        jnp.concatenate([grad_in[:384], grad_in[384:768]], axis=1),
        vector[6],
        grad_down,
        vector[2],
        vector[0],
        vector[1],
    )


def solution(mesh):
    placed = (
        P("fsdp", "ctx", None),
        P("fsdp", "ctx", None),
        P("fsdp"),
        P(None, "fsdp", "tp"),
        P(None, ("tp", "fsdp")),
        P("tp", "fsdp"),
        P("fsdp"),
        P("fsdp"),
        P("fsdp"),
        P("fsdp", "tp"),
        P(("tp", "fsdp")),
        P("tp", "fsdp"),
        P("fsdp"),
        P("fsdp"),
        P("fsdp"),
    )
    return jax.shard_map(
        body,
        mesh=mesh,
        in_specs=placed,
        out_specs=placed[:2]
        + (
            P(None, "fsdp", "tp"),
            P(None, ("tp", "fsdp")),
            P("tp", "fsdp"),
            P("fsdp"),
            P("fsdp"),
            P("fsdp"),
            P("fsdp", "tp"),
            P(("tp", "fsdp")),
            P("tp", "fsdp"),
            P("fsdp"),
            P("fsdp"),
            P("fsdp"),
        ),
        check_vma=False,
    )
```

```python
import jax
import jax.numpy as jnp
from jax import lax
from jax.experimental import pallas as pl
from jax.experimental.pallas import tpu as pltpu
from jax.sharding import PartitionSpec as P


EPS = 1e-06
MASKED = -1000000000.0
HEADS = 3
F32 = jnp.float32
BF16 = jnp.bfloat16
VMEM = pl.BlockSpec(memory_space=pltpu.VMEM)
SMEM = pl.BlockSpec(memory_space=pltpu.SMEM)


def core_swap(value):
    return lax.ppermute(value, "tp", [(t, t ^ 1) for t in range(4)])


def chip_swap(value):
    return lax.ppermute(value, "tp", [(t, t ^ 2) for t in range(4)])


def fsdp_swap(value):
    return lax.ppermute(value, "fsdp", [(0, 1), (1, 0)])


def z_shift(value, step):
    return lax.ppermute(
        value, "ctx", [(z * 4 + y, (z + step) % 4 * 4 + y) for z in range(4) for y in range(4)]
    )


def y_exchange(value):
    groups = [[z * 4 + y for y in range(4)] for z in range(4)]
    return lax.all_to_all(value, "ctx", 0, 0, axis_index_groups=groups, tiled=True)


def tp_sum(own, other):
    mine = (own + core_swap(other).astype(F32)).astype(BF16)
    return mine, chip_swap(mine)


def ctx_exchange(value):
    terms = lax.all_to_all(value, "ctx", 0, 0, tiled=True)
    return terms.reshape(16, value.shape[0] // 16, value.shape[1])


def call(kernel, outs, *args, smem=0, scratch=(), after=(), limit=40):
    count, skip = len(args), len(args) + len(after)

    def run(*refs):
        kernel(*refs[:count], *refs[skip:])

    return pl.pallas_call(
        run,
        out_shape=outs,
        in_specs=[SMEM] * smem
        + [VMEM] * (count - smem)
        + [pl.BlockSpec(memory_space=pl.ANY)] * len(after),
        out_specs=[VMEM] * len(outs),
        scratch_shapes=list(scratch),
        compiler_params=pltpu.CompilerParams(vmem_limit_bytes=limit * 1024 * 1024),
        cost_estimate=pl.CostEstimate(flops=1000, bytes_accessed=1000, transcendentals=0),
    )(*args, *after)


def place_of():
    ctx, tp = lax.axis_index("ctx"), lax.axis_index("tp")
    return (
        lax.shift_right_logical(ctx, 2),
        lax.bitwise_and(ctx, 3),
        lax.bitwise_and(tp, 1),
        lax.axis_index("fsdp"),
    )


def shape(dims, kind):
    return jax.ShapeDtypeStruct(dims, kind)


def dot(a, b):
    return jnp.dot(a, b, preferred_element_type=F32)


def dot_t(a, b):
    return lax.dot_general(a, b, (((1,), (1,)), ((), ())), preferred_element_type=F32)


def pick_kernel(src, dst):
    _, _, c, h = place_of()
    for seq in range(4):
        row = src[seq, pl.ds(pl.multiple_of(c * 64, 64), 64), :]
        low, high = row[:, :384], row[:, 384:]
        rows = slice(64 * seq, 64 * seq + 64)
        dst[rows, :384] = jnp.where(h == 0, low, high)
        dst[rows, 384:] = jnp.where(h == 0, high, low)


def prepare_kernel(tokens, w, b_qv, x_ref, pack):
    pick_kernel(tokens, x_ref)
    pack[:576, :] = w[...]
    lane = lax.broadcasted_iota(jnp.int32, (96, 384), 1)
    place = lax.broadcasted_iota(jnp.int32, (96, 384), 0) + 96 * lax.axis_index("fsdp")
    spot = jnp.where(lane == place, 1.0, 0.0).astype(BF16)
    rows = jnp.concatenate([dot(b_qv[...], spot), jnp.zeros((14, 384), F32)], axis=0)
    pack[576:592, :] = rows.astype(BF16)


def vectors_kernel(v0, v1, v2, v3, v4, v5, b_in, out, rows):
    rows[...] = jnp.zeros((16, 384), F32)
    for k, ref in enumerate((v0, v1, v2, v3, v4, v5)):
        rows[k : k + 1, :] = ref[...].astype(F32).reshape(1, 384)
    rows[pl.ds(6 + lax.axis_index("fsdp"), 1), :] = b_in[...].astype(F32).reshape(1, 384)
    out[...] = rows[...].astype(BF16)


def row_of(vectors, k):
    own, other = vectors
    return jnp.concatenate([own[k : k + 1, :], other[k : k + 1, :]], axis=1).astype(F32)


def place_kernel(own, other, out):
    _, _, c, h = place_of()
    for ref, at in ((own, c), (other, 1 - c)):
        for seq in range(4):
            row = ref[64 * seq : 64 * seq + 64, :]
            first, second = row[:, :384], row[:, 384:]
            rows = pl.ds(pl.multiple_of(at * 64, 64), 64)
            out[seq, rows, :384] = jnp.where(h == 0, first, second)
            out[seq, rows, 384:] = jnp.where(h == 0, second, first)


def qkv_kernel(x_own, x_other, w_own, w_other, q_ref, kv_ref):
    bias_q = w_own[576:577, :192].astype(F32) + w_other[576:577, :192].astype(F32)
    bias_v = w_own[577:578, :192].astype(F32) + w_other[577:578, :192].astype(F32)
    for half, x in enumerate((x_own, x_other)):
        rows = slice(half * 256, half * 256 + 256)
        low, high = x[:, :384], x[:, 384:]
        query = dot_t(low, w_own[:192, :]) + dot_t(high, w_other[:192, :]) + bias_q
        q_ref[rows, :192] = (query.astype(BF16) * BF16(0.125)).astype(BF16)
        q_ref[rows, 192:] = jnp.zeros((256, 64), BF16)
        key = dot_t(low, w_own[192:384, :]) + dot_t(high, w_other[192:384, :])
        value = dot_t(low, w_own[384:576, :]) + dot_t(high, w_other[384:576, :]) + bias_v
        kv_ref[rows, :] = jnp.concatenate([key, value], axis=1).astype(BF16)


def mask_rows(lengths, away, start, count):
    z, y, c, _ = place_of()
    row = lax.broadcasted_iota(jnp.int32, (count, 128), 0) + start
    half = lax.shift_right_logical(row, 8)
    block = lax.bitwise_and(lax.shift_right_logical(row, 6), 3)
    place = (
        512 * lax.bitwise_and(z + away, 3)
        + 128 * block
        + 64 * jnp.where(half == c, 0, 1)
        + lax.bitwise_and(row, 63)
    )
    bias = jnp.where(place < lengths[y], 0.0, MASKED).astype(F32)
    return jnp.concatenate([bias] * 4, axis=1)


def head_lanes(value, head, offset):
    lane = lax.broadcasted_iota(jnp.int32, value.shape, 1)
    low = offset + 64 * head
    return jnp.where((lane >= low) & (lane < low + 64), value, jnp.zeros_like(value))


def attend_kernel(parts, first, last, lengths, q_ref, *refs):
    pieces, refs = refs[: len(parts)], refs[len(parts) :]
    if not first:
        acc_in, stat_in, refs = refs[0], refs[1], refs[2:]
    out, stat = refs
    flipped = [kv[:, 128:].astype(F32).T.astype(BF16) for kv in pieces]
    bias = [mask_rows(lengths, at, start, kv.shape[0]) for (at, start), kv in zip(parts, pieces)]
    results, tops, totals = [], [], []
    for head in range(HEADS):
        query = head_lanes(q_ref[...], head, 0)
        rows = slice(64 * head, 64 * head + 64)
        if first:
            top = jnp.full((1, 512), -1e30, F32)
            total = jnp.zeros((1, 512), F32)
            acc = jnp.zeros((64, 512), F32)
        else:
            top = stat_in[head : head + 1, :]
            total = stat_in[3 + head : 4 + head, :]
            acc = acc_in[rows, :]
        for kv, values, invalid in zip(pieces, flipped, bias):
            scores = dot_t(kv[:, :256], query) + invalid
            peak = jnp.maximum(top, jnp.max(scores, axis=0, keepdims=True))
            keep = jnp.exp(top - peak)
            expo = jnp.exp(scores - peak)
            total = total * keep + jnp.sum(expo, axis=0, keepdims=True)
            low = 64 + 64 * head
            acc = acc * keep + dot(values[low : low + 64, :], expo.astype(BF16))
            top = peak
        if last:
            results.append(acc / total)
            tops.append(top + jnp.log(total))
        else:
            out[rows, :] = acc
            stat[head : head + 1, :] = top
            stat[3 + head : 4 + head, :] = total
    if last:
        whole = jnp.concatenate([jnp.zeros((64, 512), F32)] + results, axis=0)
        out[...] = whole.T.astype(BF16)
        for head in range(HEADS):
            stat[head : head + 1, :] = tops[head]
        stat[3:8, :] = jnp.zeros((5, 512), F32)
    else:
        stat[6:8, :] = jnp.zeros((2, 512), F32)


def attend_back_kernel(parts, first, added, lengths, q_ref, do_ref, lse, inner, *refs):
    pieces, refs = refs[: len(parts)], refs[len(parts) :]
    extras = []
    for at in added:
        extras.append(None if at is None else (at, refs[0]))
        refs = refs if at is None else refs[1:]
    if not first:
        dq_in, refs = refs[0], refs[1:]
    outs, dq_ref = refs[:-1], refs[-1]
    for index, ((away, start), kv) in enumerate(zip(parts, pieces)):
        count = kv.shape[0]
        bias = mask_rows(lengths, away, start, count)
        keys, values = kv[:, :256], kv[:, 128:]
        keys_t = keys.astype(F32).T.astype(BF16)
        dk = jnp.zeros((count, 256), F32)
        dv = jnp.zeros((count, 256), F32)
        for head in range(HEADS):
            query = head_lanes(q_ref[...], head, 0)
            grad = head_lanes(do_ref[...], head, 64)
            probs = jnp.exp(dot_t(keys, query) + bias - lse[head : head + 1, :])
            grad_probs = dot_t(values, grad) - inner[head : head + 1, :]
            grad_scores = (probs * grad_probs).astype(BF16)
            dk = dk + dot(grad_scores, query)
            dv = dv + dot(probs.astype(BF16), grad)
            rows = slice(64 * head, 64 * head + 64)
            dq = dot(keys_t[rows, :], grad_scores)
            if index:
                dq = dq + dq_ref[rows, :]
            elif not first:
                dq = dq + dq_in[rows, :]
            dq_ref[rows, :] = dq
        whole = jnp.concatenate([dk[:, :128], dk[:, 128:] + dv[:, :128], dv[:, 128:]], axis=1)
        out = outs[index]
        if extras[index] is None:
            out[...] = whole.astype(BF16)
        else:
            at, extra = extras[index]
            for low in (0, 256):
                part = whole[low : low + 256]
                if low == at:
                    part = part + extra[...].astype(F32)
                out[low : low + 256, :] = part.astype(BF16)


def out_kernel(o_ref, w_own, w_other, own, other):
    for rows, ref in ((slice(256, 512), other), (slice(0, 256), own)):
        ref[:, :384] = dot(o_ref[rows, :], w_own[...]).astype(ref.dtype)
        ref[:, 384:] = dot(o_ref[rows, :], w_other[...]).astype(ref.dtype)


def normalize(value):
    center = value - jnp.mean(value, axis=1, keepdims=True)
    inverse = lax.rsqrt(jnp.mean(center * center, axis=1, keepdims=True) + EPS)
    return center * inverse, inverse


def back_normalize(grad, normed, inverse, gain):
    scaled = grad * gain
    return inverse * (
        scaled
        - jnp.mean(scaled, axis=1, keepdims=True)
        - normed * jnp.mean(scaled * normed, axis=1, keepdims=True)
    )


def column_sums(*values):
    rows = [jnp.sum(value, axis=0, keepdims=True) for value in values]
    return jnp.concatenate(rows + [jnp.zeros((8 - len(rows), rows[0].shape[1]), F32)], axis=0)


def norm_one_kernel(x, a, b, v_own, v_other, normed_ref, inverse_ref, low_ref):
    resid = x[...].astype(F32) + (a[...].astype(F32) + b[...].astype(F32)) + row_of((v_own, v_other), 0)
    normed, inverse = normalize(resid)
    normed_ref[...] = normed
    inverse_ref[...] = jnp.broadcast_to(inverse, (256, 128))
    low_ref[...] = (normed * row_of((v_own, v_other), 1) + row_of((v_own, v_other), 2)).astype(BF16)


def norm_two_kernel(
    normed_one, a, b, cot, v_own, v_other, result_ref, grad_ref, low_ref, sums_ref
):
    hidden = normed_one[...] * row_of((v_own, v_other), 1) + row_of((v_own, v_other), 2)
    resid = hidden + (a[...].astype(F32) + b[...].astype(F32)) + row_of((v_own, v_other), 3)
    normed, inverse = normalize(resid)
    gain = row_of((v_own, v_other), 4)
    result_ref[...] = (normed * gain + row_of((v_own, v_other), 5)).astype(BF16)
    dy = cot[...].astype(F32)
    grad = back_normalize(dy, normed, inverse, gain)
    grad_ref[...] = grad
    low_ref[...] = grad.astype(BF16)
    sums_ref[...] = column_sums(dy * normed, dy, grad)


def norm_back_kernel(
    grad_two, a, b, normed_one, inverse_one, v_own, v_other, grad_ref, low_ref, sums_ref
):
    dh = grad_two[...] + (a[...].astype(F32) + b[...].astype(F32))
    normed = normed_one[...]
    grad = back_normalize(dh, normed, inverse_one[:, :1], row_of((v_own, v_other), 1))
    grad_ref[...] = grad
    low_ref[...] = grad.astype(BF16)
    sums_ref[...] = column_sums(dh * normed, dh, grad)


def mlp_kernel(
    h_own,
    h_other,
    in_own,
    in_other,
    v_own,
    v_other,
    down_own,
    down_other,
    g_ref,
    slope_ref,
    own,
    other,
):
    bias = [v_own[k : k + 1, :].astype(F32) + v_other[k : k + 1, :].astype(F32) for k in (6, 7)]
    bias = jnp.concatenate(bias, axis=1)
    for rows, h, ref in ((slice(256, 512), h_other, other), (slice(0, 256), h_own, own)):
        u = dot(h[:, :384], in_own[...]) + dot(h[:, 384:], in_other[...]) + bias
        cdf = 0.5 + 0.5 * lax.erf(u * 0.7071067811865476)
        slope_ref[rows, :] = cdf + u * (0.3989422804014327 * jnp.exp(-0.5 * u * u))
        g = (u * cdf).astype(BF16)
        g_ref[rows, :] = g
        ref[:, :384] = dot(g, down_own[...]).astype(ref.dtype)
        ref[:, 384:] = dot(g, down_other[...]).astype(ref.dtype)


def mlp_back_kernel(
    dz_own, dz_other, down_own, down_other, slope, in_own, in_other, du_ref, own, other, sums_ref
):
    total = jnp.zeros((1, 768), F32)
    for rows, dz, ref in ((slice(256, 512), dz_other, other), (slice(0, 256), dz_own, own)):
        dg = dot_t(dz[:, :384], down_own[...]) + dot_t(dz[:, 384:], down_other[...])
        du = (dg * slope[rows, :]).astype(BF16)
        du_ref[rows, :] = du
        total = total + jnp.sum(du.astype(F32), axis=0, keepdims=True)
        ref[:, :384] = dot_t(du, in_own[...]).astype(ref.dtype)
        ref[:, 384:] = dot_t(du, in_other[...]).astype(ref.dtype)
    sums_ref[...] = jnp.broadcast_to(total, (8, 768))


def out_back_kernel(da_own, da_other, w_own, w_other, o_ref, do_ref, inner_ref):
    for half, da in enumerate((da_own, da_other)):
        rows = slice(half * 256, half * 256 + 256)
        value = dot_t(da[:, :384], w_own[...]) + dot_t(da[:, 384:], w_other[...])
        do_ref[rows, :] = value.astype(BF16)
    product = (do_ref[...].astype(F32) * o_ref[...].astype(F32)).T
    rows = [jnp.sum(product[64 + 64 * k : 128 + 64 * k], axis=0, keepdims=True) for k in range(HEADS)]
    inner_ref[...] = jnp.concatenate(rows + [jnp.zeros((5, 512), F32)], axis=0)


def input_back_kernel(dkv, r1, r3, dq_t, w_own, w_other, low_ref, own, other, sums_ref):
    dq = (dq_t[...].T * 0.125).astype(BF16)
    low_ref[:, :256] = jnp.concatenate([dq, jnp.zeros((512, 64), BF16)], axis=1)
    total = dkv[...].astype(F32) + r1[...].astype(F32) + r3[...].astype(F32)
    low_ref[:, 256:] = total.astype(BF16)
    sums_ref[...] = jnp.broadcast_to(
        jnp.sum(low_ref[...].astype(F32), axis=0, keepdims=True), (8, 640)
    )
    for rows, ref in ((slice(256, 512), other), (slice(0, 256), own)):
        for cols, w in ((slice(0, 384), w_own), (slice(384, 768), w_other)):
            value = dot(low_ref[rows, :192], w[:192, :]) + dot(low_ref[rows, 256:], w[192:576, :])
            ref[:, cols] = value.astype(ref.dtype)


def flip(value):
    return value.astype(F32).T.astype(BF16)


def down_grad_kernel(g_ref, dz_own, dz_other, out):
    for part in range(3):
        rows = slice(256 * part, 256 * part + 256)
        left = flip(g_ref[:, rows])
        grad = dot(left[:, :256], dz_own[...]) + dot(left[:, 256:], dz_other[...])
        out[rows, :] = grad.astype(BF16)


def in_grad_kernel(h_own, h_other, du_ref, o_ref, da_own, da_other, out):
    for cols in (slice(0, 384), slice(384, 768)):
        grad = dot(flip(h_own[:, cols]), du_ref[:256, :]) + dot(
            flip(h_other[:, cols]), du_ref[256:, :]
        )
        out[:384, cols] = grad[:, :384].astype(BF16)
        out[384:768, cols] = grad[:, 384:].astype(BF16)
    left = flip(o_ref[...])
    grad = dot(left[64:, :256], da_own[...]) + dot(left[64:, 256:], da_other[...])
    out[768:960, :] = grad.astype(BF16)
    out[960:, :] = jnp.zeros((64, 768), BF16)


def proj_grad_kernel(low_ref, x_own, x_other, sums, core_sums, sums_in, sums_qkv, out, rows):
    for to, cols in ((slice(0, 192), slice(0, 256)), (slice(192, 576), slice(256, 640))):
        left = flip(low_ref[:, cols])[: to.stop - to.start]
        grad = dot(left[:, :256], x_own[...]) + dot(left[:, 256:], x_other[...])
        out[to, :] = grad.astype(BF16)
    h = lax.axis_index("fsdp")
    rows[...] = jnp.zeros((16, 768), F32)
    rows[0:3, :] = sums[0:3, :] + core_sums[0:3, :]
    rows[3:6, :] = sums[8:11, :] + core_sums[8:11, :]
    low, high = sums_in[:1, :384], sums_in[:1, 384:]
    rows[6:7, :384] = jnp.where(h == 0, low, high)
    rows[6:7, 384:] = jnp.where(h == 0, high, low)
    for cols in (slice(0, 384), slice(384, 768)):
        rows[7:8, cols] = sums_qkv[:1, :384]
        rows[8:9, cols] = sums_qkv[:1, 256:]
    out[576:592, :] = rows[...].astype(BF16)
    out[592:, :] = jnp.zeros((48, 768), BF16)


def sum_kernel(*refs):
    own, other = refs[-2:]
    start = 0
    for terms in refs[:-2]:
        total = terms[0].astype(F32)
        for k in range(1, 16):
            total = total + terms[k].astype(F32)
        rows = slice(start, start + total.shape[0])
        own[rows, :] = total[:, :384]
        other[rows, :] = total[:, 384:].astype(BF16)
        start = rows.stop


def copies_kernel(own, other, out):
    value = (own[...] + other[...].astype(F32)).astype(BF16)
    for k in range(16):
        out[k] = value


def early_kernel(src, down, w_in, w_out):
    for k in range(16):
        down[48 * k : 48 * k + 48, :] = src[k, :48, :].astype(F32)
        value = src[k, 48:, :].astype(F32)
        if k < 6:
            w_in[64 * k : 64 * k + 64, :384] = value
        elif k < 12:
            w_in[64 * k - 384 : 64 * k - 320, 384:] = value
        elif k < 15:
            w_out[64 * k - 768 : 64 * k - 704, :] = value


def late_kernel(src, proj, b_qv, b_out, gain_one, shift_one, b_in, b_down, gain_two, shift_two):
    proj[...] = src[:576, :].astype(F32)
    rows = src[576:592, :].astype(F32)
    refs = (gain_two, shift_two, b_down, gain_one, shift_one, b_out, b_in)
    for k, ref in enumerate(refs):
        ref[...] = rows[k]
    for k, row in enumerate((rows[7:8, :192], rows[8:9, 192:])):
        b_qv[k : k + 1, :] = jnp.where(lax.axis_index("fsdp") == 0, row[:, :96], row[:, 96:])


def to_owner(value):
    own = y_exchange(value)
    (out,) = call(place_kernel, [shape((4, 128, 768), BF16)], own, core_swap(own))
    return out


def gather(*terms):
    rows = sum(term.shape[1] for term in terms)
    own, other = call(sum_kernel, [shape((rows, 384), F32), shape((rows, 384), BF16)], *terms)
    (copies,) = call(copies_kernel, [shape((16, rows, 384), BF16)], own, fsdp_swap(other))
    return ctx_exchange(copies.reshape(16 * rows, 384))


def body(
    tokens,
    cotangent,
    lengths,
    w_qkv,
    b_qv,
    w_out,
    b_out,
    ln1_gain,
    ln1_bias,
    w_in,
    b_in,
    w_down,
    b_down,
    ln2_gain,
    ln2_bias,
):
    x_mine, pack = call(
        prepare_kernel,
        [shape((256, 768), BF16), shape((592, 384), BF16)],
        tokens,
        w_qkv.transpose(0, 2, 1).reshape(576, 384),
        b_qv,
    )
    pack_other = fsdp_swap(pack)
    x_own = y_exchange(x_mine)
    x_other = core_swap(x_own)
    query, kv = call(
        qkv_kernel,
        [shape((512, 256), BF16), shape((512, 384), BF16)],
        x_own,
        x_other,
        pack,
        pack_other,
    )

    kv_low, kv_high = z_shift(kv, 1), z_shift(kv, -1)
    far_top, far_low = z_shift(kv_low[:256], 1), z_shift(kv_high[256:], -1)

    w_out, w_in, w_down, b_out, cotangent, _ = lax.optimization_barrier(
        (w_out, w_in, w_down, b_out, cotangent, kv)
    )
    out_swapped = fsdp_swap(w_out)
    in_other = fsdp_swap(w_in)
    down_other = fsdp_swap(w_down)
    out_own = jnp.pad(w_out, ((64, 0), (0, 0)))
    out_other = jnp.pad(out_swapped, ((64, 0), (0, 0)))
    (v_own,) = call(
        vectors_kernel,
        [shape((16, 384), BF16)],
        b_out,
        ln1_gain,
        ln1_bias,
        b_down,
        ln2_gain,
        ln2_bias,
        b_in,
        scratch=[pltpu.VMEM((16, 384), F32)],
    )
    v_other = fsdp_swap(v_own)
    (cot_mine,) = call(pick_kernel, [shape((256, 768), BF16)], cotangent)
    cot = y_exchange(cot_mine)

    carry = [shape((192, 512), F32), shape((8, 512), F32)]

    def attend(parts, first, last):
        return lambda *refs: attend_kernel(parts, first, last, *refs)

    acc, stat = call(attend([(0, 0)], True, False), carry, lengths, query, kv, smem=1)
    acc, stat = call(
        attend([(3, 0), (1, 0)], False, False),
        carry,
        lengths,
        query,
        kv_low,
        kv_high,
        acc,
        stat,
        smem=1,
        after=(out_swapped,),
    )
    attn, log_total = call(
        attend([(2, 0), (2, 256)], False, True),
        [shape((512, 256), BF16), shape((8, 512), F32)],
        lengths,
        query,
        far_top,
        far_low,
        acc,
        stat,
        smem=1,
        after=(in_other,),
    )
    halves = [shape((256, 768), F32), shape((256, 768), BF16)]
    own, other = call(out_kernel, halves, attn, out_own, out_other)
    a, b = tp_sum(own, other)
    normed_one, inverse_one, hidden_own = call(
        norm_one_kernel,
        [shape((256, 768), F32), shape((256, 128), F32), shape((256, 768), BF16)],
        x_own,
        a,
        b,
        v_own,
        v_other,
    )
    hidden_other = core_swap(hidden_own)
    gelu, slope, own, other = call(
        mlp_kernel,
        [shape((512, 768), BF16), shape((512, 768), F32)] + halves,
        hidden_own,
        hidden_other,
        w_in,
        in_other,
        v_own,
        v_other,
        w_down,
        down_other,
        after=(cot,),
    )
    a, b = tp_sum(own, other)
    result, grad_two, dz_own, sums_two = call(
        norm_two_kernel,
        [
            shape((256, 768), BF16),
            shape((256, 768), F32),
            shape((256, 768), BF16),
            shape((8, 768), F32),
        ],
        normed_one,
        a,
        b,
        cot,
        v_own,
        v_other,
    )
    dz_other = core_swap(dz_own)
    du, own, other, sums_in = call(
        mlp_back_kernel,
        [shape((512, 768), BF16)] + halves + [shape((8, 768), F32)],
        dz_own,
        dz_other,
        w_down,
        down_other,
        slope,
        w_in,
        in_other,
    )
    a, b = tp_sum(own, other)
    (down_terms,) = call(down_grad_kernel, [shape((768, 768), BF16)], gelu, dz_own, dz_other)
    down_terms = ctx_exchange(down_terms)
    output = to_owner(result)
    grad_one, da_own, sums_one = call(
        norm_back_kernel,
        [shape((256, 768), F32), shape((256, 768), BF16), shape((8, 768), F32)],
        grad_two,
        a,
        b,
        normed_one,
        inverse_one,
        v_own,
        v_other,
    )
    da_other = core_swap(da_own)
    grad_heads, inner = call(
        out_back_kernel,
        [shape((512, 256), BF16), shape((8, 512), F32)],
        da_own,
        da_other,
        out_own,
        out_other,
        attn,
    )
    (in_terms,) = call(
        in_grad_kernel,
        [shape((1024, 768), BF16)],
        hidden_own,
        hidden_other,
        du,
        attn,
        da_own,
        da_other,
    )
    in_terms = ctx_exchange(in_terms)

    def attend_back(parts, first, added):
        return lambda *refs: attend_back_kernel(parts, first, added, *refs)

    base = (lengths, query, grad_heads, log_total, inner)
    dq_shape = shape((192, 512), F32)
    half, whole = shape((256, 384), BF16), shape((512, 384), BF16)
    grad_top, grad_low, dq = call(
        attend_back([(2, 0), (2, 256)], True, (None, None)),
        [half, half, dq_shape],
        *base,
        far_top,
        far_low,
        smem=1,
    )
    grad_top, grad_low = z_shift(grad_top, 1), z_shift(grad_low, -1)
    grad_kv, dq = call(
        attend_back([(0, 0)], False, (None,)),
        [whole, dq_shape],
        *base,
        kv,
        dq,
        smem=1,
        after=(down_terms,),
    )
    grad_up, grad_down_z, dq = call(
        attend_back([(1, 0), (3, 0)], False, (0, 256)),
        [whole, whole, dq_shape],
        *base,
        kv_high,
        kv_low,
        grad_top,
        grad_low,
        dq,
        smem=1,
    )
    grad_qkv, own, other, sums_qkv = call(
        input_back_kernel,
        [shape((512, 640), BF16)] + halves + [shape((8, 640), F32)],
        grad_kv,
        z_shift(grad_up, 1),
        z_shift(grad_down_z, -1),
        dq,
        pack,
        pack_other,
        after=(in_terms,),
    )
    sums = jnp.concatenate([sums_two, sums_one])
    (proj_terms,) = call(
        proj_grad_kernel,
        [shape((640, 768), BF16)],
        grad_qkv,
        x_own,
        x_other,
        sums,
        core_swap(sums),
        sums_in,
        sums_qkv,
        scratch=[pltpu.VMEM((16, 768), F32)],
    )
    late = gather(ctx_exchange(proj_terms))
    early = gather(down_terms, in_terms)
    a, b = tp_sum(own, other)
    grad_x = (grad_one + (a.astype(F32) + b.astype(F32))).astype(BF16)
    grad_tokens = to_owner(grad_x)

    grad_down, grad_in, grad_out = call(
        early_kernel,
        [shape((768, 384), F32), shape((384, 768), F32), shape((192, 384), F32)],
        early,
    )
    grad_proj, grad_b_qv, *vectors = call(
        late_kernel,
        [shape((576, 384), F32), shape((2, 96), F32)] + [shape((384,), F32)] * 7,
        late.reshape(640, 384),
    )
    g_b_out, g_gain_one, g_shift_one, g_b_in, g_b_down, g_gain_two, g_shift_two = vectors
    return (
        output,
        grad_tokens,
        grad_proj.reshape(3, 192, 384).transpose(0, 2, 1),
        grad_b_qv,
        grad_out,
        g_b_out,
        g_gain_one,
        g_shift_one,
        grad_in,
        g_b_in,
        grad_down,
        g_b_down,
        g_gain_two,
        g_shift_two,
    )


def solution(mesh):
    placed = (
        P("fsdp", "ctx", None),
        P("fsdp", "ctx", None),
        P("fsdp"),
        P(None, "fsdp", "tp"),
        P(None, ("tp", "fsdp")),
        P("tp", "fsdp"),
        P("fsdp"),
        P("fsdp"),
        P("fsdp"),
        P("fsdp", "tp"),
        P(("tp", "fsdp")),
        P("tp", "fsdp"),
        P("fsdp"),
        P("fsdp"),
        P("fsdp"),
    )
    return jax.shard_map(
        body,
        mesh=mesh,
        in_specs=placed,
        out_specs=placed[:2]
        + (
            P(None, "fsdp", "tp"),
            P(None, ("tp", "fsdp")),
            P("tp", "fsdp"),
            P("fsdp"),
            P("fsdp"),
            P("fsdp"),
            P("fsdp", "tp"),
            P(("tp", "fsdp")),
            P("tp", "fsdp"),
            P("fsdp"),
            P("fsdp"),
            P("fsdp"),
        ),
        check_vma=False,
    )
```

```python
import jax
import jax.numpy as jnp
from jax import lax
from jax.experimental import pallas as pl
from jax.experimental.pallas import tpu as pltpu
from jax.sharding import PartitionSpec as P


EPS = 1e-06
MASKED = -1000000000.0
HEADS = 3
F32 = jnp.float32
BF16 = jnp.bfloat16
VMEM = pl.BlockSpec(memory_space=pltpu.VMEM)
SMEM = pl.BlockSpec(memory_space=pltpu.SMEM)


def core_swap(value):
    return lax.ppermute(value, "tp", [(t, t ^ 1) for t in range(4)])


def chip_swap(value):
    return lax.ppermute(value, "tp", [(t, t ^ 2) for t in range(4)])


def fsdp_swap(value):
    return lax.ppermute(value, "fsdp", [(0, 1), (1, 0)])


def z_shift(value, step):
    return lax.ppermute(
        value, "ctx", [(z * 4 + y, (z + step) % 4 * 4 + y) for z in range(4) for y in range(4)]
    )


def y_exchange(value):
    groups = [[z * 4 + y for y in range(4)] for z in range(4)]
    return lax.all_to_all(value, "ctx", 0, 0, axis_index_groups=groups, tiled=True)


def tp_sum(own, other):
    mine = (own + core_swap(other).astype(F32)).astype(BF16)
    return mine, chip_swap(mine)


def ctx_exchange(value):
    terms = lax.all_to_all(value, "ctx", 0, 0, tiled=True)
    return terms.reshape(16, value.shape[0] // 16, value.shape[1])


def call(kernel, outs, *args, smem=0, scratch=(), after=(), limit=8):
    count, skip = len(args), len(args) + len(after)

    def run(*refs):
        kernel(*refs[:count], *refs[skip:])

    return pl.pallas_call(
        run,
        out_shape=outs,
        in_specs=[SMEM] * smem
        + [VMEM] * (count - smem)
        + [pl.BlockSpec(memory_space=pl.ANY)] * len(after),
        out_specs=[VMEM] * len(outs),
        scratch_shapes=list(scratch),
        compiler_params=pltpu.CompilerParams(vmem_limit_bytes=limit * 1024 * 1024),
        cost_estimate=pl.CostEstimate(flops=1000, bytes_accessed=1000, transcendentals=0),
    )(*args, *after)


def place_of():
    ctx, tp = lax.axis_index("ctx"), lax.axis_index("tp")
    return (
        lax.shift_right_logical(ctx, 2),
        lax.bitwise_and(ctx, 3),
        lax.bitwise_and(tp, 1),
        lax.axis_index("fsdp"),
    )


def shape(dims, kind):
    return jax.ShapeDtypeStruct(dims, kind)


def dot(a, b):
    return jnp.dot(a, b, preferred_element_type=F32)


def dot_t(a, b):
    return lax.dot_general(a, b, (((1,), (1,)), ((), ())), preferred_element_type=F32)


def place_kernel(tokens, cotangent, out):
    _, _, c, h = place_of()
    for start, src in ((0, tokens), (64, cotangent)):
        for seq in range(4):
            row = src[seq, pl.ds(pl.multiple_of(c * 64, 64), 64), :]
            low, high = row[:, :384], row[:, 384:]
            out[seq, start : start + 64, :384] = jnp.where(h == 0, low, high)
            out[seq, start : start + 64, 384:] = jnp.where(h == 0, high, low)


def pack_kernel(w_out, w_in, w_down, v0, v1, v2, v3, v4, v5, b_in, out, vectors, whole, rows):
    whole[:192, :] = w_out[...]
    whole[192:576, :] = w_in[:, :384]
    whole[576:960, :] = w_in[:, 384:]
    whole[960:1728, :] = w_down[...]
    rows[...] = jnp.zeros((64, 384), F32)
    for k, ref in enumerate((v0, v1, v2, v3, v4, v5)):
        rows[k : k + 1, :] = ref[...].astype(F32).reshape(1, 384)
    rows[pl.ds(6 + lax.axis_index("fsdp"), 1), :] = b_in[...].astype(F32).reshape(1, 384)
    whole[1728:, :] = rows[...].astype(BF16)
    vectors[...] = rows[:16, :].astype(BF16)
    _, y, _, _ = place_of()
    out[...] = whole[pl.ds(pl.multiple_of(448 * y, 64), 448), :]


def four_kernel(src, out):
    for k in range(4):
        out[k] = src[...]


def row_of(own, pack, k):
    return jnp.concatenate([own[k : k + 1, :], pack[1728 + k : 1729 + k, :]], axis=1).astype(F32)


def return_kernel(own, other, out, grad):
    _, _, c, h = place_of()
    for ref, at in ((own, c), (other, 1 - c)):
        for start, dst in ((0, out), (64, grad)):
            for seq in range(4):
                row = ref[seq, start : start + 64, :]
                first, second = row[:, :384], row[:, 384:]
                rows = pl.ds(pl.multiple_of(at * 64, 64), 64)
                dst[seq, rows, :384] = jnp.where(h == 0, first, second)
                dst[seq, rows, 384:] = jnp.where(h == 0, second, first)


def qkv_kernel(x_own, x_other, w_own, w_other, b_own, b_other, q_ref, kv_ref):
    h = lax.axis_index("fsdp")
    lane = lax.broadcasted_iota(jnp.int32, (96, 192), 1)
    row = lax.broadcasted_iota(jnp.int32, (96, 192), 0)
    bias = jnp.zeros((2, 192), F32)
    for ref, at in ((b_own, h), (b_other, 1 - h)):
        bias = bias + dot(ref[...], jnp.where(lane == row + 96 * at, 1.0, 0.0).astype(BF16))
    bias_q, bias_v = bias[0:1], bias[1:2]
    for half, x in enumerate((x_own, x_other)):
        rows = slice(half * 256, half * 256 + 256)
        low, high = x[:, :384], x[:, 384:]
        query = dot_t(low, w_own[:192, :]) + dot_t(high, w_other[:192, :]) + bias_q
        q_ref[rows, :192] = (query.astype(BF16) * BF16(0.125)).astype(BF16)
        q_ref[rows, 192:] = jnp.zeros((256, 64), BF16)
        key = dot_t(low, w_own[192:384, :]) + dot_t(high, w_other[192:384, :])
        value = dot_t(low, w_own[384:576, :]) + dot_t(high, w_other[384:576, :]) + bias_v
        kv_ref[rows, :] = jnp.concatenate([key, value], axis=1).astype(BF16)


def mask_rows(lengths, away, start, count):
    z, y, c, _ = place_of()
    row = lax.broadcasted_iota(jnp.int32, (count, 128), 0) + start
    half = lax.shift_right_logical(row, 8)
    block = lax.bitwise_and(lax.shift_right_logical(row, 6), 3)
    place = (
        512 * lax.bitwise_and(z + away, 3)
        + 128 * block
        + 64 * jnp.where(half == c, 0, 1)
        + lax.bitwise_and(row, 63)
    )
    bias = jnp.where(place < lengths[y], 0.0, MASKED).astype(F32)
    return jnp.concatenate([bias] * 4, axis=1)


def head_lanes(value, head, offset):
    lane = lax.broadcasted_iota(jnp.int32, value.shape, 1)
    low = offset + 64 * head
    return jnp.where((lane >= low) & (lane < low + 64), value, jnp.zeros_like(value))


def attend_kernel(parts, first, last, lengths, q_ref, *refs):
    pieces, refs = refs[: len(parts)], refs[len(parts) :]
    if not first:
        acc_in, stat_in, refs = refs[0], refs[1], refs[2:]
    out, stat = refs
    flipped = [kv[:, 128:].astype(F32).T.astype(BF16) for kv in pieces]
    bias = [mask_rows(lengths, at, start, kv.shape[0]) for (at, start), kv in zip(parts, pieces)]
    results, tops, totals = [], [], []
    for head in range(HEADS):
        query = head_lanes(q_ref[...], head, 0)
        rows = slice(64 * head, 64 * head + 64)
        if first:
            top = jnp.full((1, 512), -1e30, F32)
            total = jnp.zeros((1, 512), F32)
            acc = jnp.zeros((64, 512), F32)
        else:
            top = stat_in[head : head + 1, :]
            total = stat_in[3 + head : 4 + head, :]
            acc = acc_in[rows, :]
        for kv, values, invalid in zip(pieces, flipped, bias):
            scores = dot_t(kv[:, :256], query) + invalid
            peak = jnp.maximum(top, jnp.max(scores, axis=0, keepdims=True))
            keep = jnp.exp(top - peak)
            expo = jnp.exp(scores - peak)
            total = total * keep + jnp.sum(expo, axis=0, keepdims=True)
            low = 64 + 64 * head
            acc = acc * keep + dot(values[low : low + 64, :], expo.astype(BF16))
            top = peak
        if last:
            results.append(acc / total)
            tops.append(top + jnp.log(total))
        else:
            out[rows, :] = acc
            stat[head : head + 1, :] = top
            stat[3 + head : 4 + head, :] = total
    if last:
        whole = jnp.concatenate([jnp.zeros((64, 512), F32)] + results, axis=0)
        out[...] = whole.T.astype(BF16)
        for head in range(HEADS):
            stat[head : head + 1, :] = tops[head]
        stat[3:8, :] = jnp.zeros((5, 512), F32)
    else:
        stat[6:8, :] = jnp.zeros((2, 512), F32)


def attend_back_kernel(parts, first, added, lengths, q_ref, do_ref, lse, inner, *refs):
    pieces, refs = refs[: len(parts)], refs[len(parts) :]
    extras = []
    for at in added:
        extras.append(None if at is None else (at, refs[0]))
        refs = refs if at is None else refs[1:]
    if not first:
        dq_in, refs = refs[0], refs[1:]
    outs, dq_ref = refs[:-1], refs[-1]
    for index, ((away, start), kv) in enumerate(zip(parts, pieces)):
        count = kv.shape[0]
        bias = mask_rows(lengths, away, start, count)
        keys, values = kv[:, :256], kv[:, 128:]
        keys_t = keys.astype(F32).T.astype(BF16)
        dk = jnp.zeros((count, 256), F32)
        dv = jnp.zeros((count, 256), F32)
        for head in range(HEADS):
            query = head_lanes(q_ref[...], head, 0)
            grad = head_lanes(do_ref[...], head, 64)
            probs = jnp.exp(dot_t(keys, query) + bias - lse[head : head + 1, :])
            grad_probs = dot_t(values, grad) - inner[head : head + 1, :]
            grad_scores = (probs * grad_probs).astype(BF16)
            dk = dk + dot(grad_scores, query)
            dv = dv + dot(probs.astype(BF16), grad)
            rows = slice(64 * head, 64 * head + 64)
            dq = dot(keys_t[rows, :], grad_scores)
            if index:
                dq = dq + dq_ref[rows, :]
            elif not first:
                dq = dq + dq_in[rows, :]
            dq_ref[rows, :] = dq
        whole = jnp.concatenate([dk[:, :128], dk[:, 128:] + dv[:, :128], dv[:, 128:]], axis=1)
        out = outs[index]
        if extras[index] is None:
            out[...] = whole.astype(BF16)
        else:
            at, extra = extras[index]
            for low in (0, 256):
                part = whole[low : low + 256]
                if low == at:
                    part = part + extra[...].astype(F32)
                out[low : low + 256, :] = part.astype(BF16)


def under_zeros(w):
    return jnp.concatenate([jnp.zeros((64, 384), BF16), w], axis=0)


def out_kernel(o_ref, w_own, pack, own, other):
    weights = under_zeros(w_own[...]), under_zeros(pack[:192, :])
    for rows, ref in ((slice(256, 512), other), (slice(0, 256), own)):
        ref[:, :384] = dot(o_ref[rows, :], weights[0]).astype(ref.dtype)
        ref[:, 384:] = dot(o_ref[rows, :], weights[1]).astype(ref.dtype)


def normalize(value):
    center = value - jnp.mean(value, axis=1, keepdims=True)
    inverse = lax.rsqrt(jnp.mean(center * center, axis=1, keepdims=True) + EPS)
    return center * inverse, inverse


def back_normalize(grad, normed, inverse, gain):
    scaled = grad * gain
    return inverse * (
        scaled
        - jnp.mean(scaled, axis=1, keepdims=True)
        - normed * jnp.mean(scaled * normed, axis=1, keepdims=True)
    )


def column_sums(*values):
    rows = [jnp.sum(value, axis=0, keepdims=True) for value in values]
    return jnp.concatenate(rows + [jnp.zeros((8 - len(rows), rows[0].shape[1]), F32)], axis=0)


def norm_one_kernel(x, a, b, v_own, pack, normed_ref, inverse_ref, low_ref):
    resid = x[...].astype(F32) + (a[...].astype(F32) + b[...].astype(F32)) + row_of(v_own, pack, 0)
    normed, inverse = normalize(resid)
    normed_ref[...] = normed
    inverse_ref[...] = jnp.broadcast_to(inverse, (256, 128))
    low_ref[...] = (normed * row_of(v_own, pack, 1) + row_of(v_own, pack, 2)).astype(BF16)


def norm_two_kernel(
    normed_one, a, b, cot, v_own, pack, result_ref, grad_ref, low_ref, sums_ref
):
    hidden = normed_one[...] * row_of(v_own, pack, 1) + row_of(v_own, pack, 2)
    resid = hidden + (a[...].astype(F32) + b[...].astype(F32)) + row_of(v_own, pack, 3)
    normed, inverse = normalize(resid)
    gain = row_of(v_own, pack, 4)
    result_ref[...] = (normed * gain + row_of(v_own, pack, 5)).astype(BF16)
    dy = cot[...].astype(F32)
    grad = back_normalize(dy, normed, inverse, gain)
    grad_ref[...] = grad
    low_ref[...] = grad.astype(BF16)
    sums_ref[...] = column_sums(dy * normed, dy, grad)


def norm_back_kernel(
    grad_two, a, b, normed_one, inverse_one, v_own, pack, grad_ref, low_ref, sums_ref
):
    dh = grad_two[...] + (a[...].astype(F32) + b[...].astype(F32))
    normed = normed_one[...]
    grad = back_normalize(dh, normed, inverse_one[:, :1], row_of(v_own, pack, 1))
    grad_ref[...] = grad
    low_ref[...] = grad.astype(BF16)
    sums_ref[...] = column_sums(dh * normed, dh, grad)


def mlp_kernel(h_own, h_other, w_in, w_down, pack, v_own, g_ref, slope_ref, own, other):
    bias = [v_own[k : k + 1, :].astype(F32) + pack[1728 + k : 1729 + k, :].astype(F32) for k in (6, 7)]
    for rows, h, ref in ((slice(256, 512), h_other, other), (slice(0, 256), h_own, own)):
        for k, cols in enumerate((slice(0, 384), slice(384, 768))):
            u = dot(h[:, :384], w_in[:, cols]) + bias[k]
            u = u + dot(h[:, 384:], pack[192 + 384 * k : 576 + 384 * k, :])
            cdf = 0.5 + 0.5 * lax.erf(u * 0.7071067811865476)
            slope_ref[rows, cols] = cdf + u * (0.3989422804014327 * jnp.exp(-0.5 * u * u))
            g_ref[rows, cols] = (u * cdf).astype(BF16)
        g = g_ref[rows, :]
        ref[:, :384] = dot(g, w_down[...]).astype(ref.dtype)
        ref[:, 384:] = dot(g, pack[960:1728, :]).astype(ref.dtype)


def mlp_back_kernel(
    dz_own, dz_other, w_in, w_down, pack, slope, du_ref, own, other, sums_ref
):
    total = jnp.zeros((1, 768), F32)
    for rows, dz, ref in ((slice(256, 512), dz_other, other), (slice(0, 256), dz_own, own)):
        dg = dot_t(dz[:, :384], w_down[...]) + dot_t(dz[:, 384:], pack[960:1728, :])
        du = (dg * slope[rows, :]).astype(BF16)
        du_ref[rows, :] = du
        total = total + jnp.sum(du.astype(F32), axis=0, keepdims=True)
        ref[:, :384] = dot_t(du, w_in[...]).astype(ref.dtype)
        high = dot_t(du[:, :384], pack[192:576, :]) + dot_t(du[:, 384:], pack[576:960, :])
        ref[:, 384:] = high.astype(ref.dtype)
    sums_ref[...] = jnp.broadcast_to(total, (8, 768))


def out_back_kernel(da_own, da_other, w_own, pack, o_ref, do_ref, inner_ref):
    weights = under_zeros(w_own[...]), under_zeros(pack[:192, :])
    for half, da in enumerate((da_own, da_other)):
        rows = slice(half * 256, half * 256 + 256)
        value = dot_t(da[:, :384], weights[0]) + dot_t(da[:, 384:], weights[1])
        do_ref[rows, :] = value.astype(BF16)
    product = (do_ref[...].astype(F32) * o_ref[...].astype(F32)).T
    rows = [jnp.sum(product[64 + 64 * k : 128 + 64 * k], axis=0, keepdims=True) for k in range(HEADS)]
    inner_ref[...] = jnp.concatenate(rows + [jnp.zeros((5, 512), F32)], axis=0)


def input_back_kernel(dkv, r1, r3, dq_t, w_own, w_other, low_ref, own, other, sums_ref):
    dq = (dq_t[...].T * 0.125).astype(BF16)
    low_ref[:, :256] = jnp.concatenate([dq, jnp.zeros((512, 64), BF16)], axis=1)
    total = dkv[...].astype(F32) + r1[...].astype(F32) + r3[...].astype(F32)
    low_ref[:, 256:] = total.astype(BF16)
    sums_ref[...] = jnp.broadcast_to(
        jnp.sum(low_ref[...].astype(F32), axis=0, keepdims=True), (8, 640)
    )
    for rows, ref in ((slice(256, 512), other), (slice(0, 256), own)):
        for cols, w in ((slice(0, 384), w_own), (slice(384, 768), w_other)):
            value = dot(low_ref[rows, :192], w[:192, :]) + dot(low_ref[rows, 256:], w[192:576, :])
            ref[:, cols] = value.astype(ref.dtype)


def flip(value):
    return value.astype(F32).T.astype(BF16)


def down_grad_kernel(g_ref, dz_own, dz_other, out):
    for part in range(3):
        rows = slice(256 * part, 256 * part + 256)
        left = flip(g_ref[:, rows])
        grad = dot(left[:, :256], dz_own[...]) + dot(left[:, 256:], dz_other[...])
        out[rows, :] = grad.astype(BF16)


def in_grad_kernel(h_own, h_other, du_ref, o_ref, da_own, da_other, out):
    for cols in (slice(0, 384), slice(384, 768)):
        grad = dot(flip(h_own[:, cols]), du_ref[:256, :]) + dot(
            flip(h_other[:, cols]), du_ref[256:, :]
        )
        out[:384, cols] = grad[:, :384].astype(BF16)
        out[384:768, cols] = grad[:, 384:].astype(BF16)
    left = flip(o_ref[...])
    grad = dot(left[64:, :256], da_own[...]) + dot(left[64:, 256:], da_other[...])
    out[768:960, :] = grad.astype(BF16)
    out[960:, :] = jnp.zeros((64, 768), BF16)


def proj_grad_kernel(low_ref, x_own, x_other, sums, core_sums, sums_in, sums_qkv, out, rows):
    for to, cols in ((slice(0, 192), slice(0, 256)), (slice(192, 576), slice(256, 640))):
        left = flip(low_ref[:, cols])[: to.stop - to.start]
        grad = dot(left[:, :256], x_own[...]) + dot(left[:, 256:], x_other[...])
        out[to, :] = grad.astype(BF16)
    h = lax.axis_index("fsdp")
    rows[...] = jnp.zeros((16, 768), F32)
    rows[0:3, :] = sums[0:3, :] + core_sums[0:3, :]
    rows[3:6, :] = sums[8:11, :] + core_sums[8:11, :]
    low, high = sums_in[:1, :384], sums_in[:1, 384:]
    rows[6:7, :384] = jnp.where(h == 0, low, high)
    rows[6:7, 384:] = jnp.where(h == 0, high, low)
    for cols in (slice(0, 384), slice(384, 768)):
        rows[7:8, cols] = sums_qkv[:1, :384]
        rows[8:9, cols] = sums_qkv[:1, 256:]
    out[576:592, :] = rows[...].astype(BF16)
    out[592:, :] = jnp.zeros((48, 768), BF16)


def sum_kernel(*refs):
    own, other = refs[-2:]
    start = 0
    for terms in refs[:-2]:
        total = terms[0].astype(F32)
        for k in range(1, 16):
            total = total + terms[k].astype(F32)
        rows = slice(start, start + total.shape[0])
        own[rows, :] = total[:, :384]
        other[rows, :] = total[:, 384:].astype(BF16)
        start = rows.stop


def copies_kernel(own, other, own_late, other_late, out):
    early = (own[...] + other[...].astype(F32)).astype(BF16)
    late = (own_late[...] + other_late[...].astype(F32)).astype(BF16)
    for k in range(16):
        out[k, :112, :] = early
        out[k, 112:, :] = late


def grads_kernel(src, down, w_in, w_out, proj, b_qv, *refs):
    vectors, rows = refs[:7], refs[7]
    for k in range(16):
        down[48 * k : 48 * k + 48, :] = src[k, :48, :].astype(F32)
        value = src[k, 48:112, :].astype(F32)
        if k < 6:
            w_in[64 * k : 64 * k + 64, :384] = value
        elif k < 12:
            w_in[64 * k - 384 : 64 * k - 320, 384:] = value
        elif k < 15:
            w_out[64 * k - 768 : 64 * k - 704, :] = value
        rows[40 * k : 40 * k + 40, :] = src[k, 112:, :].astype(F32)
    proj[...] = rows[:576, :]
    for k, ref in enumerate(vectors):
        ref[...] = rows[576 + k, :]
    for k, row in enumerate((rows[583:584, :192], rows[584:585, 192:])):
        b_qv[k : k + 1, :] = jnp.where(lax.axis_index("fsdp") == 0, row[:, :96], row[:, 96:])


def ctx_sum(*terms):
    rows = sum(term.shape[1] for term in terms)
    own, other = call(sum_kernel, [shape((rows, 384), F32), shape((rows, 384), BF16)], *terms)
    return own, fsdp_swap(other)


def body(
    tokens,
    cotangent,
    lengths,
    w_qkv,
    b_qv,
    w_out,
    b_out,
    ln1_gain,
    ln1_bias,
    w_in,
    b_in,
    w_down,
    b_down,
    ln2_gain,
    ln2_bias,
):
    wt_own = w_qkv.transpose(0, 2, 1).reshape(576, 384)
    wt_other = fsdp_swap(wt_own)
    b_other = fsdp_swap(b_qv)
    (placed,) = call(place_kernel, [shape((4, 128, 768), BF16)], tokens, cotangent)
    placed = y_exchange(placed)
    x_own = placed[:, :64].reshape(256, 768)
    x_other = core_swap(x_own)
    query, kv = call(
        qkv_kernel,
        [shape((512, 256), BF16), shape((512, 384), BF16)],
        x_own,
        x_other,
        wt_own,
        wt_other,
        b_qv,
        b_other,
    )
    cot = placed[:, 64:].reshape(256, 768)

    quarter, v_own = call(
        pack_kernel,
        [shape((448, 384), BF16), shape((16, 384), BF16)],
        w_out,
        w_in,
        w_down,
        b_out,
        ln1_gain,
        ln1_bias,
        b_down,
        ln2_gain,
        ln2_bias,
        b_in,
        scratch=[pltpu.VMEM((1792, 384), BF16), pltpu.VMEM((64, 384), F32)],
    )
    quarter, _ = lax.optimization_barrier((quarter, x_own))
    (quarters,) = call(four_kernel, [shape((4, 448, 384), BF16)], fsdp_swap(quarter))
    pack = y_exchange(quarters).reshape(1792, 384)

    kv_low, kv_high = z_shift(kv, 1), z_shift(kv, -1)
    carry = [shape((192, 512), F32), shape((8, 512), F32)]

    def attend(parts, first, last):
        return lambda *refs: attend_kernel(parts, first, last, *refs)

    acc, stat = call(attend([(0, 0)], True, False), carry, lengths, query, kv, smem=1, limit=16)
    pass_up, pass_down, acc = lax.optimization_barrier((kv_low[:256], kv_high[256:], acc))
    far_top, far_low = z_shift(pass_up, 1), z_shift(pass_down, -1)
    acc, stat = call(
        attend([(3, 0), (1, 0)], False, False),
        carry,
        lengths,
        query,
        kv_low,
        kv_high,
        acc,
        stat,
        smem=1,
        limit=16,
    )
    attn, log_total = call(
        attend([(2, 0), (2, 256)], False, True),
        [shape((512, 256), BF16), shape((8, 512), F32)],
        lengths,
        query,
        far_top,
        far_low,
        acc,
        stat,
        smem=1,
        after=(pack,),
        limit=16,
    )
    halves = [shape((256, 768), F32), shape((256, 768), BF16)]
    own, other = call(out_kernel, halves, attn, w_out, pack)
    a, b = tp_sum(own, other)
    normed_one, inverse_one, hidden_own = call(
        norm_one_kernel,
        [shape((256, 768), F32), shape((256, 128), F32), shape((256, 768), BF16)],
        x_own,
        a,
        b,
        v_own,
        pack,
    )
    hidden_other = core_swap(hidden_own)
    gelu, slope, own, other = call(
        mlp_kernel,
        [shape((512, 768), BF16), shape((512, 768), F32)] + halves,
        hidden_own,
        hidden_other,
        w_in,
        w_down,
        pack,
        v_own,
    )
    a, b = tp_sum(own, other)
    result, grad_two, dz_own, sums_two = call(
        norm_two_kernel,
        [
            shape((256, 768), BF16),
            shape((256, 768), F32),
            shape((256, 768), BF16),
            shape((8, 768), F32),
        ],
        normed_one,
        a,
        b,
        cot,
        v_own,
        pack,
    )
    dz_other = core_swap(dz_own)
    du, own, other, sums_in = call(
        mlp_back_kernel,
        [shape((512, 768), BF16)] + halves + [shape((8, 768), F32)],
        dz_own,
        dz_other,
        w_in,
        w_down,
        pack,
        slope,
    )
    a, b = tp_sum(own, other)
    (down_terms,) = call(down_grad_kernel, [shape((768, 768), BF16)], gelu, dz_own, dz_other)
    down_terms = ctx_exchange(down_terms)
    grad_one, da_own, sums_one = call(
        norm_back_kernel,
        [shape((256, 768), F32), shape((256, 768), BF16), shape((8, 768), F32)],
        grad_two,
        a,
        b,
        normed_one,
        inverse_one,
        v_own,
        pack,
    )
    da_other = core_swap(da_own)
    grad_heads, inner = call(
        out_back_kernel,
        [shape((512, 256), BF16), shape((8, 512), F32)],
        da_own,
        da_other,
        w_out,
        pack,
        attn,
    )
    (in_terms,) = call(
        in_grad_kernel,
        [shape((1024, 768), BF16)],
        hidden_own,
        hidden_other,
        du,
        attn,
        da_own,
        da_other,
    )
    in_terms = ctx_exchange(in_terms)

    def attend_back(parts, first, added):
        return lambda *refs: attend_back_kernel(parts, first, added, *refs)

    base = (lengths, query, grad_heads, log_total, inner)
    dq_shape = shape((192, 512), F32)
    half, whole = shape((256, 384), BF16), shape((512, 384), BF16)
    grad_top, grad_low, dq = call(
        attend_back([(2, 0), (2, 256)], True, (None, None)),
        [half, half, dq_shape],
        *base,
        far_top,
        far_low,
        smem=1,
        limit=16,
    )
    grad_top, grad_low = z_shift(grad_top, 1), z_shift(grad_low, -1)
    grad_kv, dq = call(
        attend_back([(0, 0)], False, (None,)),
        [whole, dq_shape],
        *base,
        kv,
        dq,
        smem=1,
        after=(down_terms,),
        limit=16,
    )
    grad_up, grad_down_z, dq = call(
        attend_back([(1, 0), (3, 0)], False, (0, 256)),
        [whole, whole, dq_shape],
        *base,
        kv_high,
        kv_low,
        grad_top,
        grad_low,
        dq,
        smem=1,
        limit=16,
    )
    early_own, early_other = ctx_sum(down_terms, in_terms)
    grad_qkv, own, other, sums_qkv = call(
        input_back_kernel,
        [shape((512, 640), BF16)] + halves + [shape((8, 640), F32)],
        grad_kv,
        z_shift(grad_up, 1),
        z_shift(grad_down_z, -1),
        dq,
        wt_own,
        wt_other,
        after=(early_other,),
    )
    sums = jnp.concatenate([sums_two, sums_one])
    (proj_terms,) = call(
        proj_grad_kernel,
        [shape((640, 768), BF16)],
        grad_qkv,
        x_own,
        x_other,
        sums,
        core_swap(sums),
        sums_in,
        sums_qkv,
        scratch=[pltpu.VMEM((16, 768), F32)],
    )
    late_own, late_other = ctx_sum(ctx_exchange(proj_terms))
    (copies,) = call(
        copies_kernel,
        [shape((16, 152, 384), BF16)],
        early_own,
        early_other,
        late_own,
        late_other,
    )
    grads = ctx_exchange(copies.reshape(16 * 152, 384))
    a, b = tp_sum(own, other)
    grad_x = (grad_one + (a.astype(F32) + b.astype(F32))).astype(BF16)
    back = y_exchange(
        jnp.concatenate([result.reshape(4, 64, 768), grad_x.reshape(4, 64, 768)], axis=1)
    )
    output, grad_tokens = call(
        return_kernel, [shape((4, 128, 768), BF16)] * 2, back, core_swap(back)
    )
    grad_down, grad_in, grad_out, grad_proj, grad_b_qv, *vectors = call(
        grads_kernel,
        [
            shape((768, 384), F32),
            shape((384, 768), F32),
            shape((192, 384), F32),
            shape((576, 384), F32),
            shape((2, 96), F32),
        ]
        + [shape((384,), F32)] * 7,
        grads,
        scratch=[pltpu.VMEM((640, 384), F32)],
    )
    g_gain_two, g_shift_two, g_b_down, g_gain_one, g_shift_one, g_b_out, g_b_in = vectors
    return (
        output,
        grad_tokens,
        grad_proj.reshape(3, 192, 384).transpose(0, 2, 1),
        grad_b_qv,
        grad_out,
        g_b_out,
        g_gain_one,
        g_shift_one,
        grad_in,
        g_b_in,
        grad_down,
        g_b_down,
        g_gain_two,
        g_shift_two,
    )


def solution(mesh):
    placed = (
        P("fsdp", "ctx", None),
        P("fsdp", "ctx", None),
        P("fsdp"),
        P(None, "fsdp", "tp"),
        P(None, ("tp", "fsdp")),
        P("tp", "fsdp"),
        P("fsdp"),
        P("fsdp"),
        P("fsdp"),
        P("fsdp", "tp"),
        P(("tp", "fsdp")),
        P("tp", "fsdp"),
        P("fsdp"),
        P("fsdp"),
        P("fsdp"),
    )
    return jax.shard_map(
        body,
        mesh=mesh,
        in_specs=placed,
        out_specs=placed[:2]
        + (
            P(None, "fsdp", "tp"),
            P(None, ("tp", "fsdp")),
            P("tp", "fsdp"),
            P("fsdp"),
            P("fsdp"),
            P("fsdp"),
            P("fsdp", "tp"),
            P(("tp", "fsdp")),
            P("tp", "fsdp"),
            P("fsdp"),
            P("fsdp"),
            P("fsdp"),
        ),
        check_vma=False,
    )
```

```python
import jax
import jax.numpy as jnp
from jax import lax
from jax.experimental import pallas as pl
from jax.experimental.pallas import tpu as pltpu
from jax.sharding import PartitionSpec as P


EPS = 1e-06
MASKED = -1000000000.0
HEADS = 3
F32 = jnp.float32
BF16 = jnp.bfloat16
VMEM = pl.BlockSpec(memory_space=pltpu.VMEM)
SMEM = pl.BlockSpec(memory_space=pltpu.SMEM)


def core_swap(value):
    return lax.ppermute(value, "tp", [(t, t ^ 1) for t in range(4)])


def chip_swap(value):
    return lax.ppermute(value, "tp", [(t, t ^ 2) for t in range(4)])


def fsdp_swap(value):
    return lax.ppermute(value, "fsdp", [(0, 1), (1, 0)])


def z_shift(value, step):
    return lax.ppermute(
        value, "ctx", [(z * 4 + y, (z + step) % 4 * 4 + y) for z in range(4) for y in range(4)]
    )


def y_shift(value, step):
    return lax.ppermute(
        value, "ctx", [(z * 4 + y, z * 4 + (y + step) % 4) for z in range(4) for y in range(4)]
    )


def y_exchange(value):
    groups = [[z * 4 + y for y in range(4)] for z in range(4)]
    return lax.all_to_all(value, "ctx", 0, 0, axis_index_groups=groups, tiled=True)


def tp_sum(own, other):
    mine = (own + core_swap(other).astype(F32)).astype(BF16)
    return mine, chip_swap(mine)


def ctx_exchange(value):
    terms = lax.all_to_all(value, "ctx", 0, 0, tiled=True)
    return terms.reshape(16, value.shape[0] // 16, value.shape[1])


def call(kernel, outs, *args, smem=0, scratch=(), after=(), limit=8, load=VMEM, us=0.1):
    count, skip = len(args), len(args) + len(after)

    def run(*refs):
        kernel(*refs[:count], *refs[skip:])

    return pl.pallas_call(
        run,
        out_shape=outs,
        in_specs=[SMEM] * smem
        + [load] * (count - smem)
        + [pl.BlockSpec(memory_space=pl.ANY)] * len(after),
        out_specs=[VMEM] * len(outs),
        scratch_shapes=list(scratch),
        compiler_params=pltpu.CompilerParams(vmem_limit_bytes=limit * 1024 * 1024),
        cost_estimate=pl.CostEstimate(
            flops=int(us * 1e9), bytes_accessed=1000, transcendentals=0
        ),
    )(*args, *after)


def place_of():
    ctx, tp = lax.axis_index("ctx"), lax.axis_index("tp")
    return (
        lax.shift_right_logical(ctx, 2),
        lax.bitwise_and(ctx, 3),
        lax.bitwise_and(tp, 1),
        lax.axis_index("fsdp"),
    )


def shape(dims, kind):
    return jax.ShapeDtypeStruct(dims, kind)


def dot(a, b):
    return jnp.dot(a, b, preferred_element_type=F32)


def dot_t(a, b):
    return lax.dot_general(a, b, (((1,), (1,)), ((), ())), preferred_element_type=F32)


def place_kernel(tokens, cotangent, out):
    _, _, c, h = place_of()
    for start, src in ((0, tokens), (64, cotangent)):
        for seq in range(4):
            row = src[seq, pl.ds(pl.multiple_of(c * 64, 64), 64), :]
            low, high = row[:, :384], row[:, 384:]
            out[seq, start : start + 64, :384] = jnp.where(h == 0, low, high)
            out[seq, start : start + 64, 384:] = jnp.where(h == 0, high, low)


def pack_kernel(w_out, w_in, v0, v1, v2, v3, v4, v5, b_in, whole, vectors, rows):
    whole[:192, :] = w_out[...]
    whole[192:576, :] = w_in[:, :384]
    whole[576:960, :] = w_in[:, 384:]
    rows[...] = jnp.zeros((16, 384), F32)
    for k, ref in enumerate((v0, v1, v2, v3, v4, v5)):
        rows[k : k + 1, :] = ref[...].astype(F32).reshape(1, 384)
    rows[pl.ds(6 + lax.axis_index("fsdp"), 1), :] = b_in[...].astype(F32).reshape(1, 384)
    whole[960:, :] = rows[...].astype(BF16)
    vectors[...] = rows[...].astype(BF16)


def prepare_kernel(tokens, cotangent, w, b_qv, out, pack):
    place_kernel(tokens, cotangent, out)
    pack[:576, :] = w[...]
    lane = lax.broadcasted_iota(jnp.int32, (96, 384), 1)
    place = lax.broadcasted_iota(jnp.int32, (96, 384), 0) + 96 * lax.axis_index("fsdp")
    spot = jnp.where(lane == place, 1.0, 0.0).astype(BF16)
    rows = jnp.concatenate([dot(b_qv[...], spot), jnp.zeros((14, 384), F32)], axis=0)
    pack[576:592, :] = rows.astype(BF16)


def row_of(own, pack, k):
    return jnp.concatenate([own[k : k + 1, :], pack[960 + k : 961 + k, :]], axis=1).astype(F32)


def split_kernel(output, grad, *pieces):
    _, y, _, _ = place_of()
    for step in range(4):
        rows = pl.ds(pl.multiple_of(64 * lax.bitwise_and(y + step, 3), 64), 64)
        pieces[step][:64, :] = output[rows, :]
        pieces[step][64:, :] = grad[rows, :]


def return_kernel(own, other, out, grad):
    _, y, c, h = place_of()
    for ref, at in ((own, c), (other, 1 - c)):
        for start, dst in ((0, out), (64, grad)):
            for step in range(4):
                row = ref[128 * step + start : 128 * step + start + 64, :]
                first, second = row[:, :384], row[:, 384:]
                rows = pl.ds(pl.multiple_of(at * 64, 64), 64)
                seq = lax.bitwise_and(y + 4 - step, 3)
                dst[seq, rows, :384] = jnp.where(h == 0, first, second)
                dst[seq, rows, 384:] = jnp.where(h == 0, second, first)


def qkv_kernel(x_own, x_other, w_own, w_other, q_ref, kv_ref):
    bias = w_own[576:592, :192].astype(F32) + w_other[576:592, :192].astype(F32)
    bias_q, bias_v = bias[0:1], bias[1:2]
    for half, x in enumerate((x_own, x_other)):
        rows = slice(half * 256, half * 256 + 256)
        low, high = x[:, :384], x[:, 384:]
        query = dot_t(low, w_own[:192, :]) + dot_t(high, w_other[:192, :]) + bias_q
        q_ref[rows, :192] = (query.astype(BF16) * BF16(0.125)).astype(BF16)
        q_ref[rows, 192:] = jnp.zeros((256, 64), BF16)
        key = dot_t(low, w_own[192:384, :]) + dot_t(high, w_other[192:384, :])
        value = dot_t(low, w_own[384:576, :]) + dot_t(high, w_other[384:576, :]) + bias_v
        kv_ref[rows, :] = jnp.concatenate([key, value], axis=1).astype(BF16)


def mask_rows(lengths, away, start, count):
    z, y, c, _ = place_of()
    row = lax.broadcasted_iota(jnp.int32, (count, 128), 0) + start
    half = lax.shift_right_logical(row, 8)
    block = lax.bitwise_and(lax.shift_right_logical(row, 6), 3)
    place = (
        512 * lax.bitwise_and(z + away, 3)
        + 128 * block
        + 64 * jnp.where(half == c, 0, 1)
        + lax.bitwise_and(row, 63)
    )
    bias = jnp.where(place < lengths[y], 0.0, MASKED).astype(F32)
    return jnp.concatenate([bias] * 4, axis=1)


def head_lanes(value, head, offset):
    lane = lax.broadcasted_iota(jnp.int32, value.shape, 1)
    low = offset + 64 * head
    return jnp.where((lane >= low) & (lane < low + 64), value, jnp.zeros_like(value))


def attend_kernel(parts, first, last, lengths, q_ref, *refs):
    pieces, refs = refs[: len(parts)], refs[len(parts) :]
    if not first:
        acc_in, stat_in, refs = refs[0], refs[1], refs[2:]
    out, stat = refs
    flipped = [kv[:, 128:].astype(F32).T.astype(BF16) for kv in pieces]
    bias = [mask_rows(lengths, at, start, kv.shape[0]) for (at, start), kv in zip(parts, pieces)]
    results, tops, totals = [], [], []
    for head in range(HEADS):
        query = head_lanes(q_ref[...], head, 0)
        rows = slice(64 * head, 64 * head + 64)
        if first:
            top = jnp.full((1, 512), -1e30, F32)
            total = jnp.zeros((1, 512), F32)
            acc = jnp.zeros((64, 512), F32)
        else:
            top = stat_in[head : head + 1, :]
            total = stat_in[3 + head : 4 + head, :]
            acc = acc_in[rows, :]
        for kv, values, invalid in zip(pieces, flipped, bias):
            scores = dot_t(kv[:, :256], query) + invalid
            peak = jnp.maximum(top, jnp.max(scores, axis=0, keepdims=True))
            keep = jnp.exp(top - peak)
            expo = jnp.exp(scores - peak)
            total = total * keep + jnp.sum(expo, axis=0, keepdims=True)
            low = 64 + 64 * head
            acc = acc * keep + dot(values[low : low + 64, :], expo.astype(BF16))
            top = peak
        if last:
            results.append(acc / total)
            tops.append(top + jnp.log(total))
        else:
            out[rows, :] = acc
            stat[head : head + 1, :] = top
            stat[3 + head : 4 + head, :] = total
    if last:
        whole = jnp.concatenate([jnp.zeros((64, 512), F32)] + results, axis=0)
        out[...] = whole.T.astype(BF16)
        for head in range(HEADS):
            stat[head : head + 1, :] = tops[head]
        stat[3:8, :] = jnp.zeros((5, 512), F32)
    else:
        stat[6:8, :] = jnp.zeros((2, 512), F32)


def attend_back_kernel(parts, first, added, lengths, q_ref, do_ref, lse, inner, *refs):
    pieces, refs = refs[: len(parts)], refs[len(parts) :]
    extras = []
    for at in added:
        extras.append(None if at is None else (at, refs[0]))
        refs = refs if at is None else refs[1:]
    if not first:
        dq_in, refs = refs[0], refs[1:]
    outs, dq_ref = refs[:-1], refs[-1]
    for index, ((away, start), kv) in enumerate(zip(parts, pieces)):
        count = kv.shape[0]
        bias = mask_rows(lengths, away, start, count)
        keys, values = kv[:, :256], kv[:, 128:]
        keys_t = keys.astype(F32).T.astype(BF16)
        dk = jnp.zeros((count, 256), F32)
        dv = jnp.zeros((count, 256), F32)
        for head in range(HEADS):
            query = head_lanes(q_ref[...], head, 0)
            grad = head_lanes(do_ref[...], head, 64)
            probs = jnp.exp(dot_t(keys, query) + bias - lse[head : head + 1, :])
            grad_probs = dot_t(values, grad) - inner[head : head + 1, :]
            grad_scores = (probs * grad_probs).astype(BF16)
            dk = dk + dot(grad_scores, query)
            dv = dv + dot(probs.astype(BF16), grad)
            rows = slice(64 * head, 64 * head + 64)
            dq = dot(keys_t[rows, :], grad_scores)
            if index:
                dq = dq + dq_ref[rows, :]
            elif not first:
                dq = dq + dq_in[rows, :]
            dq_ref[rows, :] = dq
        whole = jnp.concatenate([dk[:, :128], dk[:, 128:] + dv[:, :128], dv[:, 128:]], axis=1)
        out = outs[index]
        if extras[index] is None:
            out[...] = whole.astype(BF16)
        else:
            at, extra = extras[index]
            for low in (0, 256):
                part = whole[low : low + 256]
                if low == at:
                    part = part + extra[...].astype(F32)
                out[low : low + 256, :] = part.astype(BF16)


def under_zeros(w):
    return jnp.concatenate([jnp.zeros((64, 384), BF16), w], axis=0)


def out_kernel(o_ref, w_own, pack, own, other):
    weights = under_zeros(w_own[...]), under_zeros(pack[:192, :])
    for rows, ref in ((slice(256, 512), other), (slice(0, 256), own)):
        ref[:, :384] = dot(o_ref[rows, :], weights[0]).astype(ref.dtype)
        ref[:, 384:] = dot(o_ref[rows, :], weights[1]).astype(ref.dtype)


def normalize(value):
    center = value - jnp.mean(value, axis=1, keepdims=True)
    inverse = lax.rsqrt(jnp.mean(center * center, axis=1, keepdims=True) + EPS)
    return center * inverse, inverse


def back_normalize(grad, normed, inverse, gain):
    scaled = grad * gain
    return inverse * (
        scaled
        - jnp.mean(scaled, axis=1, keepdims=True)
        - normed * jnp.mean(scaled * normed, axis=1, keepdims=True)
    )


def column_sums(*values):
    rows = [jnp.sum(value, axis=0, keepdims=True) for value in values]
    return jnp.concatenate(rows + [jnp.zeros((8 - len(rows), rows[0].shape[1]), F32)], axis=0)


def norm_one_kernel(x, a, b, v_own, pack, normed_ref, inverse_ref, low_ref):
    resid = x[...].astype(F32) + (a[...].astype(F32) + b[...].astype(F32)) + row_of(v_own, pack, 0)
    normed, inverse = normalize(resid)
    normed_ref[...] = normed
    inverse_ref[...] = jnp.broadcast_to(inverse, (256, 128))
    low_ref[...] = (normed * row_of(v_own, pack, 1) + row_of(v_own, pack, 2)).astype(BF16)


def norm_two_kernel(
    normed_one, a, b, cot, v_own, pack, result_ref, grad_ref, low_ref, sums_ref
):
    hidden = normed_one[...] * row_of(v_own, pack, 1) + row_of(v_own, pack, 2)
    resid = hidden + (a[...].astype(F32) + b[...].astype(F32)) + row_of(v_own, pack, 3)
    normed, inverse = normalize(resid)
    gain = row_of(v_own, pack, 4)
    result_ref[...] = (normed * gain + row_of(v_own, pack, 5)).astype(BF16)
    dy = cot[...].astype(F32)
    grad = back_normalize(dy, normed, inverse, gain)
    grad_ref[...] = grad
    low_ref[...] = grad.astype(BF16)
    sums_ref[...] = column_sums(dy * normed, dy, grad)


def norm_back_kernel(
    grad_two, a, b, normed_one, inverse_one, v_own, pack, grad_ref, low_ref, sums_ref
):
    dh = grad_two[...] + (a[...].astype(F32) + b[...].astype(F32))
    normed = normed_one[...]
    grad = back_normalize(dh, normed, inverse_one[:, :1], row_of(v_own, pack, 1))
    grad_ref[...] = grad
    low_ref[...] = grad.astype(BF16)
    sums_ref[...] = column_sums(dh * normed, dh, grad)


def mlp_kernel(h_own, h_other, w_in, w_down, down_other, pack, v_own, g_ref, slope_ref, own, other):
    bias = [v_own[k : k + 1, :].astype(F32) + pack[960 + k : 961 + k, :].astype(F32) for k in (6, 7)]
    for rows, h, ref in ((slice(256, 512), h_other, other), (slice(0, 256), h_own, own)):
        for k, cols in enumerate((slice(0, 384), slice(384, 768))):
            u = dot(h[:, :384], w_in[:, cols]) + bias[k]
            u = u + dot(h[:, 384:], pack[192 + 384 * k : 576 + 384 * k, :])
            cdf = 0.5 + 0.5 * lax.erf(u * 0.7071067811865476)
            slope_ref[rows, cols] = cdf + u * (0.3989422804014327 * jnp.exp(-0.5 * u * u))
            g_ref[rows, cols] = (u * cdf).astype(BF16)
        g = g_ref[rows, :]
        ref[:, :384] = dot(g, w_down[...]).astype(ref.dtype)
        ref[:, 384:] = dot(g, down_other[...]).astype(ref.dtype)


def mlp_back_kernel(
    dz_own, dz_other, w_in, w_down, down_other, pack, slope, du_ref, own, other, sums_ref
):
    total = jnp.zeros((1, 768), F32)
    for rows, dz, ref in ((slice(256, 512), dz_other, other), (slice(0, 256), dz_own, own)):
        dg = dot_t(dz[:, :384], w_down[...]) + dot_t(dz[:, 384:], down_other[...])
        du = (dg * slope[rows, :]).astype(BF16)
        du_ref[rows, :] = du
        total = total + jnp.sum(du.astype(F32), axis=0, keepdims=True)
        ref[:, :384] = dot_t(du, w_in[...]).astype(ref.dtype)
        high = dot_t(du[:, :384], pack[192:576, :]) + dot_t(du[:, 384:], pack[576:960, :])
        ref[:, 384:] = high.astype(ref.dtype)
    sums_ref[...] = jnp.broadcast_to(total, (8, 768))


def out_back_kernel(da_own, da_other, w_own, pack, o_ref, do_ref, inner_ref):
    weights = under_zeros(w_own[...]), under_zeros(pack[:192, :])
    for half, da in enumerate((da_own, da_other)):
        rows = slice(half * 256, half * 256 + 256)
        value = dot_t(da[:, :384], weights[0]) + dot_t(da[:, 384:], weights[1])
        do_ref[rows, :] = value.astype(BF16)
    product = (do_ref[...].astype(F32) * o_ref[...].astype(F32)).T
    rows = [jnp.sum(product[64 + 64 * k : 128 + 64 * k], axis=0, keepdims=True) for k in range(HEADS)]
    inner_ref[...] = jnp.concatenate(rows + [jnp.zeros((5, 512), F32)], axis=0)


def input_back_kernel(dkv, r1, r3, dq_t, w_own, w_other, low_ref, own, other, sums_ref):
    dq = (dq_t[...].T * 0.125).astype(BF16)
    low_ref[:, :256] = jnp.concatenate([dq, jnp.zeros((512, 64), BF16)], axis=1)
    total = dkv[...].astype(F32) + r1[...].astype(F32) + r3[...].astype(F32)
    low_ref[:, 256:] = total.astype(BF16)
    sums_ref[...] = jnp.broadcast_to(
        jnp.sum(low_ref[...].astype(F32), axis=0, keepdims=True), (8, 640)
    )
    for rows, ref in ((slice(256, 512), other), (slice(0, 256), own)):
        for cols, w in ((slice(0, 384), w_own), (slice(384, 768), w_other)):
            value = dot(low_ref[rows, :192], w[:192, :]) + dot(low_ref[rows, 256:], w[192:576, :])
            ref[:, cols] = value.astype(ref.dtype)


def flip(value):
    return value.astype(F32).T.astype(BF16)


def down_grad_kernel(g_ref, dz_own, dz_other, out):
    for part in range(3):
        rows = slice(256 * part, 256 * part + 256)
        left = flip(g_ref[:, rows])
        grad = dot(left[:, :256], dz_own[...]) + dot(left[:, 256:], dz_other[...])
        out[rows, :] = grad.astype(BF16)


def in_grad_kernel(h_own, h_other, du_ref, o_ref, da_own, da_other, out):
    for cols in (slice(0, 384), slice(384, 768)):
        grad = dot(flip(h_own[:, cols]), du_ref[:256, :]) + dot(
            flip(h_other[:, cols]), du_ref[256:, :]
        )
        out[:384, cols] = grad[:, :384].astype(BF16)
        out[384:768, cols] = grad[:, 384:].astype(BF16)
    left = flip(o_ref[...])
    grad = dot(left[64:, :256], da_own[...]) + dot(left[64:, 256:], da_other[...])
    out[768:960, :] = grad.astype(BF16)
    out[960:, :] = jnp.zeros((64, 768), BF16)


def proj_grad_kernel(low_ref, x_own, x_other, sums, core_sums, sums_in, sums_qkv, out, rows):
    for to, cols in ((slice(0, 192), slice(0, 256)), (slice(192, 576), slice(256, 640))):
        left = flip(low_ref[:, cols])[: to.stop - to.start]
        grad = dot(left[:, :256], x_own[...]) + dot(left[:, 256:], x_other[...])
        out[to, :] = grad.astype(BF16)
    h = lax.axis_index("fsdp")
    rows[...] = jnp.zeros((16, 768), F32)
    rows[0:3, :] = sums[0:3, :] + core_sums[0:3, :]
    rows[3:6, :] = sums[8:11, :] + core_sums[8:11, :]
    low, high = sums_in[:1, :384], sums_in[:1, 384:]
    rows[6:7, :384] = jnp.where(h == 0, low, high)
    rows[6:7, 384:] = jnp.where(h == 0, high, low)
    for cols in (slice(0, 384), slice(384, 768)):
        rows[7:8, cols] = sums_qkv[:1, :384]
        rows[8:9, cols] = sums_qkv[:1, 256:]
    out[576:592, :] = rows[...].astype(BF16)
    out[592:, :] = jnp.zeros((48, 768), BF16)


def sum_kernel(*refs):
    own, other = refs[-2:]
    start = 0
    for terms in refs[:-2]:
        total = terms[0].astype(F32)
        for k in range(1, 16):
            total = total + terms[k].astype(F32)
        rows = slice(start, start + total.shape[0])
        own[rows, :] = total[:, :384]
        other[rows, :] = total[:, 384:].astype(BF16)
        start = rows.stop


def add_kernel(own, other, out):
    out[...] = (own[...] + other[...].astype(F32)).astype(BF16)


def copies_kernel(own, other, out):
    value = (own[...] + other[...].astype(F32)).astype(BF16)
    for k in range(16):
        out[k] = value


def early_kernel(src, down, w_in, w_out):
    for k in range(16):
        down[48 * k : 48 * k + 48, :] = src[112 * k : 112 * k + 48, :].astype(F32)
        value = src[112 * k + 48 : 112 * k + 112, :].astype(F32)
        if k < 6:
            w_in[64 * k : 64 * k + 64, :384] = value
        elif k < 12:
            w_in[64 * k - 384 : 64 * k - 320, 384:] = value
        elif k < 15:
            w_out[64 * k - 768 : 64 * k - 704, :] = value


def late_kernel(src, proj, b_qv, *refs):
    vectors, rows = refs[:7], refs[7]
    rows[...] = src[...].astype(F32)
    proj[...] = rows[:576, :]
    for k, ref in enumerate(vectors):
        ref[...] = rows[576 + k, :]
    for k, row in enumerate((rows[583:584, :192], rows[584:585, 192:])):
        b_qv[k : k + 1, :] = jnp.where(lax.axis_index("fsdp") == 0, row[:, :96], row[:, 96:])


def ctx_sum(*terms):
    rows = sum(term.shape[1] for term in terms)
    own, other = call(sum_kernel, [shape((rows, 384), F32), shape((rows, 384), BF16)], *terms)
    return own, fsdp_swap(other)


def body(
    tokens,
    cotangent,
    lengths,
    w_qkv,
    b_qv,
    w_out,
    b_out,
    ln1_gain,
    ln1_bias,
    w_in,
    b_in,
    w_down,
    b_down,
    ln2_gain,
    ln2_bias,
):
    placed, wt_own = call(
        prepare_kernel,
        [shape((4, 128, 768), BF16), shape((592, 384), BF16)],
        tokens,
        cotangent,
        w_qkv.transpose(0, 2, 1).reshape(576, 384),
        b_qv,
        load=pl.BlockSpec(),
        limit=16,
    )
    wt_other = fsdp_swap(wt_own)
    placed = y_exchange(placed)
    x_own = placed[:, :64].reshape(256, 768)
    x_other = core_swap(x_own)
    query, kv = call(
        qkv_kernel,
        [shape((512, 256), BF16), shape((512, 384), BF16)],
        x_own,
        x_other,
        wt_own,
        wt_other,
    )
    cot = placed[:, 64:].reshape(256, 768)

    pack_own, v_own = call(
        pack_kernel,
        [shape((976, 384), BF16), shape((16, 384), BF16)],
        w_out,
        w_in,
        b_out,
        ln1_gain,
        ln1_bias,
        b_down,
        ln2_gain,
        ln2_bias,
        b_in,
        scratch=[pltpu.VMEM((16, 384), F32)],
        load=pl.BlockSpec(),
    )
    pack_own, w_down, kv = lax.optimization_barrier((pack_own, w_down, kv))
    pack = fsdp_swap(pack_own)
    down_other = fsdp_swap(w_down)

    kv_low, kv_high = z_shift(kv, 1), z_shift(kv, -1)
    carry = [shape((192, 512), F32), shape((8, 512), F32)]

    def attend(parts, first, last):
        return lambda *refs: attend_kernel(parts, first, last, *refs)

    acc, stat = call(attend([(0, 0)], True, False), carry, lengths, query, kv, smem=1, limit=16, us=2.4)
    pass_up, pass_down, acc = lax.optimization_barrier((kv_low[:256], kv_high[256:], acc))
    far_top, far_low = z_shift(pass_up, 1), z_shift(pass_down, -1)
    acc, stat = call(
        attend([(3, 0), (1, 0)], False, False),
        carry,
        lengths,
        query,
        kv_low,
        kv_high,
        acc,
        stat,
        smem=1,
        limit=16,
        us=4.3,
    )
    attn, log_total = call(
        attend([(2, 0), (2, 256)], False, True),
        [shape((512, 256), BF16), shape((8, 512), F32)],
        lengths,
        query,
        far_top,
        far_low,
        acc,
        stat,
        smem=1,
        after=(pack,),
        limit=16,
        us=3,
    )
    halves = [shape((256, 768), F32), shape((256, 768), BF16)]
    own, other = call(out_kernel, halves, attn, w_out, pack, after=(down_other,))
    a, b = tp_sum(own, other)
    normed_one, inverse_one, hidden_own = call(
        norm_one_kernel,
        [shape((256, 768), F32), shape((256, 128), F32), shape((256, 768), BF16)],
        x_own,
        a,
        b,
        v_own,
        pack,
    )
    hidden_other = core_swap(hidden_own)
    gelu, slope, own, other = call(
        mlp_kernel,
        [shape((512, 768), BF16), shape((512, 768), F32)] + halves,
        hidden_own,
        hidden_other,
        w_in,
        w_down,
        down_other,
        pack,
        v_own,
    )
    a, b = tp_sum(own, other)
    result, grad_two, dz_own, sums_two = call(
        norm_two_kernel,
        [
            shape((256, 768), BF16),
            shape((256, 768), F32),
            shape((256, 768), BF16),
            shape((8, 768), F32),
        ],
        normed_one,
        a,
        b,
        cot,
        v_own,
        pack,
    )
    dz_other = core_swap(dz_own)
    du, own, other, sums_in = call(
        mlp_back_kernel,
        [shape((512, 768), BF16)] + halves + [shape((8, 768), F32)],
        dz_own,
        dz_other,
        w_in,
        w_down,
        down_other,
        pack,
        slope,
    )
    a, b = tp_sum(own, other)
    gelu, dz_own, dz_other, _ = lax.optimization_barrier((gelu, dz_own, dz_other, a))
    (down_terms,) = call(down_grad_kernel, [shape((768, 768), BF16)], gelu, dz_own, dz_other)
    down_terms = ctx_exchange(down_terms)
    grad_one, da_own, sums_one = call(
        norm_back_kernel,
        [shape((256, 768), F32), shape((256, 768), BF16), shape((8, 768), F32)],
        grad_two,
        a,
        b,
        normed_one,
        inverse_one,
        v_own,
        pack,
    )
    da_other = core_swap(da_own)
    grad_heads, inner = call(
        out_back_kernel,
        [shape((512, 256), BF16), shape((8, 512), F32)],
        da_own,
        da_other,
        w_out,
        pack,
        attn,
    )
    def attend_back(parts, first, added):
        return lambda *refs: attend_back_kernel(parts, first, added, *refs)

    base = (lengths, query, grad_heads, log_total, inner)
    dq_shape = shape((192, 512), F32)
    half, whole = shape((256, 384), BF16), shape((512, 384), BF16)
    grad_top, grad_low, dq = call(
        attend_back([(2, 0), (2, 256)], True, (None, None)),
        [half, half, dq_shape],
        *base,
        far_top,
        far_low,
        smem=1,
        limit=16,
        us=3.3,
    )
    grad_top, grad_low = z_shift(grad_top, 1), z_shift(grad_low, -1)
    grad_kv, dq = call(
        attend_back([(0, 0)], False, (None,)),
        [whole, dq_shape],
        *base,
        kv,
        dq,
        smem=1,
        after=(down_terms,),
        limit=16,
        us=3,
    )
    du, hidden_own, grad_top = lax.optimization_barrier((du, hidden_own, grad_top))
    (in_terms,) = call(
        in_grad_kernel,
        [shape((1024, 768), BF16)],
        hidden_own,
        hidden_other,
        du,
        attn,
        da_own,
        da_other,
    )
    in_terms = ctx_exchange(in_terms)
    grad_up, grad_down_z, dq = call(
        attend_back([(1, 0), (3, 0)], False, (0, 256)),
        [whole, whole, dq_shape],
        *base,
        kv_high,
        kv_low,
        grad_top,
        grad_low,
        dq,
        smem=1,
        limit=16,
    )
    early_own, early_other = ctx_sum(down_terms, in_terms)
    (early,) = call(add_kernel, [shape((112, 384), BF16)], early_own, early_other)
    sums = jnp.concatenate([sums_two, sums_one])
    core_sums = core_swap(sums)
    grad_qkv, own, other, sums_qkv = call(
        input_back_kernel,
        [shape((512, 640), BF16)] + halves + [shape((8, 640), F32)],
        grad_kv,
        z_shift(grad_up, 1),
        z_shift(grad_down_z, -1),
        dq,
        wt_own,
        wt_other,
        after=(early, core_sums),
    )
    (proj_terms,) = call(
        proj_grad_kernel,
        [shape((640, 768), BF16)],
        grad_qkv,
        x_own,
        x_other,
        sums,
        core_sums,
        sums_in,
        sums_qkv,
        scratch=[pltpu.VMEM((16, 768), F32)],
    )
    late_own, late_other = ctx_sum(ctx_exchange(proj_terms))
    (copies,) = call(copies_kernel, [shape((16, 40, 384), BF16)], late_own, late_other)
    late = ctx_exchange(copies.reshape(640, 384)).reshape(640, 384)
    early = lax.all_gather(early, "ctx", axis=0, tiled=True)
    a, b = tp_sum(own, other)
    grad_x = (grad_one + (a.astype(F32) + b.astype(F32))).astype(BF16)
    outgoing = call(split_kernel, [shape((128, 768), BF16)] * 4, result, grad_x)
    back = jnp.concatenate([outgoing[0]] + [y_shift(outgoing[k], k) for k in (1, 2, 3)])
    output, grad_tokens = call(
        return_kernel, [shape((4, 128, 768), BF16)] * 2, back, core_swap(back)
    )
    grad_down, grad_in, grad_out = call(
        early_kernel,
        [shape((768, 384), F32), shape((384, 768), F32), shape((192, 384), F32)],
        early,
    )
    grad_proj, grad_b_qv, *vectors = call(
        late_kernel,
        [shape((576, 384), F32), shape((2, 96), F32)] + [shape((384,), F32)] * 7,
        late,
        scratch=[pltpu.VMEM((640, 384), F32)],
    )
    g_gain_two, g_shift_two, g_b_down, g_gain_one, g_shift_one, g_b_out, g_b_in = vectors
    return (
        output,
        grad_tokens,
        grad_proj.reshape(3, 192, 384).transpose(0, 2, 1),
        grad_b_qv,
        grad_out,
        g_b_out,
        g_gain_one,
        g_shift_one,
        grad_in,
        g_b_in,
        grad_down,
        g_b_down,
        g_gain_two,
        g_shift_two,
    )


def solution(mesh):
    placed = (
        P("fsdp", "ctx", None),
        P("fsdp", "ctx", None),
        P("fsdp"),
        P(None, "fsdp", "tp"),
        P(None, ("tp", "fsdp")),
        P("tp", "fsdp"),
        P("fsdp"),
        P("fsdp"),
        P("fsdp"),
        P("fsdp", "tp"),
        P(("tp", "fsdp")),
        P("tp", "fsdp"),
        P("fsdp"),
        P("fsdp"),
        P("fsdp"),
    )
    return jax.shard_map(
        body,
        mesh=mesh,
        in_specs=placed,
        out_specs=placed[:2]
        + (
            P(None, "fsdp", "tp"),
            P(None, ("tp", "fsdp")),
            P("tp", "fsdp"),
            P("fsdp"),
            P("fsdp"),
            P("fsdp"),
            P("fsdp", "tp"),
            P(("tp", "fsdp")),
            P("tp", "fsdp"),
            P("fsdp"),
            P("fsdp"),
            P("fsdp"),
        ),
        check_vma=False,
    )
```

```python
import jax
import jax.numpy as jnp
from jax import lax
from jax.experimental import pallas as pl
from jax.experimental.pallas import tpu as pltpu
from jax.sharding import PartitionSpec as P


EPS = 1e-06
MASKED = -1000000000.0
HEADS = 3
F32 = jnp.float32
BF16 = jnp.bfloat16
VMEM = pl.BlockSpec(memory_space=pltpu.VMEM)
SMEM = pl.BlockSpec(memory_space=pltpu.SMEM)


def core_swap(value):
    return lax.ppermute(value, "tp", [(t, t ^ 1) for t in range(4)])


def chip_swap(value):
    return lax.ppermute(value, "tp", [(t, t ^ 2) for t in range(4)])


def fsdp_swap(value):
    return lax.ppermute(value, "fsdp", [(0, 1), (1, 0)])


def z_shift(value, step):
    return lax.ppermute(
        value, "ctx", [(z * 4 + y, (z + step) % 4 * 4 + y) for z in range(4) for y in range(4)]
    )


def y_shift(value, step):
    return lax.ppermute(
        value, "ctx", [(z * 4 + y, z * 4 + (y + step) % 4) for z in range(4) for y in range(4)]
    )


def y_exchange(value):
    groups = [[z * 4 + y for y in range(4)] for z in range(4)]
    return lax.all_to_all(value, "ctx", 0, 0, axis_index_groups=groups, tiled=True)


def tp_sum(own, other):
    mine = (own + core_swap(other).astype(F32)).astype(BF16)
    return mine, chip_swap(mine)


def ctx_exchange(value):
    terms = lax.all_to_all(value, "ctx", 0, 0, tiled=True)
    return terms.reshape(16, value.shape[0] // 16, value.shape[1])


def call(kernel, outs, *args, smem=0, scratch=(), after=(), limit=8, load=VMEM, us=0.1):
    count, skip = len(args), len(args) + len(after)

    def run(*refs):
        kernel(*refs[:count], *refs[skip:])

    return pl.pallas_call(
        run,
        out_shape=outs,
        in_specs=[SMEM] * smem
        + [load] * (count - smem)
        + [pl.BlockSpec(memory_space=pl.ANY)] * len(after),
        out_specs=[VMEM] * len(outs),
        scratch_shapes=list(scratch),
        compiler_params=pltpu.CompilerParams(vmem_limit_bytes=limit * 1024 * 1024),
        cost_estimate=pl.CostEstimate(
            flops=int(us * 1e9), bytes_accessed=1000, transcendentals=0
        ),
    )(*args, *after)


def place_of():
    ctx, tp = lax.axis_index("ctx"), lax.axis_index("tp")
    return (
        lax.shift_right_logical(ctx, 2),
        lax.bitwise_and(ctx, 3),
        lax.bitwise_and(tp, 1),
        lax.axis_index("fsdp"),
    )


def shape(dims, kind):
    return jax.ShapeDtypeStruct(dims, kind)


def dot(a, b):
    return jnp.dot(a, b, preferred_element_type=F32)


def dot_t(a, b):
    return lax.dot_general(a, b, (((1,), (1,)), ((), ())), preferred_element_type=F32)


def pack_kernel(w_out, w_in, v0, v1, v2, v3, v4, v5, b_in, whole, vectors, rows):
    whole[:192, :] = w_out[...]
    whole[192:576, :] = w_in[:, :384]
    whole[576:960, :] = w_in[:, 384:]
    rows[...] = jnp.zeros((16, 384), F32)
    for k, ref in enumerate((v0, v1, v2, v3, v4, v5)):
        rows[k : k + 1, :] = ref[...].astype(F32).reshape(1, 384)
    rows[pl.ds(6 + lax.axis_index("fsdp"), 1), :] = b_in[...].astype(F32).reshape(1, 384)
    whole[960:, :] = rows[...].astype(BF16)
    vectors[...] = rows[...].astype(BF16)


def prepare_kernel(tokens, cotangent, w, b_qv, out, pack, rows_ref, bias_ref, sems):
    _, _, c, h = place_of()
    rows = pl.ds(pl.multiple_of(c * 64, 64), 64)
    copies = [
        pltpu.make_async_copy(w, pack.at[:576, :], sems.at[0]),
        pltpu.make_async_copy(b_qv, bias_ref, sems.at[1]),
        pltpu.make_async_copy(tokens.at[:, rows, :], rows_ref.at[0], sems.at[2]),
        pltpu.make_async_copy(cotangent.at[:, rows, :], rows_ref.at[1], sems.at[3]),
    ]
    for copy in copies:
        copy.start()
    for copy in copies:
        copy.wait()
    for k in range(2):
        for seq in range(4):
            low, high = rows_ref[k, seq, :, :384], rows_ref[k, seq, :, 384:]
            to = slice(64 * k, 64 * k + 64)
            out[seq, to, :384] = jnp.where(h == 0, low, high)
            out[seq, to, 384:] = jnp.where(h == 0, high, low)
    lane = lax.broadcasted_iota(jnp.int32, (96, 384), 1)
    place = lax.broadcasted_iota(jnp.int32, (96, 384), 0) + 96 * h
    spot = jnp.where(lane == place, 1.0, 0.0).astype(BF16)
    bias = jnp.concatenate([dot(bias_ref[...], spot), jnp.zeros((14, 384), F32)], axis=0)
    pack[576:592, :] = bias.astype(BF16)


def row_of(own, pack, k):
    return jnp.concatenate([own[k : k + 1, :], pack[960 + k : 961 + k, :]], axis=1).astype(F32)


def split_kernel(output, grad, *pieces):
    _, y, _, _ = place_of()
    for step in range(4):
        rows = pl.ds(pl.multiple_of(64 * lax.bitwise_and(y + step, 3), 64), 64)
        pieces[step][:64, :] = output[rows, :]
        pieces[step][64:, :] = grad[rows, :]


def return_kernel(own, other, out, grad):
    _, y, c, h = place_of()
    for ref, at in ((own, c), (other, 1 - c)):
        for start, dst in ((0, out), (64, grad)):
            for step in range(4):
                row = ref[128 * step + start : 128 * step + start + 64, :]
                first, second = row[:, :384], row[:, 384:]
                rows = pl.ds(pl.multiple_of(at * 64, 64), 64)
                seq = lax.bitwise_and(y + 4 - step, 3)
                dst[seq, rows, :384] = jnp.where(h == 0, first, second)
                dst[seq, rows, 384:] = jnp.where(h == 0, second, first)


def qkv_kernel(x_own, x_other, w_own, w_other, q_ref, kv_ref):
    bias = w_own[576:592, :192].astype(F32) + w_other[576:592, :192].astype(F32)
    bias_q, bias_v = bias[0:1], bias[1:2]
    for half, x in enumerate((x_own, x_other)):
        rows = slice(half * 256, half * 256 + 256)
        low, high = x[:, :384], x[:, 384:]
        query = dot_t(low, w_own[:192, :]) + dot_t(high, w_other[:192, :]) + bias_q
        q_ref[rows, :192] = (query.astype(BF16) * BF16(0.125)).astype(BF16)
        q_ref[rows, 192:] = jnp.zeros((256, 64), BF16)
        key = dot_t(low, w_own[192:384, :]) + dot_t(high, w_other[192:384, :])
        value = dot_t(low, w_own[384:576, :]) + dot_t(high, w_other[384:576, :]) + bias_v
        kv_ref[rows, :] = jnp.concatenate([key, value], axis=1).astype(BF16)


def mask_rows(lengths, away, start, count):
    z, y, c, _ = place_of()
    row = lax.broadcasted_iota(jnp.int32, (count, 128), 0) + start
    half = lax.shift_right_logical(row, 8)
    block = lax.bitwise_and(lax.shift_right_logical(row, 6), 3)
    place = (
        512 * lax.bitwise_and(z + away, 3)
        + 128 * block
        + 64 * jnp.where(half == c, 0, 1)
        + lax.bitwise_and(row, 63)
    )
    bias = jnp.where(place < lengths[y], 0.0, MASKED).astype(F32)
    return jnp.concatenate([bias] * 4, axis=1)


def head_lanes(value, head, offset):
    lane = lax.broadcasted_iota(jnp.int32, value.shape, 1)
    low = offset + 64 * head
    return jnp.where((lane >= low) & (lane < low + 64), value, jnp.zeros_like(value))


def attend_kernel(parts, first, last, lengths, q_ref, *refs):
    pieces, refs = refs[: len(parts)], refs[len(parts) :]
    if not first:
        acc_in, stat_in, refs = refs[0], refs[1], refs[2:]
    out, stat = refs
    flipped = [kv[:, 128:].astype(F32).T.astype(BF16) for kv in pieces]
    bias = [mask_rows(lengths, at, start, kv.shape[0]) for (at, start), kv in zip(parts, pieces)]
    results, tops, totals = [], [], []
    for head in range(HEADS):
        query = head_lanes(q_ref[...], head, 0)
        rows = slice(64 * head, 64 * head + 64)
        if first:
            top = jnp.full((1, 512), -1e30, F32)
            total = jnp.zeros((1, 512), F32)
            acc = jnp.zeros((64, 512), F32)
        else:
            top = stat_in[head : head + 1, :]
            total = stat_in[3 + head : 4 + head, :]
            acc = acc_in[rows, :]
        for kv, values, invalid in zip(pieces, flipped, bias):
            scores = dot_t(kv[:, :256], query) + invalid
            peak = jnp.maximum(top, jnp.max(scores, axis=0, keepdims=True))
            keep = jnp.exp(top - peak)
            expo = jnp.exp(scores - peak)
            total = total * keep + jnp.sum(expo, axis=0, keepdims=True)
            low = 64 + 64 * head
            acc = acc * keep + dot(values[low : low + 64, :], expo.astype(BF16))
            top = peak
        if last:
            results.append(acc / total)
            tops.append(top + jnp.log(total))
        else:
            out[rows, :] = acc
            stat[head : head + 1, :] = top
            stat[3 + head : 4 + head, :] = total
    if last:
        whole = jnp.concatenate([jnp.zeros((64, 512), F32)] + results, axis=0)
        out[...] = whole.T.astype(BF16)
        for head in range(HEADS):
            stat[head : head + 1, :] = tops[head]
        stat[3:8, :] = jnp.zeros((5, 512), F32)
    else:
        stat[6:8, :] = jnp.zeros((2, 512), F32)


def attend_back_kernel(parts, first, added, lengths, q_ref, do_ref, lse, inner, *refs):
    pieces, refs = refs[: len(parts)], refs[len(parts) :]
    extras = []
    for at in added:
        extras.append(None if at is None else (at, refs[0]))
        refs = refs if at is None else refs[1:]
    if not first:
        dq_in, refs = refs[0], refs[1:]
    outs, dq_ref = refs[:-1], refs[-1]
    for index, ((away, start), kv) in enumerate(zip(parts, pieces)):
        count = kv.shape[0]
        bias = mask_rows(lengths, away, start, count)
        keys, values = kv[:, :256], kv[:, 128:]
        keys_t = keys.astype(F32).T.astype(BF16)
        dk = jnp.zeros((count, 256), F32)
        dv = jnp.zeros((count, 256), F32)
        for head in range(HEADS):
            query = head_lanes(q_ref[...], head, 0)
            grad = head_lanes(do_ref[...], head, 64)
            probs = jnp.exp(dot_t(keys, query) + bias - lse[head : head + 1, :])
            grad_probs = dot_t(values, grad) - inner[head : head + 1, :]
            grad_scores = (probs * grad_probs).astype(BF16)
            dk = dk + dot(grad_scores, query)
            dv = dv + dot(probs.astype(BF16), grad)
            rows = slice(64 * head, 64 * head + 64)
            dq = dot(keys_t[rows, :], grad_scores)
            if index:
                dq = dq + dq_ref[rows, :]
            elif not first:
                dq = dq + dq_in[rows, :]
            dq_ref[rows, :] = dq
        whole = jnp.concatenate([dk[:, :128], dk[:, 128:] + dv[:, :128], dv[:, 128:]], axis=1)
        out = outs[index]
        if extras[index] is None:
            out[...] = whole.astype(BF16)
        else:
            at, extra = extras[index]
            for low in (0, 256):
                part = whole[low : low + 256]
                if low == at:
                    part = part + extra[...].astype(F32)
                out[low : low + 256, :] = part.astype(BF16)


def under_zeros(w):
    return jnp.concatenate([jnp.zeros((64, 384), BF16), w], axis=0)


def out_kernel(o_ref, w_own, pack, own, other):
    weights = under_zeros(w_own[...]), under_zeros(pack[:192, :])
    for rows, ref in ((slice(256, 512), other), (slice(0, 256), own)):
        ref[:, :384] = dot(o_ref[rows, :], weights[0]).astype(ref.dtype)
        ref[:, 384:] = dot(o_ref[rows, :], weights[1]).astype(ref.dtype)


def normalize(value):
    center = value - jnp.mean(value, axis=1, keepdims=True)
    inverse = lax.rsqrt(jnp.mean(center * center, axis=1, keepdims=True) + EPS)
    return center * inverse, inverse


def back_normalize(grad, normed, inverse, gain):
    scaled = grad * gain
    return inverse * (
        scaled
        - jnp.mean(scaled, axis=1, keepdims=True)
        - normed * jnp.mean(scaled * normed, axis=1, keepdims=True)
    )


def column_sums(*values):
    rows = [jnp.sum(value, axis=0, keepdims=True) for value in values]
    return jnp.concatenate(rows + [jnp.zeros((8 - len(rows), rows[0].shape[1]), F32)], axis=0)


def norm_one_kernel(x, a, b, v_own, pack, normed_ref, inverse_ref, low_ref):
    resid = x[...].astype(F32) + (a[...].astype(F32) + b[...].astype(F32)) + row_of(v_own, pack, 0)
    normed, inverse = normalize(resid)
    normed_ref[...] = normed
    inverse_ref[...] = jnp.broadcast_to(inverse, (256, 128))
    low_ref[...] = (normed * row_of(v_own, pack, 1) + row_of(v_own, pack, 2)).astype(BF16)


def norm_two_kernel(
    normed_one, a, b, cot, v_own, pack, result_ref, grad_ref, low_ref, sums_ref
):
    hidden = normed_one[...] * row_of(v_own, pack, 1) + row_of(v_own, pack, 2)
    resid = hidden + (a[...].astype(F32) + b[...].astype(F32)) + row_of(v_own, pack, 3)
    normed, inverse = normalize(resid)
    gain = row_of(v_own, pack, 4)
    result_ref[...] = (normed * gain + row_of(v_own, pack, 5)).astype(BF16)
    dy = cot[...].astype(F32)
    grad = back_normalize(dy, normed, inverse, gain)
    grad_ref[...] = grad
    low_ref[...] = grad.astype(BF16)
    sums_ref[...] = column_sums(dy * normed, dy, grad)


def norm_back_kernel(
    grad_two, a, b, normed_one, inverse_one, v_own, pack, grad_ref, low_ref, sums_ref
):
    dh = grad_two[...] + (a[...].astype(F32) + b[...].astype(F32))
    normed = normed_one[...]
    grad = back_normalize(dh, normed, inverse_one[:, :1], row_of(v_own, pack, 1))
    grad_ref[...] = grad
    low_ref[...] = grad.astype(BF16)
    sums_ref[...] = column_sums(dh * normed, dh, grad)


def mlp_kernel(h_own, h_other, w_in, w_down, down_other, pack, v_own, g_ref, slope_ref, own, other):
    bias = [v_own[k : k + 1, :].astype(F32) + pack[960 + k : 961 + k, :].astype(F32) for k in (6, 7)]
    for rows, h, ref in ((slice(256, 512), h_other, other), (slice(0, 256), h_own, own)):
        for k, cols in enumerate((slice(0, 384), slice(384, 768))):
            u = dot(h[:, :384], w_in[:, cols]) + bias[k]
            u = u + dot(h[:, 384:], pack[192 + 384 * k : 576 + 384 * k, :])
            cdf = 0.5 + 0.5 * lax.erf(u * 0.7071067811865476)
            slope_ref[rows, cols] = cdf + u * (0.3989422804014327 * jnp.exp(-0.5 * u * u))
            g_ref[rows, cols] = (u * cdf).astype(BF16)
        g = g_ref[rows, :]
        ref[:, :384] = dot(g, w_down[...]).astype(ref.dtype)
        ref[:, 384:] = dot(g, down_other[...]).astype(ref.dtype)


def mlp_back_kernel(
    dz_own, dz_other, w_in, w_down, down_other, pack, slope, du_ref, own, other, sums_ref
):
    total = jnp.zeros((1, 768), F32)
    for rows, dz, ref in ((slice(256, 512), dz_other, other), (slice(0, 256), dz_own, own)):
        dg = dot_t(dz[:, :384], w_down[...]) + dot_t(dz[:, 384:], down_other[...])
        du = (dg * slope[rows, :]).astype(BF16)
        du_ref[rows, :] = du
        total = total + jnp.sum(du.astype(F32), axis=0, keepdims=True)
        ref[:, :384] = dot_t(du, w_in[...]).astype(ref.dtype)
        high = dot_t(du[:, :384], pack[192:576, :]) + dot_t(du[:, 384:], pack[576:960, :])
        ref[:, 384:] = high.astype(ref.dtype)
    sums_ref[...] = jnp.broadcast_to(total, (8, 768))


def out_back_kernel(da_own, da_other, w_own, pack, o_ref, do_ref, inner_ref):
    weights = under_zeros(w_own[...]), under_zeros(pack[:192, :])
    for half, da in enumerate((da_own, da_other)):
        rows = slice(half * 256, half * 256 + 256)
        value = dot_t(da[:, :384], weights[0]) + dot_t(da[:, 384:], weights[1])
        do_ref[rows, :] = value.astype(BF16)
    product = (do_ref[...].astype(F32) * o_ref[...].astype(F32)).T
    rows = [jnp.sum(product[64 + 64 * k : 128 + 64 * k], axis=0, keepdims=True) for k in range(HEADS)]
    inner_ref[...] = jnp.concatenate(rows + [jnp.zeros((5, 512), F32)], axis=0)


def input_back_kernel(dkv, r1, r3, dq_t, w_own, w_other, low_ref, own, other, sums_ref):
    dq = (dq_t[...].T * 0.125).astype(BF16)
    low_ref[:, :256] = jnp.concatenate([dq, jnp.zeros((512, 64), BF16)], axis=1)
    total = dkv[...].astype(F32) + r1[...].astype(F32) + r3[...].astype(F32)
    low_ref[:, 256:] = total.astype(BF16)
    sums_ref[...] = jnp.broadcast_to(
        jnp.sum(low_ref[...].astype(F32), axis=0, keepdims=True), (8, 640)
    )
    for rows, ref in ((slice(256, 512), other), (slice(0, 256), own)):
        for cols, w in ((slice(0, 384), w_own), (slice(384, 768), w_other)):
            value = dot(low_ref[rows, :192], w[:192, :]) + dot(low_ref[rows, 256:], w[192:576, :])
            ref[:, cols] = value.astype(ref.dtype)


def flip(value):
    return value.astype(F32).T.astype(BF16)


def down_grad_kernel(g_ref, dz_own, dz_other, out):
    for part in range(3):
        rows = slice(256 * part, 256 * part + 256)
        left = flip(g_ref[:, rows])
        grad = dot(left[:, :256], dz_own[...]) + dot(left[:, 256:], dz_other[...])
        out[rows, :] = grad.astype(BF16)


def in_grad_kernel(h_own, h_other, du_ref, o_ref, da_own, da_other, out):
    for cols in (slice(0, 384), slice(384, 768)):
        grad = dot(flip(h_own[:, cols]), du_ref[:256, :]) + dot(
            flip(h_other[:, cols]), du_ref[256:, :]
        )
        out[:384, cols] = grad[:, :384].astype(BF16)
        out[384:768, cols] = grad[:, 384:].astype(BF16)
    left = flip(o_ref[...])
    grad = dot(left[64:, :256], da_own[...]) + dot(left[64:, 256:], da_other[...])
    out[768:960, :] = grad.astype(BF16)
    out[960:, :] = jnp.zeros((64, 768), BF16)


def proj_grad_kernel(low_ref, x_own, x_other, sums, core_sums, sums_in, sums_qkv, out, rows):
    for to, cols in ((slice(0, 192), slice(0, 256)), (slice(192, 576), slice(256, 640))):
        left = flip(low_ref[:, cols])[: to.stop - to.start]
        grad = dot(left[:, :256], x_own[...]) + dot(left[:, 256:], x_other[...])
        out[to, :] = grad.astype(BF16)
    h = lax.axis_index("fsdp")
    rows[...] = jnp.zeros((16, 768), F32)
    rows[0:3, :] = sums[0:3, :] + core_sums[0:3, :]
    rows[3:6, :] = sums[8:11, :] + core_sums[8:11, :]
    low, high = sums_in[:1, :384], sums_in[:1, 384:]
    rows[6:7, :384] = jnp.where(h == 0, low, high)
    rows[6:7, 384:] = jnp.where(h == 0, high, low)
    for cols in (slice(0, 384), slice(384, 768)):
        rows[7:8, cols] = sums_qkv[:1, :384]
        rows[8:9, cols] = sums_qkv[:1, 256:]
    out[576:592, :] = rows[...].astype(BF16)
    out[592:, :] = jnp.zeros((48, 768), BF16)


def sum_kernel(*refs):
    own, other = refs[-2:]
    start = 0
    for terms in refs[:-2]:
        total = terms[0].astype(F32)
        for k in range(1, 16):
            total = total + terms[k].astype(F32)
        rows = slice(start, start + total.shape[0])
        own[rows, :] = total[:, :384]
        other[rows, :] = total[:, 384:].astype(BF16)
        start = rows.stop


def copies_kernel(own, other, own_late, other_late, out):
    early = (own[...] + other[...].astype(F32)).astype(BF16)
    late = (own_late[...] + other_late[...].astype(F32)).astype(BF16)
    for k in range(16):
        out[k, :112, :] = early
        out[k, 112:, :] = late


def grads_kernel(src, down, w_in, w_out, proj, b_qv, *refs):
    vectors, rows = refs[:7], refs[7]
    for k in range(16):
        down[48 * k : 48 * k + 48, :] = src[k, :48, :].astype(F32)
        value = src[k, 48:112, :].astype(F32)
        if k < 6:
            w_in[64 * k : 64 * k + 64, :384] = value
        elif k < 12:
            w_in[64 * k - 384 : 64 * k - 320, 384:] = value
        elif k < 15:
            w_out[64 * k - 768 : 64 * k - 704, :] = value
        rows[40 * k : 40 * k + 40, :] = src[k, 112:, :].astype(F32)
    proj[...] = rows[:576, :]
    for k, ref in enumerate(vectors):
        ref[...] = rows[576 + k, :]
    for k, row in enumerate((rows[583:584, :192], rows[584:585, 192:])):
        b_qv[k : k + 1, :] = jnp.where(lax.axis_index("fsdp") == 0, row[:, :96], row[:, 96:])


def ctx_sum(*terms):
    rows = sum(term.shape[1] for term in terms)
    own, other = call(sum_kernel, [shape((rows, 384), F32), shape((rows, 384), BF16)], *terms)
    return own, fsdp_swap(other)


def body(
    tokens,
    cotangent,
    lengths,
    w_qkv,
    b_qv,
    w_out,
    b_out,
    ln1_gain,
    ln1_bias,
    w_in,
    b_in,
    w_down,
    b_down,
    ln2_gain,
    ln2_bias,
):
    placed, wt_own = call(
        prepare_kernel,
        [shape((4, 128, 768), BF16), shape((592, 384), BF16)],
        tokens,
        cotangent,
        w_qkv.transpose(0, 2, 1).reshape(576, 384),
        b_qv,
        scratch=[
            pltpu.VMEM((2, 4, 64, 768), BF16),
            pltpu.VMEM((2, 96), BF16),
            pltpu.SemaphoreType.DMA((4,)),
        ],
        load=pl.BlockSpec(memory_space=pltpu.HBM),
    )
    wt_other = fsdp_swap(wt_own)
    placed = y_exchange(placed)
    x_own = placed[:, :64].reshape(256, 768)
    x_other = core_swap(x_own)
    query, kv = call(
        qkv_kernel,
        [shape((512, 256), BF16), shape((512, 384), BF16)],
        x_own,
        x_other,
        wt_own,
        wt_other,
    )
    cot = placed[:, 64:].reshape(256, 768)

    pack_own, v_own = call(
        pack_kernel,
        [shape((976, 384), BF16), shape((16, 384), BF16)],
        w_out,
        w_in,
        b_out,
        ln1_gain,
        ln1_bias,
        b_down,
        ln2_gain,
        ln2_bias,
        b_in,
        scratch=[pltpu.VMEM((16, 384), F32)],
        load=pl.BlockSpec(),
    )
    pack_own, w_down, _ = lax.optimization_barrier((pack_own, w_down, wt_other))
    pack = fsdp_swap(pack_own)
    down_other = fsdp_swap(w_down)

    kv_low, kv_high = z_shift(kv, 1), z_shift(kv, -1)
    carry = [shape((192, 512), F32), shape((8, 512), F32)]

    def attend(parts, first, last):
        return lambda *refs: attend_kernel(parts, first, last, *refs)

    acc, stat = call(attend([(0, 0)], True, False), carry, lengths, query, kv, smem=1, after=(pack,), limit=16, us=2.4)
    pass_up, pass_down, acc = lax.optimization_barrier((kv_low[:256], kv_high[256:], acc))
    far_top, far_low = z_shift(pass_up, 1), z_shift(pass_down, -1)
    acc, stat = call(
        attend([(3, 0), (1, 0)], False, False),
        carry,
        lengths,
        query,
        kv_low,
        kv_high,
        acc,
        stat,
        smem=1,
        limit=16,
        us=4.3,
    )
    attn, log_total = call(
        attend([(2, 0), (2, 256)], False, True),
        [shape((512, 256), BF16), shape((8, 512), F32)],
        lengths,
        query,
        far_top,
        far_low,
        acc,
        stat,
        smem=1,
        limit=16,
        us=3,
    )
    halves = [shape((256, 768), F32), shape((256, 768), BF16)]
    own, other = call(out_kernel, halves, attn, w_out, pack, after=(down_other,))
    a, b = tp_sum(own, other)
    normed_one, inverse_one, hidden_own = call(
        norm_one_kernel,
        [shape((256, 768), F32), shape((256, 128), F32), shape((256, 768), BF16)],
        x_own,
        a,
        b,
        v_own,
        pack,
    )
    hidden_other = core_swap(hidden_own)
    gelu, slope, own, other = call(
        mlp_kernel,
        [shape((512, 768), BF16), shape((512, 768), F32)] + halves,
        hidden_own,
        hidden_other,
        w_in,
        w_down,
        down_other,
        pack,
        v_own,
    )
    a, b = tp_sum(own, other)
    result, grad_two, dz_own, sums_two = call(
        norm_two_kernel,
        [
            shape((256, 768), BF16),
            shape((256, 768), F32),
            shape((256, 768), BF16),
            shape((8, 768), F32),
        ],
        normed_one,
        a,
        b,
        cot,
        v_own,
        pack,
    )
    dz_other = core_swap(dz_own)
    du, own, other, sums_in = call(
        mlp_back_kernel,
        [shape((512, 768), BF16)] + halves + [shape((8, 768), F32)],
        dz_own,
        dz_other,
        w_in,
        w_down,
        down_other,
        pack,
        slope,
    )
    a, b = tp_sum(own, other)
    gelu, dz_own, dz_other, _ = lax.optimization_barrier((gelu, dz_own, dz_other, a))
    (down_terms,) = call(down_grad_kernel, [shape((768, 768), BF16)], gelu, dz_own, dz_other)
    down_terms = ctx_exchange(down_terms)
    grad_one, da_own, sums_one = call(
        norm_back_kernel,
        [shape((256, 768), F32), shape((256, 768), BF16), shape((8, 768), F32)],
        grad_two,
        a,
        b,
        normed_one,
        inverse_one,
        v_own,
        pack,
    )
    da_other = core_swap(da_own)
    grad_heads, inner = call(
        out_back_kernel,
        [shape((512, 256), BF16), shape((8, 512), F32)],
        da_own,
        da_other,
        w_out,
        pack,
        attn,
    )
    def attend_back(parts, first, added):
        return lambda *refs: attend_back_kernel(parts, first, added, *refs)

    base = (lengths, query, grad_heads, log_total, inner)
    dq_shape = shape((192, 512), F32)
    half, whole = shape((256, 384), BF16), shape((512, 384), BF16)
    grad_top, grad_low, dq = call(
        attend_back([(2, 0), (2, 256)], True, (None, None)),
        [half, half, dq_shape],
        *base,
        far_top,
        far_low,
        smem=1,
        limit=16,
        us=3.3,
    )
    grad_top, grad_low = z_shift(grad_top, 1), z_shift(grad_low, -1)
    grad_kv, dq = call(
        attend_back([(0, 0)], False, (None,)),
        [whole, dq_shape],
        *base,
        kv,
        dq,
        smem=1,
        after=(down_terms,),
        limit=16,
        us=3,
    )
    du, hidden_own, grad_top, grad_low, grad_kv = lax.optimization_barrier(
        (du, hidden_own, grad_top, grad_low, grad_kv)
    )
    (in_terms,) = call(
        in_grad_kernel,
        [shape((1024, 768), BF16)],
        hidden_own,
        hidden_other,
        du,
        attn,
        da_own,
        da_other,
    )
    in_terms = ctx_exchange(in_terms)
    grad_up, grad_down_z, dq = call(
        attend_back([(1, 0), (3, 0)], False, (0, 256)),
        [whole, whole, dq_shape],
        *base,
        kv_high,
        kv_low,
        grad_top,
        grad_low,
        dq,
        smem=1,
        limit=16,
    )
    early_own, early_other = ctx_sum(down_terms, in_terms)
    sums = jnp.concatenate([sums_two, sums_one])
    core_sums = core_swap(sums)
    grad_qkv, own, other, sums_qkv = call(
        input_back_kernel,
        [shape((512, 640), BF16)] + halves + [shape((8, 640), F32)],
        grad_kv,
        z_shift(grad_up, 1),
        z_shift(grad_down_z, -1),
        dq,
        wt_own,
        wt_other,
        after=(in_terms, core_sums),
    )
    (proj_terms,) = call(
        proj_grad_kernel,
        [shape((640, 768), BF16)],
        grad_qkv,
        x_own,
        x_other,
        sums,
        core_sums,
        sums_in,
        sums_qkv,
        scratch=[pltpu.VMEM((16, 768), F32)],
    )
    late_own, late_other = ctx_sum(ctx_exchange(proj_terms))
    (copies,) = call(
        copies_kernel,
        [shape((16, 152, 384), BF16)],
        early_own,
        early_other,
        late_own,
        late_other,
    )
    grads = ctx_exchange(copies.reshape(2432, 384))
    a, b = tp_sum(own, other)
    grad_x = (grad_one + (a.astype(F32) + b.astype(F32))).astype(BF16)
    outgoing = call(split_kernel, [shape((128, 768), BF16)] * 4, result, grad_x)
    back = jnp.concatenate([outgoing[0]] + [y_shift(outgoing[k], k) for k in (1, 2, 3)])
    output, grad_tokens = call(
        return_kernel, [shape((4, 128, 768), BF16)] * 2, back, core_swap(back)
    )
    grad_down, grad_in, grad_out, grad_proj, grad_b_qv, *vectors = call(
        grads_kernel,
        [
            shape((768, 384), F32),
            shape((384, 768), F32),
            shape((192, 384), F32),
            shape((576, 384), F32),
            shape((2, 96), F32),
        ]
        + [shape((384,), F32)] * 7,
        grads,
        scratch=[pltpu.VMEM((640, 384), F32)],
    )
    g_gain_two, g_shift_two, g_b_down, g_gain_one, g_shift_one, g_b_out, g_b_in = vectors
    return (
        output,
        grad_tokens,
        grad_proj.reshape(3, 192, 384).transpose(0, 2, 1),
        grad_b_qv,
        grad_out,
        g_b_out,
        g_gain_one,
        g_shift_one,
        grad_in,
        g_b_in,
        grad_down,
        g_b_down,
        g_gain_two,
        g_shift_two,
    )


def solution(mesh):
    placed = (
        P("fsdp", "ctx", None),
        P("fsdp", "ctx", None),
        P("fsdp"),
        P(None, "fsdp", "tp"),
        P(None, ("tp", "fsdp")),
        P("tp", "fsdp"),
        P("fsdp"),
        P("fsdp"),
        P("fsdp"),
        P("fsdp", "tp"),
        P(("tp", "fsdp")),
        P("tp", "fsdp"),
        P("fsdp"),
        P("fsdp"),
        P("fsdp"),
    )
    return jax.shard_map(
        body,
        mesh=mesh,
        in_specs=placed,
        out_specs=placed[:2]
        + (
            P(None, "fsdp", "tp"),
            P(None, ("tp", "fsdp")),
            P("tp", "fsdp"),
            P("fsdp"),
            P("fsdp"),
            P("fsdp"),
            P("fsdp", "tp"),
            P(("tp", "fsdp")),
            P("tp", "fsdp"),
            P("fsdp"),
            P("fsdp"),
            P("fsdp"),
        ),
        check_vma=False,
    )
```

```python
import jax
import jax.numpy as jnp
from jax import lax
from jax.experimental import pallas as pl
from jax.experimental.pallas import tpu as pltpu
from jax.sharding import PartitionSpec as P


EPS = 1e-06
MASKED = -1000000000.0
HEADS = 3
F32 = jnp.float32
BF16 = jnp.bfloat16
VMEM = pl.BlockSpec(memory_space=pltpu.VMEM)
SMEM = pl.BlockSpec(memory_space=pltpu.SMEM)


def core_swap(value):
    return lax.ppermute(value, "tp", [(t, t ^ 1) for t in range(4)])


def chip_swap(value):
    return lax.ppermute(value, "tp", [(t, t ^ 2) for t in range(4)])


def fsdp_swap(value):
    return lax.ppermute(value, "fsdp", [(0, 1), (1, 0)])


def z_shift(value, step):
    return lax.ppermute(
        value, "ctx", [(z * 4 + y, (z + step) % 4 * 4 + y) for z in range(4) for y in range(4)]
    )


def y_shift(value, step):
    return lax.ppermute(
        value, "ctx", [(z * 4 + y, z * 4 + (y + step) % 4) for z in range(4) for y in range(4)]
    )


def y_exchange(value):
    groups = [[z * 4 + y for y in range(4)] for z in range(4)]
    return lax.all_to_all(value, "ctx", 0, 0, axis_index_groups=groups, tiled=True)


def tp_sum(own, other):
    mine = (own + core_swap(other).astype(F32)).astype(BF16)
    return mine, chip_swap(mine)


def ctx_exchange(value):
    terms = lax.all_to_all(value, "ctx", 0, 0, tiled=True)
    return terms.reshape(16, value.shape[0] // 16, value.shape[1])


def call(
    kernel, outs, *args, smem=0, scratch=(), after=(), limit=8, load=VMEM, us=0.1, fetch=False
):
    count, skip = len(args), len(args) + len(after)
    scratch = list(scratch)
    if fetch:
        limit, load = 58, pl.BlockSpec(memory_space=pl.ANY)
        moved = args[smem:]
        scratch += [pltpu.VMEM(a.shape, a.dtype) for a in moved]
        scratch += [pltpu.SemaphoreType.DMA((len(moved),))]

    def run(*refs):
        if not fetch:
            return kernel(*refs[:count], *refs[skip:])
        first = len(refs) - 1 - len(moved)
        buffers, sems = refs[first:-1], refs[-1]
        copies = [
            pltpu.make_async_copy(src, dst, sems.at[k])
            for k, (src, dst) in enumerate(zip(refs[smem:count], buffers))
        ]
        for copy in copies:
            copy.start()
        for copy in copies:
            copy.wait()
        kernel(*refs[:smem], *buffers, *refs[skip:first])

    return pl.pallas_call(
        run,
        out_shape=outs,
        in_specs=[SMEM] * smem
        + [load] * (count - smem)
        + [pl.BlockSpec(memory_space=pl.ANY)] * len(after),
        out_specs=[VMEM] * len(outs),
        scratch_shapes=scratch,
        compiler_params=pltpu.CompilerParams(vmem_limit_bytes=limit * 1024 * 1024),
        cost_estimate=pl.CostEstimate(
            flops=int(us * 1e9), bytes_accessed=1000, transcendentals=0
        ),
    )(*args, *after)


def place_of():
    ctx, tp = lax.axis_index("ctx"), lax.axis_index("tp")
    return (
        lax.shift_right_logical(ctx, 2),
        lax.bitwise_and(ctx, 3),
        lax.bitwise_and(tp, 1),
        lax.axis_index("fsdp"),
    )


def shape(dims, kind):
    return jax.ShapeDtypeStruct(dims, kind)


def dot(a, b):
    return jnp.dot(a, b, preferred_element_type=F32)


def dot_t(a, b):
    return lax.dot_general(a, b, (((1,), (1,)), ((), ())), preferred_element_type=F32)


def pack_kernel(w_out, w_in, v0, v1, v2, v3, v4, v5, b_in, whole, vectors, rows):
    whole[:192, :] = w_out[...]
    whole[192:576, :] = w_in[:, :384]
    whole[576:960, :] = w_in[:, 384:]
    rows[...] = jnp.zeros((16, 384), F32)
    for k, ref in enumerate((v0, v1, v2, v3, v4, v5)):
        rows[k : k + 1, :] = ref[...].astype(F32).reshape(1, 384)
    rows[pl.ds(6 + lax.axis_index("fsdp"), 1), :] = b_in[...].astype(F32).reshape(1, 384)
    whole[960:, :] = rows[...].astype(BF16)
    vectors[...] = rows[...].astype(BF16)


def prepare_kernel(tokens, cotangent, w, b_qv, out, pack, rows_ref, bias_ref, sems):
    _, _, c, h = place_of()
    rows = pl.ds(pl.multiple_of(c * 64, 64), 64)
    copies = [
        pltpu.make_async_copy(w, pack.at[:576, :], sems.at[0]),
        pltpu.make_async_copy(b_qv, bias_ref, sems.at[1]),
        pltpu.make_async_copy(tokens.at[:, rows, :], rows_ref.at[0], sems.at[2]),
        pltpu.make_async_copy(cotangent.at[:, rows, :], rows_ref.at[1], sems.at[3]),
    ]
    for copy in copies:
        copy.start()
    for copy in copies:
        copy.wait()
    for k in range(2):
        for seq in range(4):
            low, high = rows_ref[k, seq, :, :384], rows_ref[k, seq, :, 384:]
            to = slice(64 * k, 64 * k + 64)
            out[seq, to, :384] = jnp.where(h == 0, low, high)
            out[seq, to, 384:] = jnp.where(h == 0, high, low)
    lane = lax.broadcasted_iota(jnp.int32, (96, 384), 1)
    place = lax.broadcasted_iota(jnp.int32, (96, 384), 0) + 96 * h
    spot = jnp.where(lane == place, 1.0, 0.0).astype(BF16)
    bias = jnp.concatenate([dot(bias_ref[...], spot), jnp.zeros((14, 384), F32)], axis=0)
    pack[576:592, :] = bias.astype(BF16)


def row_of(own, pack, k):
    return jnp.concatenate([own[k : k + 1, :], pack[960 + k : 961 + k, :]], axis=1).astype(F32)


def split_kernel(output, grad, *pieces):
    _, y, _, _ = place_of()
    for step in range(4):
        rows = pl.ds(pl.multiple_of(64 * lax.bitwise_and(y + step, 3), 64), 64)
        pieces[step][:64, :] = output[rows, :]
        pieces[step][64:, :] = grad[rows, :]


def return_kernel(own, other, out, grad):
    _, y, c, h = place_of()
    for ref, at in ((own, c), (other, 1 - c)):
        for start, dst in ((0, out), (64, grad)):
            for step in range(4):
                row = ref[128 * step + start : 128 * step + start + 64, :]
                first, second = row[:, :384], row[:, 384:]
                rows = pl.ds(pl.multiple_of(at * 64, 64), 64)
                seq = lax.bitwise_and(y + 4 - step, 3)
                dst[seq, rows, :384] = jnp.where(h == 0, first, second)
                dst[seq, rows, 384:] = jnp.where(h == 0, second, first)


def qkv_kernel(x_own, x_other, w_own, w_other, q_ref, kv_ref):
    bias = w_own[576:592, :192].astype(F32) + w_other[576:592, :192].astype(F32)
    bias_q, bias_v = bias[0:1], bias[1:2]
    for half, x in enumerate((x_own, x_other)):
        rows = slice(half * 256, half * 256 + 256)
        low, high = x[:, :384], x[:, 384:]
        query = dot_t(low, w_own[:192, :]) + dot_t(high, w_other[:192, :]) + bias_q
        q_ref[rows, :192] = (query.astype(BF16) * BF16(0.125)).astype(BF16)
        q_ref[rows, 192:] = jnp.zeros((256, 64), BF16)
        key = dot_t(low, w_own[192:384, :]) + dot_t(high, w_other[192:384, :])
        value = dot_t(low, w_own[384:576, :]) + dot_t(high, w_other[384:576, :]) + bias_v
        kv_ref[rows, :] = jnp.concatenate([key, value], axis=1).astype(BF16)


def mask_rows(lengths, away, start, count):
    z, y, c, _ = place_of()
    row = lax.broadcasted_iota(jnp.int32, (count, 128), 0) + start
    half = lax.shift_right_logical(row, 8)
    block = lax.bitwise_and(lax.shift_right_logical(row, 6), 3)
    place = (
        512 * lax.bitwise_and(z + away, 3)
        + 128 * block
        + 64 * jnp.where(half == c, 0, 1)
        + lax.bitwise_and(row, 63)
    )
    bias = jnp.where(place < lengths[y], 0.0, MASKED).astype(F32)
    return jnp.concatenate([bias] * 4, axis=1)


def head_lanes(value, head, offset):
    lane = lax.broadcasted_iota(jnp.int32, value.shape, 1)
    low = offset + 64 * head
    return jnp.where((lane >= low) & (lane < low + 64), value, jnp.zeros_like(value))


def attend_kernel(parts, first, last, lengths, q_ref, *refs):
    pieces, refs = refs[: len(parts)], refs[len(parts) :]
    if not first:
        acc_in, stat_in, refs = refs[0], refs[1], refs[2:]
    out, stat = refs
    flipped = [kv[:, 128:].astype(F32).T.astype(BF16) for kv in pieces]
    bias = [mask_rows(lengths, at, start, kv.shape[0]) for (at, start), kv in zip(parts, pieces)]
    results, tops, totals = [], [], []
    for head in range(HEADS):
        query = head_lanes(q_ref[...], head, 0)
        rows = slice(64 * head, 64 * head + 64)
        if first:
            top = jnp.full((1, 512), -1e30, F32)
            total = jnp.zeros((1, 512), F32)
            acc = jnp.zeros((64, 512), F32)
        else:
            top = stat_in[head : head + 1, :]
            total = stat_in[3 + head : 4 + head, :]
            acc = acc_in[rows, :]
        for kv, values, invalid in zip(pieces, flipped, bias):
            scores = dot_t(kv[:, :256], query) + invalid
            peak = jnp.maximum(top, jnp.max(scores, axis=0, keepdims=True))
            keep = jnp.exp(top - peak)
            expo = jnp.exp(scores - peak)
            total = total * keep + jnp.sum(expo, axis=0, keepdims=True)
            low = 64 + 64 * head
            acc = acc * keep + dot(values[low : low + 64, :], expo.astype(BF16))
            top = peak
        if last:
            results.append(acc / total)
            tops.append(top + jnp.log(total))
        else:
            out[rows, :] = acc
            stat[head : head + 1, :] = top
            stat[3 + head : 4 + head, :] = total
    if last:
        whole = jnp.concatenate([jnp.zeros((64, 512), F32)] + results, axis=0)
        out[...] = whole.T.astype(BF16)
        for head in range(HEADS):
            stat[head : head + 1, :] = tops[head]
        stat[3:8, :] = jnp.zeros((5, 512), F32)
    else:
        stat[6:8, :] = jnp.zeros((2, 512), F32)


def attend_back_kernel(parts, first, added, lengths, q_ref, do_ref, lse, inner, *refs):
    pieces, refs = refs[: len(parts)], refs[len(parts) :]
    extras = []
    for at in added:
        extras.append(None if at is None else (at, refs[0]))
        refs = refs if at is None else refs[1:]
    if not first:
        dq_in, refs = refs[0], refs[1:]
    outs, dq_ref = refs[:-1], refs[-1]
    for index, ((away, start), kv) in enumerate(zip(parts, pieces)):
        count = kv.shape[0]
        bias = mask_rows(lengths, away, start, count)
        keys, values = kv[:, :256], kv[:, 128:]
        keys_t = keys.astype(F32).T.astype(BF16)
        dk = jnp.zeros((count, 256), F32)
        dv = jnp.zeros((count, 256), F32)
        for head in range(HEADS):
            query = head_lanes(q_ref[...], head, 0)
            grad = head_lanes(do_ref[...], head, 64)
            probs = jnp.exp(dot_t(keys, query) + bias - lse[head : head + 1, :])
            grad_probs = dot_t(values, grad) - inner[head : head + 1, :]
            grad_scores = (probs * grad_probs).astype(BF16)
            dk = dk + dot(grad_scores, query)
            dv = dv + dot(probs.astype(BF16), grad)
            rows = slice(64 * head, 64 * head + 64)
            dq = dot(keys_t[rows, :], grad_scores)
            if index:
                dq = dq + dq_ref[rows, :]
            elif not first:
                dq = dq + dq_in[rows, :]
            dq_ref[rows, :] = dq
        whole = jnp.concatenate([dk[:, :128], dk[:, 128:] + dv[:, :128], dv[:, 128:]], axis=1)
        out = outs[index]
        if extras[index] is None:
            out[...] = whole.astype(BF16)
        else:
            at, extra = extras[index]
            for low in (0, 256):
                part = whole[low : low + 256]
                if low == at:
                    part = part + extra[...].astype(F32)
                out[low : low + 256, :] = part.astype(BF16)


def under_zeros(w):
    return jnp.concatenate([jnp.zeros((64, 384), BF16), w], axis=0)


def out_kernel(o_ref, w_own, pack, own, other):
    weights = under_zeros(w_own[...]), under_zeros(pack[:192, :])
    for rows, ref in ((slice(256, 512), other), (slice(0, 256), own)):
        ref[:, :384] = dot(o_ref[rows, :], weights[0]).astype(ref.dtype)
        ref[:, 384:] = dot(o_ref[rows, :], weights[1]).astype(ref.dtype)


def normalize(value):
    center = value - jnp.mean(value, axis=1, keepdims=True)
    inverse = lax.rsqrt(jnp.mean(center * center, axis=1, keepdims=True) + EPS)
    return center * inverse, inverse


def back_normalize(grad, normed, inverse, gain):
    scaled = grad * gain
    return inverse * (
        scaled
        - jnp.mean(scaled, axis=1, keepdims=True)
        - normed * jnp.mean(scaled * normed, axis=1, keepdims=True)
    )


def column_sums(*values):
    rows = [jnp.sum(value, axis=0, keepdims=True) for value in values]
    return jnp.concatenate(rows + [jnp.zeros((8 - len(rows), rows[0].shape[1]), F32)], axis=0)


def norm_one_kernel(x, a, b, v_own, pack, normed_ref, inverse_ref, low_ref):
    resid = x[...].astype(F32) + (a[...].astype(F32) + b[...].astype(F32)) + row_of(v_own, pack, 0)
    normed, inverse = normalize(resid)
    normed_ref[...] = normed
    inverse_ref[...] = jnp.broadcast_to(inverse, (256, 128))
    low_ref[...] = (normed * row_of(v_own, pack, 1) + row_of(v_own, pack, 2)).astype(BF16)


def norm_two_kernel(
    normed_one, a, b, cot, v_own, pack, result_ref, grad_ref, low_ref, sums_ref
):
    hidden = normed_one[...] * row_of(v_own, pack, 1) + row_of(v_own, pack, 2)
    resid = hidden + (a[...].astype(F32) + b[...].astype(F32)) + row_of(v_own, pack, 3)
    normed, inverse = normalize(resid)
    gain = row_of(v_own, pack, 4)
    result_ref[...] = (normed * gain + row_of(v_own, pack, 5)).astype(BF16)
    dy = cot[...].astype(F32)
    grad = back_normalize(dy, normed, inverse, gain)
    grad_ref[...] = grad
    low_ref[...] = grad.astype(BF16)
    sums_ref[...] = column_sums(dy * normed, dy, grad)


def norm_back_kernel(
    grad_two, a, b, normed_one, inverse_one, v_own, pack, grad_ref, low_ref, sums_ref
):
    dh = grad_two[...] + (a[...].astype(F32) + b[...].astype(F32))
    normed = normed_one[...]
    grad = back_normalize(dh, normed, inverse_one[:, :1], row_of(v_own, pack, 1))
    grad_ref[...] = grad
    low_ref[...] = grad.astype(BF16)
    sums_ref[...] = column_sums(dh * normed, dh, grad)


def mlp_kernel(h_own, h_other, w_in, w_down, down_other, pack, v_own, g_ref, slope_ref, own, other):
    bias = [v_own[k : k + 1, :].astype(F32) + pack[960 + k : 961 + k, :].astype(F32) for k in (6, 7)]
    for rows, h, ref in ((slice(256, 512), h_other, other), (slice(0, 256), h_own, own)):
        for k, cols in enumerate((slice(0, 384), slice(384, 768))):
            u = dot(h[:, :384], w_in[:, cols]) + bias[k]
            u = u + dot(h[:, 384:], pack[192 + 384 * k : 576 + 384 * k, :])
            cdf = 0.5 + 0.5 * lax.erf(u * 0.7071067811865476)
            slope_ref[rows, cols] = cdf + u * (0.3989422804014327 * jnp.exp(-0.5 * u * u))
            g_ref[rows, cols] = (u * cdf).astype(BF16)
        g = g_ref[rows, :]
        ref[:, :384] = dot(g, w_down[...]).astype(ref.dtype)
        ref[:, 384:] = dot(g, down_other[...]).astype(ref.dtype)


def mlp_back_kernel(
    dz_own, dz_other, w_in, w_down, down_other, pack, slope, du_ref, own, other, sums_ref
):
    total = jnp.zeros((1, 768), F32)
    for rows, dz, ref in ((slice(256, 512), dz_other, other), (slice(0, 256), dz_own, own)):
        dg = dot_t(dz[:, :384], w_down[...]) + dot_t(dz[:, 384:], down_other[...])
        du = (dg * slope[rows, :]).astype(BF16)
        du_ref[rows, :] = du
        total = total + jnp.sum(du.astype(F32), axis=0, keepdims=True)
        ref[:, :384] = dot_t(du, w_in[...]).astype(ref.dtype)
        high = dot_t(du[:, :384], pack[192:576, :]) + dot_t(du[:, 384:], pack[576:960, :])
        ref[:, 384:] = high.astype(ref.dtype)
    sums_ref[...] = jnp.broadcast_to(total, (8, 768))


def out_back_kernel(da_own, da_other, w_own, pack, o_ref, do_ref, inner_ref):
    weights = under_zeros(w_own[...]), under_zeros(pack[:192, :])
    for half, da in enumerate((da_own, da_other)):
        rows = slice(half * 256, half * 256 + 256)
        value = dot_t(da[:, :384], weights[0]) + dot_t(da[:, 384:], weights[1])
        do_ref[rows, :] = value.astype(BF16)
    product = (do_ref[...].astype(F32) * o_ref[...].astype(F32)).T
    rows = [jnp.sum(product[64 + 64 * k : 128 + 64 * k], axis=0, keepdims=True) for k in range(HEADS)]
    inner_ref[...] = jnp.concatenate(rows + [jnp.zeros((5, 512), F32)], axis=0)


def input_back_kernel(dkv, r1, r3, dq_t, w_own, w_other, low_ref, own, other, sums_ref):
    dq = (dq_t[...].T * 0.125).astype(BF16)
    low_ref[:, :256] = jnp.concatenate([dq, jnp.zeros((512, 64), BF16)], axis=1)
    total = dkv[...].astype(F32) + r1[...].astype(F32) + r3[...].astype(F32)
    low_ref[:, 256:] = total.astype(BF16)
    sums_ref[...] = jnp.broadcast_to(
        jnp.sum(low_ref[...].astype(F32), axis=0, keepdims=True), (8, 640)
    )
    for rows, ref in ((slice(256, 512), other), (slice(0, 256), own)):
        for cols, w in ((slice(0, 384), w_own), (slice(384, 768), w_other)):
            value = dot(low_ref[rows, :192], w[:192, :]) + dot(low_ref[rows, 256:], w[192:576, :])
            ref[:, cols] = value.astype(ref.dtype)


def flip(value):
    return value.astype(F32).T.astype(BF16)


def down_grad_kernel(g_ref, dz_own, dz_other, out):
    for part in range(3):
        rows = slice(256 * part, 256 * part + 256)
        left = flip(g_ref[:, rows])
        grad = dot(left[:, :256], dz_own[...]) + dot(left[:, 256:], dz_other[...])
        out[rows, :] = grad.astype(BF16)


def in_grad_kernel(h_own, h_other, du_ref, o_ref, da_own, da_other, out):
    for cols in (slice(0, 384), slice(384, 768)):
        grad = dot(flip(h_own[:, cols]), du_ref[:256, :]) + dot(
            flip(h_other[:, cols]), du_ref[256:, :]
        )
        out[:384, cols] = grad[:, :384].astype(BF16)
        out[384:768, cols] = grad[:, 384:].astype(BF16)
    left = flip(o_ref[...])
    grad = dot(left[64:, :256], da_own[...]) + dot(left[64:, 256:], da_other[...])
    out[768:960, :] = grad.astype(BF16)
    out[960:, :] = jnp.zeros((64, 768), BF16)


def proj_grad_kernel(low_ref, x_own, x_other, sums, core_sums, sums_in, sums_qkv, out, rows):
    for to, cols in ((slice(0, 192), slice(0, 256)), (slice(192, 576), slice(256, 640))):
        left = flip(low_ref[:, cols])[: to.stop - to.start]
        grad = dot(left[:, :256], x_own[...]) + dot(left[:, 256:], x_other[...])
        out[to, :] = grad.astype(BF16)
    h = lax.axis_index("fsdp")
    rows[...] = jnp.zeros((16, 768), F32)
    rows[0:3, :] = sums[0:3, :] + core_sums[0:3, :]
    rows[3:6, :] = sums[8:11, :] + core_sums[8:11, :]
    low, high = sums_in[:1, :384], sums_in[:1, 384:]
    rows[6:7, :384] = jnp.where(h == 0, low, high)
    rows[6:7, 384:] = jnp.where(h == 0, high, low)
    for cols in (slice(0, 384), slice(384, 768)):
        rows[7:8, cols] = sums_qkv[:1, :384]
        rows[8:9, cols] = sums_qkv[:1, 256:]
    out[576:592, :] = rows[...].astype(BF16)
    out[592:, :] = jnp.zeros((48, 768), BF16)


def sum_kernel(*refs):
    own, other = refs[-2:]
    start = 0
    for terms in refs[:-2]:
        total = terms[0].astype(F32)
        for k in range(1, 16):
            total = total + terms[k].astype(F32)
        rows = slice(start, start + total.shape[0])
        own[rows, :] = total[:, :384]
        other[rows, :] = total[:, 384:].astype(BF16)
        start = rows.stop


def copies_kernel(own, other, out):
    value = (own[...] + other[...].astype(F32)).astype(BF16)
    for k in range(16):
        out[k] = value


def early_kernel(src, down, w_in, w_out):
    for k in range(16):
        down[48 * k : 48 * k + 48, :] = src[k, :48, :].astype(F32)
        value = src[k, 48:, :].astype(F32)
        if k < 6:
            w_in[64 * k : 64 * k + 64, :384] = value
        elif k < 12:
            w_in[64 * k - 384 : 64 * k - 320, 384:] = value
        elif k < 15:
            w_out[64 * k - 768 : 64 * k - 704, :] = value


def late_kernel(src, proj, b_qv, *refs):
    vectors, rows = refs[:7], refs[7]
    rows[...] = src[...].astype(F32)
    proj[...] = rows[:576, :]
    for k, ref in enumerate(vectors):
        ref[...] = rows[576 + k, :]
    for k, row in enumerate((rows[583:584, :192], rows[584:585, 192:])):
        b_qv[k : k + 1, :] = jnp.where(lax.axis_index("fsdp") == 0, row[:, :96], row[:, 96:])


def ctx_sum(*terms):
    rows = sum(term.shape[1] for term in terms)
    own, other = call(sum_kernel, [shape((rows, 384), F32), shape((rows, 384), BF16)], *terms)
    return own, fsdp_swap(other)


def gather(own, other, after=()):
    rows = own.shape[0]
    (copies,) = call(copies_kernel, [shape((16, rows, 384), BF16)], own, other, after=after)
    return ctx_exchange(copies.reshape(16 * rows, 384))


def body(
    tokens,
    cotangent,
    lengths,
    w_qkv,
    b_qv,
    w_out,
    b_out,
    ln1_gain,
    ln1_bias,
    w_in,
    b_in,
    w_down,
    b_down,
    ln2_gain,
    ln2_bias,
):
    placed, wt_own = call(
        prepare_kernel,
        [shape((4, 128, 768), BF16), shape((592, 384), BF16)],
        tokens,
        cotangent,
        w_qkv.transpose(0, 2, 1).reshape(576, 384),
        b_qv,
        scratch=[
            pltpu.VMEM((2, 4, 64, 768), BF16),
            pltpu.VMEM((2, 96), BF16),
            pltpu.SemaphoreType.DMA((4,)),
        ],
        load=pl.BlockSpec(memory_space=pl.ANY),
        limit=58,
    )
    wt_other = fsdp_swap(wt_own)
    placed = y_exchange(placed)
    x_own = placed[:, :64].reshape(256, 768)
    x_other = core_swap(x_own)
    query, kv = call(
        qkv_kernel,
        [shape((512, 256), BF16), shape((512, 384), BF16)],
        x_own,
        x_other,
        wt_own,
        wt_other,
    )
    cot = placed[:, 64:].reshape(256, 768)

    pack_own, v_own = call(
        pack_kernel,
        [shape((976, 384), BF16), shape((16, 384), BF16)],
        w_out,
        w_in,
        b_out,
        ln1_gain,
        ln1_bias,
        b_down,
        ln2_gain,
        ln2_bias,
        b_in,
        scratch=[pltpu.VMEM((16, 384), F32)],
        load=pl.BlockSpec(),
    )
    pack_own, w_down, _ = lax.optimization_barrier((pack_own, w_down, wt_other))
    pack = fsdp_swap(pack_own)
    down_other = fsdp_swap(w_down)

    kv_low, kv_high = z_shift(kv, 1), z_shift(kv, -1)
    carry = [shape((192, 512), F32), shape((8, 512), F32)]

    def attend(parts, first, last):
        return lambda *refs: attend_kernel(parts, first, last, *refs)

    acc, stat = call(attend([(0, 0)], True, False), carry, lengths, query, kv, smem=1, after=(pack,), limit=16, us=2.4)
    pass_up, pass_down, acc = lax.optimization_barrier((kv_low[:256], kv_high[256:], acc))
    far_top, far_low = z_shift(pass_up, 1), z_shift(pass_down, -1)
    acc, stat = call(
        attend([(3, 0), (1, 0)], False, False),
        carry,
        lengths,
        query,
        kv_low,
        kv_high,
        acc,
        stat,
        smem=1,
        limit=16,
        us=4.3,
    )
    attn, log_total = call(
        attend([(2, 0), (2, 256)], False, True),
        [shape((512, 256), BF16), shape((8, 512), F32)],
        lengths,
        query,
        far_top,
        far_low,
        acc,
        stat,
        smem=1,
        limit=16,
        us=3,
    )
    halves = [shape((256, 768), F32), shape((256, 768), BF16)]
    own, other = call(out_kernel, halves, attn, w_out, pack, after=(down_other,))
    a, b = tp_sum(own, other)
    normed_one, inverse_one, hidden_own = call(
        norm_one_kernel,
        [shape((256, 768), F32), shape((256, 128), F32), shape((256, 768), BF16)],
        x_own,
        a,
        b,
        v_own,
        pack,
    )
    hidden_other = core_swap(hidden_own)
    gelu, slope, own, other = call(
        mlp_kernel,
        [shape((512, 768), BF16), shape((512, 768), F32)] + halves,
        hidden_own,
        hidden_other,
        w_in,
        w_down,
        down_other,
        pack,
        v_own,
    )
    a, b = tp_sum(own, other)
    result, grad_two, dz_own, sums_two = call(
        norm_two_kernel,
        [
            shape((256, 768), BF16),
            shape((256, 768), F32),
            shape((256, 768), BF16),
            shape((8, 768), F32),
        ],
        normed_one,
        a,
        b,
        cot,
        v_own,
        pack,
    )
    dz_other = core_swap(dz_own)
    du, own, other, sums_in = call(
        mlp_back_kernel,
        [shape((512, 768), BF16)] + halves + [shape((8, 768), F32)],
        dz_own,
        dz_other,
        w_in,
        w_down,
        down_other,
        pack,
        slope,
    )
    a, b = tp_sum(own, other)
    gelu, dz_own, dz_other, _ = lax.optimization_barrier((gelu, dz_own, dz_other, a))
    (down_terms,) = call(down_grad_kernel, [shape((768, 768), BF16)], gelu, dz_own, dz_other)
    down_terms = ctx_exchange(down_terms)
    grad_one, da_own, sums_one = call(
        norm_back_kernel,
        [shape((256, 768), F32), shape((256, 768), BF16), shape((8, 768), F32)],
        grad_two,
        a,
        b,
        normed_one,
        inverse_one,
        v_own,
        pack,
    )
    da_other = core_swap(da_own)
    grad_heads, inner = call(
        out_back_kernel,
        [shape((512, 256), BF16), shape((8, 512), F32)],
        da_own,
        da_other,
        w_out,
        pack,
        attn,
    )
    def attend_back(parts, first, added):
        return lambda *refs: attend_back_kernel(parts, first, added, *refs)

    base = (lengths, query, grad_heads, log_total, inner)
    dq_shape = shape((192, 512), F32)
    half, whole = shape((256, 384), BF16), shape((512, 384), BF16)
    grad_top, grad_low, dq = call(
        attend_back([(2, 0), (2, 256)], True, (None, None)),
        [half, half, dq_shape],
        *base,
        far_top,
        far_low,
        smem=1,
        limit=16,
        us=3.3,
    )
    grad_top, grad_low = z_shift(grad_top, 1), z_shift(grad_low, -1)
    grad_kv, dq = call(
        attend_back([(0, 0)], False, (None,)),
        [whole, dq_shape],
        *base,
        kv,
        dq,
        smem=1,
        us=3,
        fetch=True,
    )
    du, hidden_own, grad_top, grad_low, grad_kv = lax.optimization_barrier(
        (du, hidden_own, grad_top, grad_low, grad_kv)
    )
    (in_terms,) = call(
        in_grad_kernel,
        [shape((1024, 768), BF16)],
        hidden_own,
        hidden_other,
        du,
        attn,
        da_own,
        da_other,
    )
    in_terms = ctx_exchange(in_terms)
    grad_up, grad_down_z, dq = call(
        attend_back([(1, 0), (3, 0)], False, (0, 256)),
        [whole, whole, dq_shape],
        *base,
        kv_high,
        kv_low,
        grad_top,
        grad_low,
        dq,
        smem=1,
        fetch=True,
    )
    early = gather(*ctx_sum(down_terms, in_terms))
    sums = jnp.concatenate([sums_two, sums_one])
    core_sums = core_swap(sums)
    grad_qkv, own, other, sums_qkv = call(
        input_back_kernel,
        [shape((512, 640), BF16)] + halves + [shape((8, 640), F32)],
        grad_kv,
        z_shift(grad_up, 1),
        z_shift(grad_down_z, -1),
        dq,
        wt_own,
        wt_other,
        after=(core_sums,),
        fetch=True,
    )
    (proj_terms,) = call(
        proj_grad_kernel,
        [shape((640, 768), BF16)],
        grad_qkv,
        x_own,
        x_other,
        sums,
        core_sums,
        sums_in,
        sums_qkv,
        scratch=[pltpu.VMEM((16, 768), F32)],
        after=(early,),
    )
    late_own, late_other = ctx_sum(ctx_exchange(proj_terms))
    a, b = tp_sum(own, other)
    grad_x = (grad_one + (a.astype(F32) + b.astype(F32))).astype(BF16)
    outgoing = call(split_kernel, [shape((128, 768), BF16)] * 4, result, grad_x)
    back = jnp.concatenate([outgoing[0]] + [y_shift(outgoing[k], k) for k in (1, 2, 3)])
    late = gather(late_own, late_other, after=(back,)).reshape(640, 384)
    output, grad_tokens = call(
        return_kernel, [shape((4, 128, 768), BF16)] * 2, back, core_swap(back)
    )
    grad_down, grad_in, grad_out = call(
        early_kernel,
        [shape((768, 384), F32), shape((384, 768), F32), shape((192, 384), F32)],
        early,
    )
    grad_proj, grad_b_qv, *vectors = call(
        late_kernel,
        [shape((576, 384), F32), shape((2, 96), F32)] + [shape((384,), F32)] * 7,
        late,
        scratch=[pltpu.VMEM((640, 384), F32)],
    )
    g_gain_two, g_shift_two, g_b_down, g_gain_one, g_shift_one, g_b_out, g_b_in = vectors
    return (
        output,
        grad_tokens,
        grad_proj.reshape(3, 192, 384).transpose(0, 2, 1),
        grad_b_qv,
        grad_out,
        g_b_out,
        g_gain_one,
        g_shift_one,
        grad_in,
        g_b_in,
        grad_down,
        g_b_down,
        g_gain_two,
        g_shift_two,
    )


def solution(mesh):
    placed = (
        P("fsdp", "ctx", None),
        P("fsdp", "ctx", None),
        P("fsdp"),
        P(None, "fsdp", "tp"),
        P(None, ("tp", "fsdp")),
        P("tp", "fsdp"),
        P("fsdp"),
        P("fsdp"),
        P("fsdp"),
        P("fsdp", "tp"),
        P(("tp", "fsdp")),
        P("tp", "fsdp"),
        P("fsdp"),
        P("fsdp"),
        P("fsdp"),
    )
    return jax.shard_map(
        body,
        mesh=mesh,
        in_specs=placed,
        out_specs=placed[:2]
        + (
            P(None, "fsdp", "tp"),
            P(None, ("tp", "fsdp")),
            P("tp", "fsdp"),
            P("fsdp"),
            P("fsdp"),
            P("fsdp"),
            P("fsdp", "tp"),
            P(("tp", "fsdp")),
            P("tp", "fsdp"),
            P("fsdp"),
            P("fsdp"),
            P("fsdp"),
        ),
        check_vma=False,
    )
```

```python
import jax
import jax.numpy as jnp
from jax import lax
from jax.experimental import pallas as pl
from jax.experimental.pallas import tpu as pltpu
from jax.sharding import PartitionSpec as P


EPS = 1e-06
MASKED = -1000000000.0
HEADS = 3
F32 = jnp.float32
BF16 = jnp.bfloat16
VMEM = pl.BlockSpec(memory_space=pltpu.VMEM)
SMEM = pl.BlockSpec(memory_space=pltpu.SMEM)


def core_swap(value):
    return lax.ppermute(value, "tp", [(t, t ^ 1) for t in range(4)])


def chip_swap(value):
    return lax.ppermute(value, "tp", [(t, t ^ 2) for t in range(4)])


def fsdp_swap(value):
    return lax.ppermute(value, "fsdp", [(0, 1), (1, 0)])


def z_shift(value, step):
    return lax.ppermute(
        value, "ctx", [(z * 4 + y, (z + step) % 4 * 4 + y) for z in range(4) for y in range(4)]
    )


def y_shift(value, step):
    return lax.ppermute(
        value, "ctx", [(z * 4 + y, z * 4 + (y + step) % 4) for z in range(4) for y in range(4)]
    )


def y_exchange(value):
    groups = [[z * 4 + y for y in range(4)] for z in range(4)]
    return lax.all_to_all(value, "ctx", 0, 0, axis_index_groups=groups, tiled=True)


def tp_sum(own, other):
    mine = (own + core_swap(other).astype(F32)).astype(BF16)
    return mine, chip_swap(mine)


def ctx_exchange(value):
    terms = lax.all_to_all(value, "ctx", 0, 0, tiled=True)
    return terms.reshape(16, value.shape[0] // 16, value.shape[1])


def call(
    kernel, outs, *args, smem=0, scratch=(), after=(), limit=8, load=VMEM, us=0.1, fetch=False
):
    count, skip = len(args), len(args) + len(after)
    scratch = list(scratch)
    if fetch:
        limit, load = 58, pl.BlockSpec(memory_space=pl.ANY)
        moved = args[smem:]
        scratch += [pltpu.VMEM(a.shape, a.dtype) for a in moved]
        scratch += [pltpu.SemaphoreType.DMA((len(moved),))]

    def run(*refs):
        if not fetch:
            return kernel(*refs[:count], *refs[skip:])
        first = len(refs) - 1 - len(moved)
        buffers, sems = refs[first:-1], refs[-1]
        copies = [
            pltpu.make_async_copy(src, dst, sems.at[k])
            for k, (src, dst) in enumerate(zip(refs[smem:count], buffers))
        ]
        for copy in copies:
            copy.start()
        for copy in copies:
            copy.wait()
        kernel(*refs[:smem], *buffers, *refs[skip:first])

    return pl.pallas_call(
        run,
        out_shape=outs,
        in_specs=[SMEM] * smem
        + [load] * (count - smem)
        + [pl.BlockSpec(memory_space=pl.ANY)] * len(after),
        out_specs=[VMEM] * len(outs),
        scratch_shapes=scratch,
        compiler_params=pltpu.CompilerParams(vmem_limit_bytes=limit * 1024 * 1024),
        cost_estimate=pl.CostEstimate(
            flops=int(us * 1e9), bytes_accessed=1000, transcendentals=0
        ),
    )(*args, *after)


def place_of():
    ctx, tp = lax.axis_index("ctx"), lax.axis_index("tp")
    return (
        lax.shift_right_logical(ctx, 2),
        lax.bitwise_and(ctx, 3),
        lax.bitwise_and(tp, 1),
        lax.axis_index("fsdp"),
    )


def shape(dims, kind):
    return jax.ShapeDtypeStruct(dims, kind)


def dot(a, b):
    return jnp.dot(a, b, preferred_element_type=F32)


def dot_t(a, b):
    return lax.dot_general(a, b, (((1,), (1,)), ((), ())), preferred_element_type=F32)


def pack_kernel(w_out, w_in, v0, v1, v2, v3, v4, v5, b_in, whole, vectors, rows):
    whole[:192, :] = w_out[...]
    whole[192:576, :] = w_in[:, :384]
    whole[576:960, :] = w_in[:, 384:]
    rows[...] = jnp.zeros((16, 384), F32)
    for k, ref in enumerate((v0, v1, v2, v3, v4, v5)):
        rows[k : k + 1, :] = ref[...].astype(F32).reshape(1, 384)
    rows[pl.ds(6 + lax.axis_index("fsdp"), 1), :] = b_in[...].astype(F32).reshape(1, 384)
    whole[960:, :] = rows[...].astype(BF16)
    vectors[...] = rows[...].astype(BF16)


def prepare_kernel(tokens, cotangent, w, b_qv, out, pack, rows_ref, bias_ref, sems):
    _, _, c, h = place_of()
    rows = pl.ds(pl.multiple_of(c * 64, 64), 64)
    copies = [
        pltpu.make_async_copy(w, pack.at[:576, :], sems.at[0]),
        pltpu.make_async_copy(b_qv, bias_ref, sems.at[1]),
        pltpu.make_async_copy(tokens.at[:, rows, :], rows_ref.at[0], sems.at[2]),
        pltpu.make_async_copy(cotangent.at[:, rows, :], rows_ref.at[1], sems.at[3]),
    ]
    for copy in copies:
        copy.start()
    for copy in copies:
        copy.wait()
    for k in range(2):
        for seq in range(4):
            low, high = rows_ref[k, seq, :, :384], rows_ref[k, seq, :, 384:]
            to = slice(64 * k, 64 * k + 64)
            out[seq, to, :384] = jnp.where(h == 0, low, high)
            out[seq, to, 384:] = jnp.where(h == 0, high, low)
    lane = lax.broadcasted_iota(jnp.int32, (96, 384), 1)
    place = lax.broadcasted_iota(jnp.int32, (96, 384), 0) + 96 * h
    spot = jnp.where(lane == place, 1.0, 0.0).astype(BF16)
    bias = jnp.concatenate([dot(bias_ref[...], spot), jnp.zeros((14, 384), F32)], axis=0)
    pack[576:592, :] = bias.astype(BF16)


def row_of(own, pack, k):
    rows = own[...].astype(F32), pack[960:976, :].astype(F32)
    return jnp.concatenate([row[k : k + 1] for row in rows], axis=1)


def split_kernel(output, grad, *pieces):
    _, y, _, _ = place_of()
    for step in range(4):
        rows = pl.ds(pl.multiple_of(64 * lax.bitwise_and(y + step, 3), 64), 64)
        pieces[step][:64, :] = output[rows, :]
        pieces[step][64:, :] = grad[rows, :]


def return_kernel(own, other, out, grad):
    _, y, c, h = place_of()
    for ref, at in ((own, c), (other, 1 - c)):
        for start, dst in ((0, out), (64, grad)):
            for step in range(4):
                row = ref[128 * step + start : 128 * step + start + 64, :]
                first, second = row[:, :384], row[:, 384:]
                rows = pl.ds(pl.multiple_of(at * 64, 64), 64)
                seq = lax.bitwise_and(y + 4 - step, 3)
                dst[seq, rows, :384] = jnp.where(h == 0, first, second)
                dst[seq, rows, 384:] = jnp.where(h == 0, second, first)


def qkv_kernel(x_own, x_other, w_own, w_other, q_ref, kv_ref):
    bias = w_own[576:592, :192].astype(F32) + w_other[576:592, :192].astype(F32)
    bias_q, bias_v = bias[0:1], bias[1:2]
    for half, x in enumerate((x_own, x_other)):
        rows = slice(half * 256, half * 256 + 256)
        low, high = x[:, :384], x[:, 384:]
        query = dot_t(low, w_own[:192, :]) + dot_t(high, w_other[:192, :]) + bias_q
        q_ref[rows, :192] = (query.astype(BF16) * BF16(0.125)).astype(BF16)
        q_ref[rows, 192:] = jnp.zeros((256, 64), BF16)
        key = dot_t(low, w_own[192:384, :]) + dot_t(high, w_other[192:384, :])
        value = dot_t(low, w_own[384:576, :]) + dot_t(high, w_other[384:576, :]) + bias_v
        kv_ref[rows, :] = jnp.concatenate([key, value], axis=1).astype(BF16)


def mask_rows(lengths, away, start, count):
    z, y, c, _ = place_of()
    row = lax.broadcasted_iota(jnp.int32, (count, 128), 0) + start
    half = lax.shift_right_logical(row, 8)
    block = lax.bitwise_and(lax.shift_right_logical(row, 6), 3)
    place = (
        512 * lax.bitwise_and(z + away, 3)
        + 128 * block
        + 64 * jnp.where(half == c, 0, 1)
        + lax.bitwise_and(row, 63)
    )
    bias = jnp.where(place < lengths[y], 0.0, MASKED).astype(F32)
    return jnp.concatenate([bias] * 4, axis=1)


def head_lanes(value, head, offset):
    lane = lax.broadcasted_iota(jnp.int32, value.shape, 1)
    low = offset + 64 * head
    return jnp.where((lane >= low) & (lane < low + 64), value, jnp.zeros_like(value))


def attend_kernel(parts, first, last, lengths, q_ref, *refs):
    pieces, refs = refs[: len(parts)], refs[len(parts) :]
    if not first:
        acc_in, stat_in, refs = refs[0], refs[1], refs[2:]
    out, stat = refs
    flipped = [kv[:, 128:].astype(F32).T.astype(BF16) for kv in pieces]
    bias = [mask_rows(lengths, at, start, kv.shape[0]) for (at, start), kv in zip(parts, pieces)]
    results, tops, totals = [], [], []
    for head in range(HEADS):
        query = head_lanes(q_ref[...], head, 0)
        rows = slice(64 * head, 64 * head + 64)
        if first:
            top = jnp.full((1, 512), -1e30, F32)
            total = jnp.zeros((1, 512), F32)
            acc = jnp.zeros((64, 512), F32)
        else:
            top = stat_in[head : head + 1, :]
            total = stat_in[3 + head : 4 + head, :]
            acc = acc_in[rows, :]
        for kv, values, invalid in zip(pieces, flipped, bias):
            scores = dot_t(kv[:, :256], query) + invalid
            peak = jnp.maximum(top, jnp.max(scores, axis=0, keepdims=True))
            keep = jnp.exp(top - peak)
            expo = jnp.exp(scores - peak)
            total = total * keep + jnp.sum(expo, axis=0, keepdims=True)
            low = 64 + 64 * head
            acc = acc * keep + dot(values[low : low + 64, :], expo.astype(BF16))
            top = peak
        if last:
            results.append(acc / total)
            tops.append(top + jnp.log(total))
        else:
            out[rows, :] = acc
            stat[head : head + 1, :] = top
            stat[3 + head : 4 + head, :] = total
    if last:
        whole = jnp.concatenate([jnp.zeros((64, 512), F32)] + results, axis=0)
        out[...] = whole.T.astype(BF16)
        for head in range(HEADS):
            stat[head : head + 1, :] = tops[head]
        stat[3:8, :] = jnp.zeros((5, 512), F32)
    else:
        stat[6:8, :] = jnp.zeros((2, 512), F32)


def attend_back_kernel(parts, first, added, lengths, q_ref, do_ref, lse, inner, *refs):
    pieces, refs = refs[: len(parts)], refs[len(parts) :]
    extras = []
    for at in added:
        extras.append(None if at is None else (at, refs[0]))
        refs = refs if at is None else refs[1:]
    if not first:
        dq_in, refs = refs[0], refs[1:]
    outs, dq_ref = refs[:-1], refs[-1]
    for index, ((away, start), kv) in enumerate(zip(parts, pieces)):
        count = kv.shape[0]
        bias = mask_rows(lengths, away, start, count)
        keys, values = kv[:, :256], kv[:, 128:]
        keys_t = keys.astype(F32).T.astype(BF16)
        dk = jnp.zeros((count, 256), F32)
        dv = jnp.zeros((count, 256), F32)
        for head in range(HEADS):
            query = head_lanes(q_ref[...], head, 0)
            grad = head_lanes(do_ref[...], head, 64)
            probs = jnp.exp(dot_t(keys, query) + bias - lse[head : head + 1, :])
            grad_probs = dot_t(values, grad) - inner[head : head + 1, :]
            grad_scores = (probs * grad_probs).astype(BF16)
            dk = dk + dot(grad_scores, query)
            dv = dv + dot(probs.astype(BF16), grad)
            rows = slice(64 * head, 64 * head + 64)
            dq = dot(keys_t[rows, :], grad_scores)
            if index:
                dq = dq + dq_ref[rows, :]
            elif not first:
                dq = dq + dq_in[rows, :]
            dq_ref[rows, :] = dq
        whole = jnp.concatenate([dk[:, :128], dk[:, 128:] + dv[:, :128], dv[:, 128:]], axis=1)
        out = outs[index]
        if extras[index] is None:
            out[...] = whole.astype(BF16)
        else:
            at, extra = extras[index]
            for low in (0, 256):
                part = whole[low : low + 256]
                if low == at:
                    part = part + extra[...].astype(F32)
                out[low : low + 256, :] = part.astype(BF16)


def under_zeros(w):
    return jnp.concatenate([jnp.zeros((64, 384), BF16), w], axis=0)


def out_kernel(o_ref, w_own, pack, own, other):
    weights = under_zeros(w_own[...]), under_zeros(pack[:192, :])
    for rows, ref in ((slice(256, 512), other), (slice(0, 256), own)):
        ref[:, :384] = dot(o_ref[rows, :], weights[0]).astype(ref.dtype)
        ref[:, 384:] = dot(o_ref[rows, :], weights[1]).astype(ref.dtype)


def normalize(value):
    center = value - jnp.mean(value, axis=1, keepdims=True)
    inverse = lax.rsqrt(jnp.mean(center * center, axis=1, keepdims=True) + EPS)
    return center * inverse, inverse


def back_normalize(grad, normed, inverse, gain):
    scaled = grad * gain
    return inverse * (
        scaled
        - jnp.mean(scaled, axis=1, keepdims=True)
        - normed * jnp.mean(scaled * normed, axis=1, keepdims=True)
    )


def column_sums(*values):
    rows = [jnp.sum(value, axis=0, keepdims=True) for value in values]
    return jnp.concatenate(rows + [jnp.zeros((8 - len(rows), rows[0].shape[1]), F32)], axis=0)


def norm_one_kernel(x, a, b, v_own, pack, normed_ref, inverse_ref, low_ref):
    resid = x[...].astype(F32) + (a[...].astype(F32) + b[...].astype(F32)) + row_of(v_own, pack, 0)
    normed, inverse = normalize(resid)
    normed_ref[...] = normed
    inverse_ref[...] = jnp.broadcast_to(inverse, (256, 128))
    low_ref[...] = (normed * row_of(v_own, pack, 1) + row_of(v_own, pack, 2)).astype(BF16)


def norm_two_kernel(
    normed_one, a, b, cot, v_own, pack, result_ref, grad_ref, low_ref, sums_ref
):
    hidden = normed_one[...] * row_of(v_own, pack, 1) + row_of(v_own, pack, 2)
    resid = hidden + (a[...].astype(F32) + b[...].astype(F32)) + row_of(v_own, pack, 3)
    normed, inverse = normalize(resid)
    gain = row_of(v_own, pack, 4)
    result_ref[...] = (normed * gain + row_of(v_own, pack, 5)).astype(BF16)
    dy = cot[...].astype(F32)
    grad = back_normalize(dy, normed, inverse, gain)
    grad_ref[...] = grad
    low_ref[...] = grad.astype(BF16)
    sums_ref[...] = column_sums(dy * normed, dy, grad)


def norm_back_kernel(
    grad_two, a, b, normed_one, inverse_one, v_own, pack, grad_ref, low_ref, sums_ref
):
    dh = grad_two[...] + (a[...].astype(F32) + b[...].astype(F32))
    normed = normed_one[...]
    grad = back_normalize(dh, normed, inverse_one[:, :1], row_of(v_own, pack, 1))
    grad_ref[...] = grad
    low_ref[...] = grad.astype(BF16)
    sums_ref[...] = column_sums(dh * normed, dh, grad)


def mlp_kernel(h_own, h_other, w_in, w_down, down_other, pack, v_own, g_ref, slope_ref, own, other):
    bias = v_own[...].astype(F32) + pack[960:976, :].astype(F32)
    bias = [bias[6:7], bias[7:8]]
    for rows, h, ref in ((slice(256, 512), h_other, other), (slice(0, 256), h_own, own)):
        for k, cols in enumerate((slice(0, 384), slice(384, 768))):
            u = dot(h[:, :384], w_in[:, cols]) + bias[k]
            u = u + dot(h[:, 384:], pack[192 + 384 * k : 576 + 384 * k, :])
            cdf = 0.5 + 0.5 * lax.erf(u * 0.7071067811865476)
            slope_ref[rows, cols] = cdf + u * (0.3989422804014327 * jnp.exp(-0.5 * u * u))
            g_ref[rows, cols] = (u * cdf).astype(BF16)
        g = g_ref[rows, :]
        ref[:, :384] = dot(g, w_down[...]).astype(ref.dtype)
        ref[:, 384:] = dot(g, down_other[...]).astype(ref.dtype)


def mlp_back_kernel(
    dz_own, dz_other, w_in, w_down, down_other, pack, slope, du_ref, own, other, sums_ref
):
    total = jnp.zeros((1, 768), F32)
    for rows, dz, ref in ((slice(256, 512), dz_other, other), (slice(0, 256), dz_own, own)):
        dg = dot_t(dz[:, :384], w_down[...]) + dot_t(dz[:, 384:], down_other[...])
        du = (dg * slope[rows, :]).astype(BF16)
        du_ref[rows, :] = du
        total = total + jnp.sum(du.astype(F32), axis=0, keepdims=True)
        ref[:, :384] = dot_t(du, w_in[...]).astype(ref.dtype)
        high = dot_t(du[:, :384], pack[192:576, :]) + dot_t(du[:, 384:], pack[576:960, :])
        ref[:, 384:] = high.astype(ref.dtype)
    sums_ref[...] = jnp.broadcast_to(total, (8, 768))


def out_back_kernel(da_own, da_other, w_own, pack, o_ref, do_ref, inner_ref):
    weights = under_zeros(w_own[...]), under_zeros(pack[:192, :])
    for half, da in enumerate((da_own, da_other)):
        rows = slice(half * 256, half * 256 + 256)
        value = dot_t(da[:, :384], weights[0]) + dot_t(da[:, 384:], weights[1])
        do_ref[rows, :] = value.astype(BF16)
    product = (do_ref[...].astype(F32) * o_ref[...].astype(F32)).T
    rows = [jnp.sum(product[64 + 64 * k : 128 + 64 * k], axis=0, keepdims=True) for k in range(HEADS)]
    inner_ref[...] = jnp.concatenate(rows + [jnp.zeros((5, 512), F32)], axis=0)


def input_back_kernel(dkv, r1, r3, dq_t, w_own, w_other, low_ref, own, other, sums_ref):
    dq = (dq_t[...].T * 0.125).astype(BF16)
    low_ref[:, :256] = jnp.concatenate([dq, jnp.zeros((512, 64), BF16)], axis=1)
    total = dkv[...].astype(F32) + r1[...].astype(F32) + r3[...].astype(F32)
    low_ref[:, 256:] = total.astype(BF16)
    sums_ref[...] = jnp.broadcast_to(
        jnp.sum(low_ref[...].astype(F32), axis=0, keepdims=True), (8, 640)
    )
    for rows, ref in ((slice(256, 512), other), (slice(0, 256), own)):
        for cols, w in ((slice(0, 384), w_own), (slice(384, 768), w_other)):
            value = dot(low_ref[rows, :192], w[:192, :]) + dot(low_ref[rows, 256:], w[192:576, :])
            ref[:, cols] = value.astype(ref.dtype)


def flip(value):
    return value.astype(F32).T.astype(BF16)


def down_grad_kernel(g_ref, dz_own, dz_other, out):
    for part in range(3):
        rows = slice(256 * part, 256 * part + 256)
        left = flip(g_ref[:, rows])
        grad = dot(left[:, :256], dz_own[...]) + dot(left[:, 256:], dz_other[...])
        out[rows, :] = grad.astype(BF16)


def in_grad_kernel(h_own, h_other, du_ref, o_ref, da_own, da_other, out):
    for cols in (slice(0, 384), slice(384, 768)):
        grad = dot(flip(h_own[:, cols]), du_ref[:256, :]) + dot(
            flip(h_other[:, cols]), du_ref[256:, :]
        )
        out[:384, cols] = grad[:, :384].astype(BF16)
        out[384:768, cols] = grad[:, 384:].astype(BF16)
    left = flip(o_ref[...])
    grad = dot(left[64:, :256], da_own[...]) + dot(left[64:, 256:], da_other[...])
    out[768:960, :] = grad.astype(BF16)
    out[960:, :] = jnp.zeros((64, 768), BF16)


def proj_grad_kernel(low_ref, x_own, x_other, sums, core_sums, sums_in, sums_qkv, out, rows):
    for to, cols in ((slice(0, 192), slice(0, 256)), (slice(192, 576), slice(256, 640))):
        left = flip(low_ref[:, cols])[: to.stop - to.start]
        grad = dot(left[:, :256], x_own[...]) + dot(left[:, 256:], x_other[...])
        out[to, :] = grad.astype(BF16)
    h = lax.axis_index("fsdp")
    rows[...] = jnp.zeros((16, 768), F32)
    rows[0:3, :] = sums[0:3, :] + core_sums[0:3, :]
    rows[3:6, :] = sums[8:11, :] + core_sums[8:11, :]
    low, high = sums_in[:1, :384], sums_in[:1, 384:]
    rows[6:7, :384] = jnp.where(h == 0, low, high)
    rows[6:7, 384:] = jnp.where(h == 0, high, low)
    for cols in (slice(0, 384), slice(384, 768)):
        rows[7:8, cols] = sums_qkv[:1, :384]
        rows[8:9, cols] = sums_qkv[:1, 256:]
    out[576:592, :] = rows[...].astype(BF16)
    out[592:, :] = jnp.zeros((48, 768), BF16)


def sum_kernel(*refs):
    own, other = refs[-2:]
    start = 0
    for terms in refs[:-2]:
        total = terms[0].astype(F32)
        for k in range(1, 16):
            total = total + terms[k].astype(F32)
        rows = slice(start, start + total.shape[0])
        own[rows, :] = total[:, :384]
        other[rows, :] = total[:, 384:].astype(BF16)
        start = rows.stop


def copies_kernel(own, other, out):
    value = (own[...] + other[...].astype(F32)).astype(BF16)
    for k in range(16):
        out[k] = value


def early_kernel(src, down, w_in, w_out):
    for k in range(16):
        down[48 * k : 48 * k + 48, :] = src[k, :48, :].astype(F32)
        value = src[k, 48:, :].astype(F32)
        if k < 6:
            w_in[64 * k : 64 * k + 64, :384] = value
        elif k < 12:
            w_in[64 * k - 384 : 64 * k - 320, 384:] = value
        elif k < 15:
            w_out[64 * k - 768 : 64 * k - 704, :] = value


def late_kernel(src, proj, b_qv, *refs):
    vectors, rows = refs[:7], refs[7]
    rows[...] = src[...].astype(F32)
    proj[...] = rows[:576, :]
    for k, ref in enumerate(vectors):
        ref[...] = rows[576 + k, :]
    for k, row in enumerate((rows[583:584, :192], rows[584:585, 192:])):
        b_qv[k : k + 1, :] = jnp.where(lax.axis_index("fsdp") == 0, row[:, :96], row[:, 96:])


def ctx_sum(*terms):
    rows = sum(term.shape[1] for term in terms)
    own, other = call(sum_kernel, [shape((rows, 384), F32), shape((rows, 384), BF16)], *terms)
    return own, fsdp_swap(other)


def gather(own, other, after=()):
    rows = own.shape[0]
    (copies,) = call(copies_kernel, [shape((16, rows, 384), BF16)], own, other, after=after)
    return ctx_exchange(copies.reshape(16 * rows, 384))


def body(
    tokens,
    cotangent,
    lengths,
    w_qkv,
    b_qv,
    w_out,
    b_out,
    ln1_gain,
    ln1_bias,
    w_in,
    b_in,
    w_down,
    b_down,
    ln2_gain,
    ln2_bias,
):
    placed, wt_own = call(
        prepare_kernel,
        [shape((4, 128, 768), BF16), shape((592, 384), BF16)],
        tokens,
        cotangent,
        w_qkv.transpose(0, 2, 1).reshape(576, 384),
        b_qv,
        scratch=[
            pltpu.VMEM((2, 4, 64, 768), BF16),
            pltpu.VMEM((2, 96), BF16),
            pltpu.SemaphoreType.DMA((4,)),
        ],
        load=pl.BlockSpec(memory_space=pl.ANY),
        limit=58,
    )
    wt_other = fsdp_swap(wt_own)
    placed = y_exchange(placed)
    x_own = placed[:, :64].reshape(256, 768)
    x_other = core_swap(x_own)
    query, kv = call(
        qkv_kernel,
        [shape((512, 256), BF16), shape((512, 384), BF16)],
        x_own,
        x_other,
        wt_own,
        wt_other,
    )
    cot = placed[:, 64:].reshape(256, 768)

    pack_own, v_own = call(
        pack_kernel,
        [shape((976, 384), BF16), shape((16, 384), BF16)],
        w_out,
        w_in,
        b_out,
        ln1_gain,
        ln1_bias,
        b_down,
        ln2_gain,
        ln2_bias,
        b_in,
        scratch=[pltpu.VMEM((16, 384), F32)],
        load=pl.BlockSpec(),
    )
    pack_own, w_down, _ = lax.optimization_barrier((pack_own, w_down, wt_other))
    pack = fsdp_swap(pack_own)
    down_other = fsdp_swap(w_down)

    kv_low, kv_high = z_shift(kv, 1), z_shift(kv, -1)
    carry = [shape((192, 512), F32), shape((8, 512), F32)]

    def attend(parts, first, last):
        return lambda *refs: attend_kernel(parts, first, last, *refs)

    acc, stat = call(attend([(0, 0)], True, False), carry, lengths, query, kv, smem=1, after=(pack,), limit=16, us=2.4)
    pass_up, pass_down, acc = lax.optimization_barrier((kv_low[:256], kv_high[256:], acc))
    far_top, far_low = z_shift(pass_up, 1), z_shift(pass_down, -1)
    acc, stat = call(
        attend([(3, 0), (1, 0)], False, False),
        carry,
        lengths,
        query,
        kv_low,
        kv_high,
        acc,
        stat,
        smem=1,
        limit=16,
        us=4.3,
    )
    attn, log_total = call(
        attend([(2, 0), (2, 256)], False, True),
        [shape((512, 256), BF16), shape((8, 512), F32)],
        lengths,
        query,
        far_top,
        far_low,
        acc,
        stat,
        smem=1,
        limit=16,
        us=3,
    )
    halves = [shape((256, 768), F32), shape((256, 768), BF16)]
    own, other = call(out_kernel, halves, attn, w_out, pack, after=(down_other,))
    a, b = tp_sum(own, other)
    normed_one, inverse_one, hidden_own = call(
        norm_one_kernel,
        [shape((256, 768), F32), shape((256, 128), F32), shape((256, 768), BF16)],
        x_own,
        a,
        b,
        v_own,
        pack,
    )
    hidden_other = core_swap(hidden_own)
    gelu, slope, own, other = call(
        mlp_kernel,
        [shape((512, 768), BF16), shape((512, 768), F32)] + halves,
        hidden_own,
        hidden_other,
        w_in,
        w_down,
        down_other,
        pack,
        v_own,
    )
    a, b = tp_sum(own, other)
    result, grad_two, dz_own, sums_two = call(
        norm_two_kernel,
        [
            shape((256, 768), BF16),
            shape((256, 768), F32),
            shape((256, 768), BF16),
            shape((8, 768), F32),
        ],
        normed_one,
        a,
        b,
        cot,
        v_own,
        pack,
    )
    dz_other = core_swap(dz_own)
    du, own, other, sums_in = call(
        mlp_back_kernel,
        [shape((512, 768), BF16)] + halves + [shape((8, 768), F32)],
        dz_own,
        dz_other,
        w_in,
        w_down,
        down_other,
        pack,
        slope,
    )
    a, b = tp_sum(own, other)
    gelu, dz_own, dz_other, _ = lax.optimization_barrier((gelu, dz_own, dz_other, a))
    (down_terms,) = call(down_grad_kernel, [shape((768, 768), BF16)], gelu, dz_own, dz_other)
    down_terms = ctx_exchange(down_terms)
    grad_one, da_own, sums_one = call(
        norm_back_kernel,
        [shape((256, 768), F32), shape((256, 768), BF16), shape((8, 768), F32)],
        grad_two,
        a,
        b,
        normed_one,
        inverse_one,
        v_own,
        pack,
    )
    da_other = core_swap(da_own)
    grad_heads, inner = call(
        out_back_kernel,
        [shape((512, 256), BF16), shape((8, 512), F32)],
        da_own,
        da_other,
        w_out,
        pack,
        attn,
    )
    def attend_back(parts, first, added):
        return lambda *refs: attend_back_kernel(parts, first, added, *refs)

    base = (lengths, query, grad_heads, log_total, inner)
    dq_shape = shape((192, 512), F32)
    half, whole = shape((256, 384), BF16), shape((512, 384), BF16)
    grad_top, grad_low, dq = call(
        attend_back([(2, 0), (2, 256)], True, (None, None)),
        [half, half, dq_shape],
        *base,
        far_top,
        far_low,
        smem=1,
        limit=16,
        us=3.3,
    )
    grad_top, grad_low = z_shift(grad_top, 1), z_shift(grad_low, -1)
    grad_kv, dq = call(
        attend_back([(0, 0)], False, (None,)),
        [whole, dq_shape],
        *base,
        kv,
        dq,
        smem=1,
        us=3,
        fetch=True,
    )
    du, hidden_own, grad_top, grad_low, grad_kv = lax.optimization_barrier(
        (du, hidden_own, grad_top, grad_low, grad_kv)
    )
    (in_terms,) = call(
        in_grad_kernel,
        [shape((1024, 768), BF16)],
        hidden_own,
        hidden_other,
        du,
        attn,
        da_own,
        da_other,
    )
    in_terms = ctx_exchange(in_terms)
    grad_up, grad_down_z, dq = call(
        attend_back([(1, 0), (3, 0)], False, (0, 256)),
        [whole, whole, dq_shape],
        *base,
        kv_high,
        kv_low,
        grad_top,
        grad_low,
        dq,
        smem=1,
        fetch=True,
    )
    early = gather(*ctx_sum(down_terms, in_terms))
    sums = jnp.concatenate([sums_two, sums_one])
    core_sums = core_swap(sums)
    grad_qkv, own, other, sums_qkv = call(
        input_back_kernel,
        [shape((512, 640), BF16)] + halves + [shape((8, 640), F32)],
        grad_kv,
        z_shift(grad_up, 1),
        z_shift(grad_down_z, -1),
        dq,
        wt_own,
        wt_other,
        after=(core_sums,),
        fetch=True,
    )
    (proj_terms,) = call(
        proj_grad_kernel,
        [shape((640, 768), BF16)],
        grad_qkv,
        x_own,
        x_other,
        sums,
        core_sums,
        sums_in,
        sums_qkv,
        scratch=[pltpu.VMEM((16, 768), F32)],
        after=(early,),
    )
    late_own, late_other = ctx_sum(ctx_exchange(proj_terms))
    a, b = tp_sum(own, other)
    grad_x = (grad_one + (a.astype(F32) + b.astype(F32))).astype(BF16)
    outgoing = call(split_kernel, [shape((128, 768), BF16)] * 4, result, grad_x)
    back = jnp.concatenate([outgoing[0]] + [y_shift(outgoing[k], k) for k in (1, 2, 3)])
    late = gather(late_own, late_other, after=(back,)).reshape(640, 384)
    output, grad_tokens = call(
        return_kernel, [shape((4, 128, 768), BF16)] * 2, back, core_swap(back)
    )
    grad_down, grad_in, grad_out = call(
        early_kernel,
        [shape((768, 384), F32), shape((384, 768), F32), shape((192, 384), F32)],
        early,
    )
    grad_proj, grad_b_qv, *vectors = call(
        late_kernel,
        [shape((576, 384), F32), shape((2, 96), F32)] + [shape((384,), F32)] * 7,
        late,
        scratch=[pltpu.VMEM((640, 384), F32)],
    )
    g_gain_two, g_shift_two, g_b_down, g_gain_one, g_shift_one, g_b_out, g_b_in = vectors
    return (
        output,
        grad_tokens,
        grad_proj.reshape(3, 192, 384).transpose(0, 2, 1),
        grad_b_qv,
        grad_out,
        g_b_out,
        g_gain_one,
        g_shift_one,
        grad_in,
        g_b_in,
        grad_down,
        g_b_down,
        g_gain_two,
        g_shift_two,
    )


def solution(mesh):
    placed = (
        P("fsdp", "ctx", None),
        P("fsdp", "ctx", None),
        P("fsdp"),
        P(None, "fsdp", "tp"),
        P(None, ("tp", "fsdp")),
        P("tp", "fsdp"),
        P("fsdp"),
        P("fsdp"),
        P("fsdp"),
        P("fsdp", "tp"),
        P(("tp", "fsdp")),
        P("tp", "fsdp"),
        P("fsdp"),
        P("fsdp"),
        P("fsdp"),
    )
    return jax.shard_map(
        body,
        mesh=mesh,
        in_specs=placed,
        out_specs=placed[:2]
        + (
            P(None, "fsdp", "tp"),
            P(None, ("tp", "fsdp")),
            P("tp", "fsdp"),
            P("fsdp"),
            P("fsdp"),
            P("fsdp"),
            P("fsdp", "tp"),
            P(("tp", "fsdp")),
            P("tp", "fsdp"),
            P("fsdp"),
            P("fsdp"),
            P("fsdp"),
        ),
        check_vma=False,
    )
```

```python
import jax
import jax.numpy as jnp
from jax import lax
from jax.experimental import pallas as pl
from jax.experimental.pallas import tpu as pltpu
from jax.sharding import PartitionSpec as P


EPS = 1e-06
MASKED = -1000000000.0
HEADS = 3
F32 = jnp.float32
BF16 = jnp.bfloat16
VMEM = pl.BlockSpec(memory_space=pltpu.VMEM)
SMEM = pl.BlockSpec(memory_space=pltpu.SMEM)


def core_swap(value):
    return lax.ppermute(value, "tp", [(t, t ^ 1) for t in range(4)])


def chip_swap(value):
    return lax.ppermute(value, "tp", [(t, t ^ 2) for t in range(4)])


def fsdp_swap(value):
    return lax.ppermute(value, "fsdp", [(0, 1), (1, 0)])


def z_shift(value, step):
    return lax.ppermute(
        value, "ctx", [(z * 4 + y, (z + step) % 4 * 4 + y) for z in range(4) for y in range(4)]
    )


def y_shift(value, step):
    return lax.ppermute(
        value, "ctx", [(z * 4 + y, z * 4 + (y + step) % 4) for z in range(4) for y in range(4)]
    )


def y_exchange(value):
    groups = [[z * 4 + y for y in range(4)] for z in range(4)]
    return lax.all_to_all(value, "ctx", 0, 0, axis_index_groups=groups, tiled=True)


def tp_sum(own, other):
    mine = (own + core_swap(other).astype(F32)).astype(BF16)
    return mine, chip_swap(mine)


def ctx_exchange(value):
    terms = lax.all_to_all(value, "ctx", 0, 0, tiled=True)
    return terms.reshape(16, value.shape[0] // 16, value.shape[1])


def call(
    kernel, outs, *args, smem=0, scratch=(), after=(), limit=8, load=VMEM, us=0.1, fetch=False
):
    count, skip = len(args), len(args) + len(after)
    scratch = list(scratch)
    if fetch:
        limit, load = 58, pl.BlockSpec(memory_space=pl.ANY)
        moved = args[smem:]
        scratch += [pltpu.VMEM(a.shape, a.dtype) for a in moved]
        scratch += [pltpu.SemaphoreType.DMA((len(moved),))]

    def run(*refs):
        if not fetch:
            return kernel(*refs[:count], *refs[skip:])
        first = len(refs) - 1 - len(moved)
        buffers, sems = refs[first:-1], refs[-1]
        copies = [
            pltpu.make_async_copy(src, dst, sems.at[k])
            for k, (src, dst) in enumerate(zip(refs[smem:count], buffers))
        ]
        for copy in copies:
            copy.start()
        for copy in copies:
            copy.wait()
        kernel(*refs[:smem], *buffers, *refs[skip:first])

    return pl.pallas_call(
        run,
        out_shape=outs,
        in_specs=[SMEM] * smem
        + [load] * (count - smem)
        + [pl.BlockSpec(memory_space=pl.ANY)] * len(after),
        out_specs=[VMEM] * len(outs),
        scratch_shapes=scratch,
        compiler_params=pltpu.CompilerParams(vmem_limit_bytes=limit * 1024 * 1024),
        cost_estimate=pl.CostEstimate(
            flops=int(us * 1e9), bytes_accessed=1000, transcendentals=0
        ),
    )(*args, *after)


def place_of():
    ctx, tp = lax.axis_index("ctx"), lax.axis_index("tp")
    return (
        lax.shift_right_logical(ctx, 2),
        lax.bitwise_and(ctx, 3),
        lax.bitwise_and(tp, 1),
        lax.axis_index("fsdp"),
    )


def shape(dims, kind):
    return jax.ShapeDtypeStruct(dims, kind)


def dot(a, b):
    return jnp.dot(a, b, preferred_element_type=F32)


def dot_t(a, b):
    return lax.dot_general(a, b, (((1,), (1,)), ((), ())), preferred_element_type=F32)


def pack_kernel(w_out, w_in, v0, v1, v2, v3, v4, v5, b_in, whole, vectors, rows):
    whole[:192, :] = w_out[...]
    whole[192:576, :] = w_in[:, :384]
    whole[576:960, :] = w_in[:, 384:]
    rows[...] = jnp.zeros((16, 384), F32)
    for k, ref in enumerate((v0, v1, v2, v3, v4, v5)):
        rows[k : k + 1, :] = ref[...].astype(F32).reshape(1, 384)
    rows[pl.ds(6 + lax.axis_index("fsdp"), 1), :] = b_in[...].astype(F32).reshape(1, 384)
    whole[960:, :] = rows[...].astype(BF16)
    vectors[...] = rows[...].astype(BF16)


def prepare_kernel(tokens, cotangent, w, b_qv, out, pack, rows_ref, bias_ref, sems):
    _, _, c, h = place_of()
    rows = pl.ds(pl.multiple_of(c * 64, 64), 64)
    copies = [
        pltpu.make_async_copy(w, pack.at[:576, :], sems.at[0]),
        pltpu.make_async_copy(b_qv, bias_ref, sems.at[1]),
        pltpu.make_async_copy(tokens.at[:, rows, :], rows_ref.at[0], sems.at[2]),
        pltpu.make_async_copy(cotangent.at[:, rows, :], rows_ref.at[1], sems.at[3]),
    ]
    for copy in copies:
        copy.start()
    for copy in copies:
        copy.wait()
    for k in range(2):
        for seq in range(4):
            low, high = rows_ref[k, seq, :, :384], rows_ref[k, seq, :, 384:]
            to = slice(64 * k, 64 * k + 64)
            out[seq, to, :384] = jnp.where(h == 0, low, high)
            out[seq, to, 384:] = jnp.where(h == 0, high, low)
    lane = lax.broadcasted_iota(jnp.int32, (96, 384), 1)
    place = lax.broadcasted_iota(jnp.int32, (96, 384), 0) + 96 * h
    spot = jnp.where(lane == place, 1.0, 0.0).astype(BF16)
    bias = jnp.concatenate([dot(bias_ref[...], spot), jnp.zeros((14, 384), F32)], axis=0)
    pack[576:592, :] = bias.astype(BF16)


def row_of(own, pack, k):
    rows = own[...].astype(F32), pack[960:976, :].astype(F32)
    return jnp.concatenate([row[k : k + 1] for row in rows], axis=1)


def split_kernel(output, grad, *pieces):
    _, y, _, _ = place_of()
    for step in range(4):
        rows = pl.ds(pl.multiple_of(64 * lax.bitwise_and(y + step, 3), 64), 64)
        pieces[step][:64, :] = output[rows, :]
        pieces[step][64:, :] = grad[rows, :]


def return_kernel(own, other, out, grad):
    _, y, c, h = place_of()
    for ref, at in ((own, c), (other, 1 - c)):
        for start, dst in ((0, out), (64, grad)):
            for step in range(4):
                row = ref[128 * step + start : 128 * step + start + 64, :]
                first, second = row[:, :384], row[:, 384:]
                rows = pl.ds(pl.multiple_of(at * 64, 64), 64)
                seq = lax.bitwise_and(y + 4 - step, 3)
                dst[seq, rows, :384] = jnp.where(h == 0, first, second)
                dst[seq, rows, 384:] = jnp.where(h == 0, second, first)


def qkv_kernel(x_own, x_other, w_own, w_other, q_ref, kv_ref):
    bias = w_own[576:592, :192].astype(F32) + w_other[576:592, :192].astype(F32)
    bias_q, bias_v = bias[0:1], bias[1:2]
    for half, x in enumerate((x_own, x_other)):
        rows = slice(half * 256, half * 256 + 256)
        low, high = x[:, :384], x[:, 384:]
        query = dot_t(low, w_own[:192, :]) + dot_t(high, w_other[:192, :]) + bias_q
        q_ref[rows, :192] = (query.astype(BF16) * BF16(0.125)).astype(BF16)
        q_ref[rows, 192:] = jnp.zeros((256, 64), BF16)
        key = dot_t(low, w_own[192:384, :]) + dot_t(high, w_other[192:384, :])
        value = dot_t(low, w_own[384:576, :]) + dot_t(high, w_other[384:576, :]) + bias_v
        kv_ref[rows, :] = jnp.concatenate([key, value], axis=1).astype(BF16)


def mask_rows(lengths, away, start, count):
    z, y, c, _ = place_of()
    row = lax.broadcasted_iota(jnp.int32, (count, 128), 0) + start
    half = lax.shift_right_logical(row, 8)
    block = lax.bitwise_and(lax.shift_right_logical(row, 6), 3)
    place = (
        512 * lax.bitwise_and(z + away, 3)
        + 128 * block
        + 64 * jnp.where(half == c, 0, 1)
        + lax.bitwise_and(row, 63)
    )
    bias = jnp.where(place < lengths[y], 0.0, MASKED).astype(F32)
    return jnp.concatenate([bias] * 4, axis=1)


def head_lanes(value, head, offset):
    lane = lax.broadcasted_iota(jnp.int32, value.shape, 1)
    low = offset + 64 * head
    return jnp.where((lane >= low) & (lane < low + 64), value, jnp.zeros_like(value))


def attend_kernel(parts, first, last, lengths, q_ref, *refs):
    pieces, refs = refs[: len(parts)], refs[len(parts) :]
    if not first:
        acc_in, stat_in, refs = refs[0], refs[1], refs[2:]
    out, stat = refs
    flipped = [kv[:, 128:].astype(F32).T.astype(BF16) for kv in pieces]
    bias = [mask_rows(lengths, at, start, kv.shape[0]) for (at, start), kv in zip(parts, pieces)]
    results, tops, totals = [], [], []
    for head in range(HEADS):
        query = head_lanes(q_ref[...], head, 0)
        rows = slice(64 * head, 64 * head + 64)
        if first:
            top = jnp.full((1, 512), -1e30, F32)
            total = jnp.zeros((1, 512), F32)
            acc = jnp.zeros((64, 512), F32)
        else:
            top = stat_in[head : head + 1, :]
            total = stat_in[3 + head : 4 + head, :]
            acc = acc_in[rows, :]
        for kv, values, invalid in zip(pieces, flipped, bias):
            scores = dot_t(kv[:, :256], query) + invalid
            peak = jnp.maximum(top, jnp.max(scores, axis=0, keepdims=True))
            keep = jnp.exp(top - peak)
            expo = jnp.exp(scores - peak)
            total = total * keep + jnp.sum(expo, axis=0, keepdims=True)
            low = 64 + 64 * head
            acc = acc * keep + dot(values[low : low + 64, :], expo.astype(BF16))
            top = peak
        if last:
            results.append(acc / total)
            tops.append(top + jnp.log(total))
        else:
            out[rows, :] = acc
            stat[head : head + 1, :] = top
            stat[3 + head : 4 + head, :] = total
    if last:
        whole = jnp.concatenate([jnp.zeros((64, 512), F32)] + results, axis=0)
        out[...] = whole.T.astype(BF16)
        for head in range(HEADS):
            stat[head : head + 1, :] = tops[head]
        stat[3:8, :] = jnp.zeros((5, 512), F32)
    else:
        stat[6:8, :] = jnp.zeros((2, 512), F32)


def attend_back_kernel(parts, first, added, lengths, q_ref, do_ref, lse, inner, *refs):
    pieces, refs = refs[: len(parts)], refs[len(parts) :]
    extras = []
    for at in added:
        extras.append(None if at is None else (at, refs[0]))
        refs = refs if at is None else refs[1:]
    if not first:
        dq_in, refs = refs[0], refs[1:]
    outs, dq_ref = refs[:-1], refs[-1]
    for index, ((away, start), kv) in enumerate(zip(parts, pieces)):
        count = kv.shape[0]
        bias = mask_rows(lengths, away, start, count)
        keys, values = kv[:, :256], kv[:, 128:]
        keys_t = keys.astype(F32).T.astype(BF16)
        dk = jnp.zeros((count, 256), F32)
        dv = jnp.zeros((count, 256), F32)
        for head in range(HEADS):
            query = head_lanes(q_ref[...], head, 0)
            grad = head_lanes(do_ref[...], head, 64)
            probs = jnp.exp(dot_t(keys, query) + bias - lse[head : head + 1, :])
            grad_probs = dot_t(values, grad) - inner[head : head + 1, :]
            grad_scores = (probs * grad_probs).astype(BF16)
            dk = dk + dot(grad_scores, query)
            dv = dv + dot(probs.astype(BF16), grad)
            rows = slice(64 * head, 64 * head + 64)
            dq = dot(keys_t[rows, :], grad_scores)
            if index:
                dq = dq + dq_ref[rows, :]
            elif not first:
                dq = dq + dq_in[rows, :]
            dq_ref[rows, :] = dq
        whole = jnp.concatenate([dk[:, :128], dk[:, 128:] + dv[:, :128], dv[:, 128:]], axis=1)
        out = outs[index]
        if extras[index] is None:
            out[...] = whole.astype(BF16)
        else:
            at, extra = extras[index]
            for low in (0, 256):
                part = whole[low : low + 256]
                if low == at:
                    part = part + extra[...].astype(F32)
                out[low : low + 256, :] = part.astype(BF16)


def under_zeros(w):
    return jnp.concatenate([jnp.zeros((64, 384), BF16), w], axis=0)


def out_kernel(o_ref, w_own, pack, own, other):
    weights = under_zeros(w_own[...]), under_zeros(pack[:192, :])
    for rows, ref in ((slice(256, 512), other), (slice(0, 256), own)):
        ref[:, :384] = dot(o_ref[rows, :], weights[0]).astype(ref.dtype)
        ref[:, 384:] = dot(o_ref[rows, :], weights[1]).astype(ref.dtype)


def normalize(value):
    center = value - jnp.mean(value, axis=1, keepdims=True)
    inverse = lax.rsqrt(jnp.mean(center * center, axis=1, keepdims=True) + EPS)
    return center * inverse, inverse


def back_normalize(grad, normed, inverse, gain):
    scaled = grad * gain
    return inverse * (
        scaled
        - jnp.mean(scaled, axis=1, keepdims=True)
        - normed * jnp.mean(scaled * normed, axis=1, keepdims=True)
    )


def column_sums(*values):
    rows = [jnp.sum(value, axis=0, keepdims=True) for value in values]
    return jnp.concatenate(rows + [jnp.zeros((8 - len(rows), rows[0].shape[1]), F32)], axis=0)


def norm_one_kernel(x, a, b, v_own, pack, normed_ref, inverse_ref, low_ref):
    resid = x[...].astype(F32) + (a[...].astype(F32) + b[...].astype(F32)) + row_of(v_own, pack, 0)
    normed, inverse = normalize(resid)
    normed_ref[...] = normed
    inverse_ref[...] = jnp.broadcast_to(inverse, (256, 128))
    low_ref[...] = (normed * row_of(v_own, pack, 1) + row_of(v_own, pack, 2)).astype(BF16)


def norm_two_kernel(
    normed_one, a, b, cot, v_own, pack, result_ref, grad_ref, low_ref, sums_ref
):
    hidden = normed_one[...] * row_of(v_own, pack, 1) + row_of(v_own, pack, 2)
    resid = hidden + (a[...].astype(F32) + b[...].astype(F32)) + row_of(v_own, pack, 3)
    normed, inverse = normalize(resid)
    gain = row_of(v_own, pack, 4)
    result_ref[...] = (normed * gain + row_of(v_own, pack, 5)).astype(BF16)
    dy = cot[...].astype(F32)
    grad = back_normalize(dy, normed, inverse, gain)
    grad_ref[...] = grad
    low_ref[...] = grad.astype(BF16)
    sums_ref[...] = column_sums(dy * normed, dy, grad)


def norm_back_kernel(
    grad_two, a, b, normed_one, inverse_one, v_own, pack, grad_ref, low_ref, sums_ref
):
    dh = grad_two[...] + (a[...].astype(F32) + b[...].astype(F32))
    normed = normed_one[...]
    grad = back_normalize(dh, normed, inverse_one[:, :1], row_of(v_own, pack, 1))
    grad_ref[...] = grad
    low_ref[...] = grad.astype(BF16)
    sums_ref[...] = column_sums(dh * normed, dh, grad)


def mlp_kernel(h_own, h_other, w_in, w_down, down_other, pack, v_own, g_ref, slope_ref, own, other):
    bias = v_own[...].astype(F32) + pack[960:976, :].astype(F32)
    bias = [bias[6:7], bias[7:8]]
    for rows, h, ref in ((slice(256, 512), h_other, other), (slice(0, 256), h_own, own)):
        for k, cols in enumerate((slice(0, 384), slice(384, 768))):
            u = dot(h[:, :384], w_in[:, cols]) + bias[k]
            u = u + dot(h[:, 384:], pack[192 + 384 * k : 576 + 384 * k, :])
            cdf = 0.5 + 0.5 * lax.erf(u * 0.7071067811865476)
            slope_ref[rows, cols] = cdf + u * (0.3989422804014327 * jnp.exp(-0.5 * u * u))
            g_ref[rows, cols] = (u * cdf).astype(BF16)
        g = g_ref[rows, :]
        ref[:, :384] = dot(g, w_down[...]).astype(ref.dtype)
        ref[:, 384:] = dot(g, down_other[...]).astype(ref.dtype)


def mlp_back_kernel(
    dz_own, dz_other, w_in, w_down, down_other, pack, slope, du_ref, own, other, sums_ref
):
    total = jnp.zeros((1, 768), F32)
    for rows, dz, ref in ((slice(256, 512), dz_other, other), (slice(0, 256), dz_own, own)):
        dg = dot_t(dz[:, :384], w_down[...]) + dot_t(dz[:, 384:], down_other[...])
        du = (dg * slope[rows, :]).astype(BF16)
        du_ref[rows, :] = du
        total = total + jnp.sum(du.astype(F32), axis=0, keepdims=True)
        ref[:, :384] = dot_t(du, w_in[...]).astype(ref.dtype)
        high = dot_t(du[:, :384], pack[192:576, :]) + dot_t(du[:, 384:], pack[576:960, :])
        ref[:, 384:] = high.astype(ref.dtype)
    sums_ref[...] = jnp.broadcast_to(total, (8, 768))


def out_back_kernel(da_own, da_other, w_own, pack, o_ref, do_ref, inner_ref):
    weights = under_zeros(w_own[...]), under_zeros(pack[:192, :])
    for half, da in enumerate((da_own, da_other)):
        rows = slice(half * 256, half * 256 + 256)
        value = dot_t(da[:, :384], weights[0]) + dot_t(da[:, 384:], weights[1])
        do_ref[rows, :] = value.astype(BF16)
    product = (do_ref[...].astype(F32) * o_ref[...].astype(F32)).T
    rows = [jnp.sum(product[64 + 64 * k : 128 + 64 * k], axis=0, keepdims=True) for k in range(HEADS)]
    inner_ref[...] = jnp.concatenate(rows + [jnp.zeros((5, 512), F32)], axis=0)


def input_back_kernel(dkv, r1, r3, dq_t, w_own, w_other, low_ref, own, other, sums_ref):
    dq = (dq_t[...].T * 0.125).astype(BF16)
    low_ref[:, :256] = jnp.concatenate([dq, jnp.zeros((512, 64), BF16)], axis=1)
    total = dkv[...].astype(F32) + r1[...].astype(F32) + r3[...].astype(F32)
    low_ref[:, 256:] = total.astype(BF16)
    sums_ref[...] = jnp.broadcast_to(
        jnp.sum(low_ref[...].astype(F32), axis=0, keepdims=True), (8, 640)
    )
    for rows, ref in ((slice(256, 512), other), (slice(0, 256), own)):
        for cols, w in ((slice(0, 384), w_own), (slice(384, 768), w_other)):
            value = dot(low_ref[rows, :192], w[:192, :]) + dot(low_ref[rows, 256:], w[192:576, :])
            ref[:, cols] = value.astype(ref.dtype)


def flip(value):
    return value.astype(F32).T.astype(BF16)


def down_grad_kernel(g_ref, dz_own, dz_other, out):
    for part in range(3):
        rows = slice(256 * part, 256 * part + 256)
        left = flip(g_ref[:, rows])
        grad = dot(left[:, :256], dz_own[...]) + dot(left[:, 256:], dz_other[...])
        out[rows, :] = grad.astype(BF16)


def in_grad_kernel(h_own, h_other, du_ref, o_ref, da_own, da_other, out):
    for cols in (slice(0, 384), slice(384, 768)):
        grad = dot(flip(h_own[:, cols]), du_ref[:256, :]) + dot(
            flip(h_other[:, cols]), du_ref[256:, :]
        )
        out[:384, cols] = grad[:, :384].astype(BF16)
        out[384:768, cols] = grad[:, 384:].astype(BF16)
    left = flip(o_ref[...])
    grad = dot(left[64:, :256], da_own[...]) + dot(left[64:, 256:], da_other[...])
    out[768:960, :] = grad.astype(BF16)
    out[960:, :] = jnp.zeros((64, 768), BF16)


def proj_grad_kernel(low_ref, x_own, x_other, sums, core_sums, sums_in, sums_qkv, out, rows):
    for to, cols in ((slice(0, 192), slice(0, 256)), (slice(192, 576), slice(256, 640))):
        left = flip(low_ref[:, cols])[: to.stop - to.start]
        grad = dot(left[:, :256], x_own[...]) + dot(left[:, 256:], x_other[...])
        out[to, :] = grad.astype(BF16)
    h = lax.axis_index("fsdp")
    rows[...] = jnp.zeros((16, 768), F32)
    rows[0:3, :] = sums[0:3, :] + core_sums[0:3, :]
    rows[3:6, :] = sums[8:11, :] + core_sums[8:11, :]
    low, high = sums_in[:1, :384], sums_in[:1, 384:]
    rows[6:7, :384] = jnp.where(h == 0, low, high)
    rows[6:7, 384:] = jnp.where(h == 0, high, low)
    for cols in (slice(0, 384), slice(384, 768)):
        rows[7:8, cols] = sums_qkv[:1, :384]
        rows[8:9, cols] = sums_qkv[:1, 256:]
    out[576:592, :] = rows[...].astype(BF16)
    out[592:, :] = jnp.zeros((48, 768), BF16)


def sum_kernel(*refs):
    own, other = refs[-2:]
    start = 0
    for terms in refs[:-2]:
        total = terms[0].astype(F32)
        for k in range(1, 16):
            total = total + terms[k].astype(F32)
        rows = slice(start, start + total.shape[0])
        own[rows, :] = total[:, :384]
        other[rows, :] = total[:, 384:].astype(BF16)
        start = rows.stop


def copies_kernel(own, other, out):
    value = (own[...] + other[...].astype(F32)).astype(BF16)
    for k in range(16):
        out[k] = value


def early_kernel(src, down, w_in, w_out):
    for k in range(16):
        down[48 * k : 48 * k + 48, :] = src[k, :48, :].astype(F32)
        value = src[k, 48:, :].astype(F32)
        if k < 6:
            w_in[64 * k : 64 * k + 64, :384] = value
        elif k < 12:
            w_in[64 * k - 384 : 64 * k - 320, 384:] = value
        elif k < 15:
            w_out[64 * k - 768 : 64 * k - 704, :] = value


def late_kernel(src, proj, b_qv, *refs):
    vectors, rows = refs[:7], refs[7]
    rows[...] = src[...].astype(F32)
    proj[...] = rows[:576, :]
    for k, ref in enumerate(vectors):
        ref[...] = rows[576 + k, :]
    for k, row in enumerate((rows[583:584, :192], rows[584:585, 192:])):
        b_qv[k : k + 1, :] = jnp.where(lax.axis_index("fsdp") == 0, row[:, :96], row[:, 96:])


def ctx_sum(*terms):
    rows = sum(term.shape[1] for term in terms)
    own, other = call(sum_kernel, [shape((rows, 384), F32), shape((rows, 384), BF16)], *terms)
    return own, fsdp_swap(other)


def gather(own, other, after=()):
    rows = own.shape[0]
    (copies,) = call(copies_kernel, [shape((16, rows, 384), BF16)], own, other, after=after)
    return ctx_exchange(copies.reshape(16 * rows, 384))


def body(
    tokens,
    cotangent,
    lengths,
    w_qkv,
    b_qv,
    w_out,
    b_out,
    ln1_gain,
    ln1_bias,
    w_in,
    b_in,
    w_down,
    b_down,
    ln2_gain,
    ln2_bias,
):
    placed, wt_own = call(
        prepare_kernel,
        [shape((4, 128, 768), BF16), shape((592, 384), BF16)],
        tokens,
        cotangent,
        w_qkv.transpose(0, 2, 1).reshape(576, 384),
        b_qv,
        scratch=[
            pltpu.VMEM((2, 4, 64, 768), BF16),
            pltpu.VMEM((2, 96), BF16),
            pltpu.SemaphoreType.DMA((4,)),
        ],
        load=pl.BlockSpec(memory_space=pl.ANY),
        limit=58,
    )
    wt_other = fsdp_swap(wt_own)
    placed = y_exchange(placed)
    x_own = placed[:, :64].reshape(256, 768)
    x_other = core_swap(x_own)
    query, kv = call(
        qkv_kernel,
        [shape((512, 256), BF16), shape((512, 384), BF16)],
        x_own,
        x_other,
        wt_own,
        wt_other,
    )
    cot = placed[:, 64:].reshape(256, 768)

    pack_own, v_own = call(
        pack_kernel,
        [shape((976, 384), BF16), shape((16, 384), BF16)],
        w_out,
        w_in,
        b_out,
        ln1_gain,
        ln1_bias,
        b_down,
        ln2_gain,
        ln2_bias,
        b_in,
        scratch=[pltpu.VMEM((16, 384), F32)],
        load=pl.BlockSpec(),
    )
    pack_own, w_down, _, _ = lax.optimization_barrier((pack_own, w_down, wt_other, x_other))
    pack = fsdp_swap(pack_own)
    down_other = fsdp_swap(w_down)

    kv_low, kv_high = z_shift(kv, 1), z_shift(kv, -1)
    carry = [shape((192, 512), F32), shape((8, 512), F32)]

    def attend(parts, first, last):
        return lambda *refs: attend_kernel(parts, first, last, *refs)

    acc, stat = call(attend([(0, 0)], True, False), carry, lengths, query, kv, smem=1, after=(pack,), limit=16, us=2.4)
    pass_up, pass_down, acc = lax.optimization_barrier((kv_low[:256], kv_high[256:], acc))
    far_top, far_low = z_shift(pass_up, 1), z_shift(pass_down, -1)
    acc, stat = call(
        attend([(3, 0), (1, 0)], False, False),
        carry,
        lengths,
        query,
        kv_low,
        kv_high,
        acc,
        stat,
        smem=1,
        limit=16,
        us=4.3,
    )
    attn, log_total = call(
        attend([(2, 0), (2, 256)], False, True),
        [shape((512, 256), BF16), shape((8, 512), F32)],
        lengths,
        query,
        far_top,
        far_low,
        acc,
        stat,
        smem=1,
        limit=16,
        us=3,
    )
    halves = [shape((256, 768), F32), shape((256, 768), BF16)]
    own, other = call(out_kernel, halves, attn, w_out, pack, after=(down_other,))
    a, b = tp_sum(own, other)
    normed_one, inverse_one, hidden_own = call(
        norm_one_kernel,
        [shape((256, 768), F32), shape((256, 128), F32), shape((256, 768), BF16)],
        x_own,
        a,
        b,
        v_own,
        pack,
    )
    hidden_other = core_swap(hidden_own)
    gelu, slope, own, other = call(
        mlp_kernel,
        [shape((512, 768), BF16), shape((512, 768), F32)] + halves,
        hidden_own,
        hidden_other,
        w_in,
        w_down,
        down_other,
        pack,
        v_own,
    )
    a, b = tp_sum(own, other)
    result, grad_two, dz_own, sums_two = call(
        norm_two_kernel,
        [
            shape((256, 768), BF16),
            shape((256, 768), F32),
            shape((256, 768), BF16),
            shape((8, 768), F32),
        ],
        normed_one,
        a,
        b,
        cot,
        v_own,
        pack,
    )
    dz_other = core_swap(dz_own)
    du, own, other, sums_in = call(
        mlp_back_kernel,
        [shape((512, 768), BF16)] + halves + [shape((8, 768), F32)],
        dz_own,
        dz_other,
        w_in,
        w_down,
        down_other,
        pack,
        slope,
    )
    a, b = tp_sum(own, other)
    gelu, dz_own, dz_other, _ = lax.optimization_barrier((gelu, dz_own, dz_other, a))
    (down_terms,) = call(down_grad_kernel, [shape((768, 768), BF16)], gelu, dz_own, dz_other)
    down_terms = ctx_exchange(down_terms)
    grad_one, da_own, sums_one = call(
        norm_back_kernel,
        [shape((256, 768), F32), shape((256, 768), BF16), shape((8, 768), F32)],
        grad_two,
        a,
        b,
        normed_one,
        inverse_one,
        v_own,
        pack,
    )
    da_other = core_swap(da_own)
    grad_heads, inner = call(
        out_back_kernel,
        [shape((512, 256), BF16), shape((8, 512), F32)],
        da_own,
        da_other,
        w_out,
        pack,
        attn,
    )
    def attend_back(parts, first, added):
        return lambda *refs: attend_back_kernel(parts, first, added, *refs)

    base = (lengths, query, grad_heads, log_total, inner)
    dq_shape = shape((192, 512), F32)
    half, whole = shape((256, 384), BF16), shape((512, 384), BF16)
    grad_top, grad_low, dq = call(
        attend_back([(2, 0), (2, 256)], True, (None, None)),
        [half, half, dq_shape],
        *base,
        far_top,
        far_low,
        smem=1,
        limit=16,
        us=3.3,
    )
    grad_top, grad_low = z_shift(grad_top, 1), z_shift(grad_low, -1)
    grad_kv, dq = call(
        attend_back([(0, 0)], False, (None,)),
        [whole, dq_shape],
        *base,
        kv,
        dq,
        smem=1,
        us=3,
        fetch=True,
    )
    du, hidden_own, grad_top, grad_low, grad_kv = lax.optimization_barrier(
        (du, hidden_own, grad_top, grad_low, grad_kv)
    )
    (in_terms,) = call(
        in_grad_kernel,
        [shape((1024, 768), BF16)],
        hidden_own,
        hidden_other,
        du,
        attn,
        da_own,
        da_other,
    )
    in_terms = ctx_exchange(in_terms)
    grad_up, grad_down_z, dq = call(
        attend_back([(1, 0), (3, 0)], False, (0, 256)),
        [whole, whole, dq_shape],
        *base,
        kv_high,
        kv_low,
        grad_top,
        grad_low,
        dq,
        smem=1,
        fetch=True,
    )
    early = gather(*ctx_sum(down_terms, in_terms))
    sums = jnp.concatenate([sums_two, sums_one])
    core_sums = core_swap(sums)
    grad_qkv, own, other, sums_qkv = call(
        input_back_kernel,
        [shape((512, 640), BF16)] + halves + [shape((8, 640), F32)],
        grad_kv,
        z_shift(grad_up, 1),
        z_shift(grad_down_z, -1),
        dq,
        wt_own,
        wt_other,
        after=(core_sums,),
        fetch=True,
    )
    (proj_terms,) = call(
        proj_grad_kernel,
        [shape((640, 768), BF16)],
        grad_qkv,
        x_own,
        x_other,
        sums,
        core_sums,
        sums_in,
        sums_qkv,
        scratch=[pltpu.VMEM((16, 768), F32)],
        after=(early,),
    )
    late_own, late_other = ctx_sum(ctx_exchange(proj_terms))
    a, b = tp_sum(own, other)
    grad_x = (grad_one + (a.astype(F32) + b.astype(F32))).astype(BF16)
    outgoing = call(split_kernel, [shape((128, 768), BF16)] * 4, result, grad_x)
    back = jnp.concatenate([outgoing[0]] + [y_shift(outgoing[k], k) for k in (1, 2, 3)])
    late = gather(late_own, late_other, after=(back,)).reshape(640, 384)
    output, grad_tokens = call(
        return_kernel, [shape((4, 128, 768), BF16)] * 2, back, core_swap(back)
    )
    grad_down, grad_in, grad_out = call(
        early_kernel,
        [shape((768, 384), F32), shape((384, 768), F32), shape((192, 384), F32)],
        early,
    )
    grad_proj, grad_b_qv, *vectors = call(
        late_kernel,
        [shape((576, 384), F32), shape((2, 96), F32)] + [shape((384,), F32)] * 7,
        late,
        scratch=[pltpu.VMEM((640, 384), F32)],
    )
    g_gain_two, g_shift_two, g_b_down, g_gain_one, g_shift_one, g_b_out, g_b_in = vectors
    return (
        output,
        grad_tokens,
        grad_proj.reshape(3, 192, 384).transpose(0, 2, 1),
        grad_b_qv,
        grad_out,
        g_b_out,
        g_gain_one,
        g_shift_one,
        grad_in,
        g_b_in,
        grad_down,
        g_b_down,
        g_gain_two,
        g_shift_two,
    )


def solution(mesh):
    placed = (
        P("fsdp", "ctx", None),
        P("fsdp", "ctx", None),
        P("fsdp"),
        P(None, "fsdp", "tp"),
        P(None, ("tp", "fsdp")),
        P("tp", "fsdp"),
        P("fsdp"),
        P("fsdp"),
        P("fsdp"),
        P("fsdp", "tp"),
        P(("tp", "fsdp")),
        P("tp", "fsdp"),
        P("fsdp"),
        P("fsdp"),
        P("fsdp"),
    )
    return jax.shard_map(
        body,
        mesh=mesh,
        in_specs=placed,
        out_specs=placed[:2]
        + (
            P(None, "fsdp", "tp"),
            P(None, ("tp", "fsdp")),
            P("tp", "fsdp"),
            P("fsdp"),
            P("fsdp"),
            P("fsdp"),
            P("fsdp", "tp"),
            P(("tp", "fsdp")),
            P("tp", "fsdp"),
            P("fsdp"),
            P("fsdp"),
            P("fsdp"),
        ),
        check_vma=False,
    )
```
